32 devices in a mesh: row: 4 (over x, core), seq: 8 (over z, y).
Axes of the slice: x: 2, y: 2, z: 4, core: 2. Of those that a mesh axis runs over, the one named last changes fastest.
Arguments:
- layer_input: float32 [8, 3072, 768], P('row', 'seq'), may hold values from -6 to 6
- doc_ids: int32 [8, 3072], P('row', 'seq'), may hold values from -1 to 1, as said below
- cotangent: float32 [8, 3072, 768], P('row', 'seq'), may hold values from -6 to 6
- attn_norm_gain: float32 [768], replicated, may hold values from 0.5 to 1.5
- attn_norm_bias: float32 [768], replicated, may hold values from -1.75 to 1.75
- query_weight: bfloat16 [768, 768], replicated, may hold values from -0.21875 to 0.21875
- query_bias: float32 [768], replicated, may hold values from -1.75 to 1.75
- key_weight: bfloat16 [768, 768], replicated, may hold values from -0.21875 to 0.21875
- value_weight: bfloat16 [768, 768], replicated, may hold values from -0.21875 to 0.21875
- value_bias: float32 [768], replicated, may hold values from -1.75 to 1.75
- output_weight: bfloat16 [768, 768], replicated, may hold values from -3.5 to 3.5
- output_bias: float32 [768], replicated, may hold values from -1.75 to 1.75
- feed_norm_gain: float32 [768], replicated, may hold values from 0.5 to 1.5
- feed_norm_bias: float32 [768], replicated, may hold values from -1.75 to 1.75
- up_weight: bfloat16 [768, 3072], replicated, may hold values from -0.21875 to 0.21875
- up_bias: float32 [3072], replicated, may hold values from -1.75 to 1.75
- down_weight: bfloat16 [3072, 768], replicated, may hold values from -0.109375 to 0.109375
- down_bias: float32 [768], replicated, may hold values from -1.75 to 1.75
Outputs:
- out: float32 [8, 3072, 768], P('row', 'seq')
- input_grad: float32 [8, 3072, 768], P('row', 'seq')
- grad_attn_norm_gain: float32 [768], P('seq')
- grad_attn_norm_bias: float32 [768], P('seq')
- grad_query_weight: float32 [768, 768], P('seq')
- grad_query_bias: float32 [768], P('seq')
- grad_key_weight: float32 [768, 768], P('seq')
- grad_value_weight: float32 [768, 768], P('seq')
- grad_value_bias: float32 [768], P('seq')
- grad_output_weight: float32 [768, 768], P('seq')
- grad_output_bias: float32 [768], P('seq')
- grad_feed_norm_gain: float32 [768], P('seq')
- grad_feed_norm_bias: float32 [768], P('seq')
- grad_up_weight: float32 [768, 3072], P('seq')
- grad_up_bias: float32 [3072], P('seq')
- grad_down_weight: float32 [3072, 768], P('seq')
- grad_down_bias: float32 [768], P('seq')
The draws below stay inside these ranges and needn't reach their ends.
Inputs may be any that keep to these rules, and one draw needn't show every extreme that they name: `doc_ids`: in every packed row, document 0 fills the first 1 to 192 positions, document 1 runs from there until the padding, and padding (-1) fills the last 1 to 192 positions.
All inputs are finite; a program needn't handle non-finite values.
Results may differ from the reference program's by a relative error of at most 0.015.
Values may be sent and summed in bfloat16 or wider, within the bound.
No kernel may reach another device: no remote copies, remote signals or barrier semaphores. Data moves between devices by JAX's collectives and lax.ppermute only.
A program may use at most 512 MiB of HBM per device.

```python
import jax
import jax.numpy as jnp
from jax import lax

D = 768
HEADS = 12
HEAD_DIM = 64
FF = 3072
TOK_SEQ = 384
FIRST_DILATION = 1
SECOND_DILATION = 2
THIRD_DILATION = 4
FOURTH_DILATION = 6
FIFTH_DILATION = 12
LEN = 3072
ROWS = 8
FIRST_SEGMENT = 1536
SECOND_SEGMENT = 3072
THIRD_SEGMENT = 3072
FOURTH_SEGMENT = 3072
FIFTH_SEGMENT = 3072


def draw_doc_ids(key, part):
    key = jax.random.fold_in(key, 7)
    first_key, pad_key = jax.random.split(key)
    first = jax.random.randint(first_key, (ROWS, 1), 1, TOK_SEQ // 2 + 1)
    padding = jax.random.randint(pad_key, (ROWS, 1), 1, TOK_SEQ // 2 + 1)
    places = jnp.arange(LEN, dtype=jnp.int32)[None, :]
    numbers = jnp.where(places < first, 0, 1)
    return jnp.where(places >= LEN - padding, -1, numbers).astype(jnp.int32)


def levels(own_key, shape, pieces, least, largest):
    level, own = 1.0, jax.random.fold_in(own_key, 6)
    for axis_at, shards_of in pieces:
        heights = jnp.exp(jax.random.uniform(jax.random.fold_in(own, axis_at), (shards_of,), jnp.float32, least / len(pieces), largest / len(pieces)))
        level = level * jnp.repeat(heights, shape[axis_at] // shards_of).reshape([-1 if axis == axis_at else 1 for axis in range(len(shape))])
    return level


def scatter_about(key, dims, deviation, most, shards=(), held_as=jnp.bfloat16):
    drawn = deviation * jax.random.normal(key, dims, jnp.float32)
    if shards:
        drawn = drawn * levels(key, dims, shards, -0.22, 0.18)
    return jnp.clip(drawn, -most, most).astype(held_as)


def setup_inputs(seed: int = 0) -> dict:
    streams_of = jax.random.split(jax.random.key(seed), 19)
    return {
        "layer_input": scatter_about(streams_of[0], (ROWS, LEN, D), 1.0, 6.0, ((0, 4), (1, 8)), jnp.float32),
        "doc_ids": draw_doc_ids(jax.random.fold_in(streams_of[18], 71), 0),
        "cotangent": scatter_about(streams_of[2], (ROWS, LEN, D), 1.0, 6.0, ((0, 4), (1, 8)), jnp.float32),
        "attn_norm_gain": jnp.clip(1.0 + 0.1 * jax.random.normal(streams_of[3], (D,), jnp.float32), 0.5, 1.5),
        "attn_norm_bias": scatter_about(streams_of[4], (D,), 0.3, 1.75, (), jnp.float32),
        "query_weight": scatter_about(streams_of[5], (D, D), D ** -0.5, 0.21875),
        "query_bias": scatter_about(streams_of[6], (D,), 0.3, 1.75, (), jnp.float32),
        "key_weight": scatter_about(streams_of[7], (D, D), D ** -0.5, 0.21875),
        "value_weight": scatter_about(streams_of[8], (D, D), D ** -0.5, 0.21875),
        "value_bias": scatter_about(streams_of[9], (D,), 0.3, 1.75, (), jnp.float32),
        "output_weight": scatter_about(streams_of[10], (D, D), (max(D // 256, 1)) ** -0.5, 3.5),
        "output_bias": scatter_about(streams_of[11], (D,), 0.3, 1.75, (), jnp.float32),
        "feed_norm_gain": jnp.clip(1.0 + 0.1 * jax.random.normal(streams_of[12], (D,), jnp.float32), 0.5, 1.5),
        "feed_norm_bias": scatter_about(streams_of[13], (D,), 0.3, 1.75, (), jnp.float32),
        "up_weight": scatter_about(streams_of[14], (D, FF), D ** -0.5, 0.21875),
        "up_bias": scatter_about(streams_of[15], (FF,), 0.3, 1.75, (), jnp.float32),
        "down_weight": scatter_about(streams_of[16], (FF, D), FF ** -0.5, 0.109375),
        "down_bias": scatter_about(streams_of[17], (D,), 0.3, 1.75, (), jnp.float32),
    }


EPS = 1e-05
NEG = -1e+30
HIGH = lax.Precision.HIGHEST

@jax.custom_vjp
def low(v):
    return lax.optimization_barrier(v.astype(jnp.bfloat16)).astype(jnp.float32)

@jax.custom_vjp
def low_back(v):
    return v

def low_keep(v):
    return (low(v), None)

def low_pass(kept, grad):
    return (grad,)

def back_keep(v):
    return (v, None)

def back_low(kept, grad):
    return (low(grad),)
low.defvjp(low_keep, low_pass)
low_back.defvjp(back_keep, back_low)

def layer_norm(values, gain, bias):
    center = values - lax.optimization_barrier(jnp.mean(values, axis=-1, keepdims=True))
    spread = lax.optimization_barrier(jnp.mean(center * center, axis=-1, keepdims=True))
    return center * lax.rsqrt(spread + EPS) * gain + bias

def matmul(left, right):
    return jnp.dot(left, right, precision=HIGH)

def dilate(array, segments, picks, stride, offset):
    shaped = array.reshape(segments, picks, stride, HEAD_DIM)
    return lax.dynamic_index_in_dim(shaped, offset, 2, keepdims=False)

def head_attention(query_head, key_head, value_head, doc_row, head_index):
    score_scale = HEAD_DIM ** (-0.5)
    branch_settings = ((FIRST_SEGMENT, FIRST_DILATION), (SECOND_SEGMENT, SECOND_DILATION), (THIRD_SEGMENT, THIRD_DILATION), (FOURTH_SEGMENT, FOURTH_DILATION), (FIFTH_SEGMENT, FIFTH_DILATION))
    total = jnp.full((LEN,), NEG, dtype=jnp.float32)
    branches = []
    for span, stride in branch_settings:
        segments = LEN // span
        picks = span // stride
        offset = head_index % stride
        query_sel = dilate(query_head, segments, picks, stride, offset)
        key_sel = dilate(key_head, segments, picks, stride, offset)
        value_sel = dilate(value_head, segments, picks, stride, offset)
        docs = lax.dynamic_index_in_dim(doc_row.reshape(segments, picks, stride), offset, 2, keepdims=False)
        places = jnp.arange(picks, dtype=jnp.int32)
        mask = (places[None, None, :] <= places[None, :, None]) & (docs[:, None, :] == docs[:, :, None])
        score = low_back(score_scale * jnp.einsum('gqe,gke->gqk', query_sel, key_sel, precision=HIGH))
        score = jnp.where(mask, score, NEG)
        part_total = jax.nn.logsumexp(score, axis=-1)
        chosen = jnp.arange(stride, dtype=jnp.int32) == offset
        spread = jnp.where(chosen[None, None, :], part_total[:, :, None], NEG).reshape(LEN)
        total = jnp.logaddexp(total, spread)
        branches.append((score, value_sel, chosen, segments, picks, stride, offset))
    result = jnp.zeros((LEN, HEAD_DIM), dtype=jnp.float32)
    for score, value_sel, chosen, segments, picks, stride, offset in branches:
        total_sel = lax.dynamic_index_in_dim(total.reshape(segments, picks, stride), offset, 2, keepdims=False)
        prob = low(jnp.exp(score - total_sel[:, :, None]))
        part = jnp.einsum('gqk,gke->gqe', prob, value_sel, precision=HIGH)
        result = result + jnp.where(chosen[None, None, :, None], part[:, :, None, :], 0.0).reshape(LEN, HEAD_DIM)
    return result

def sequence(row_input, doc_row, weights):
    norm1_gain, norm1_bias, wq, bq, wk, wv, bv, wo, bo, norm2_gain, norm2_bias, wu, bu, wd, bd = weights
    h_first = low(layer_norm(row_input, norm1_gain, norm1_bias))
    queries = low(low_back(matmul(h_first, wq) + bq))
    keys = low(low_back(matmul(h_first, wk)))
    values = low(low_back(matmul(h_first, wv) + bv))

    def split_heads(array):
        return array.reshape(LEN, HEADS, HEAD_DIM).transpose(1, 0, 2)
    head_numbers = jnp.arange(HEADS, dtype=jnp.int32)

    def one_head(item):
        return head_attention(item[0], item[1], item[2], doc_row, item[3])
    head_outs = lax.map(jax.checkpoint(one_head), (split_heads(queries), split_heads(keys), split_heads(values), head_numbers))
    attended = low(low_back(head_outs.transpose(1, 0, 2).reshape(LEN, D)))
    middle = row_input + low_back(matmul(attended, wo) + bo)
    h_second = low(layer_norm(middle, norm2_gain, norm2_bias))
    hidden = low_back(matmul(h_second, wu) + bu)
    active = low(jax.nn.gelu(hidden))
    return middle + low_back(matmul(active, wd) + bd)

def reference(layer_input, doc_ids, cotangent, attn_norm_gain, attn_norm_bias, query_weight, query_bias, key_weight, value_weight, value_bias, output_weight, output_bias, feed_norm_gain, feed_norm_bias, up_weight, up_bias, down_weight, down_bias):
    weights = (attn_norm_gain, attn_norm_bias, query_weight.astype(jnp.float32), query_bias, key_weight.astype(jnp.float32), value_weight.astype(jnp.float32), value_bias, output_weight.astype(jnp.float32), output_bias, feed_norm_gain, feed_norm_bias, up_weight.astype(jnp.float32), up_bias, down_weight.astype(jnp.float32), down_bias)

    def forward(inputs_all, params):

        def one_row(item):
            return sequence(item[0], item[1], params)
        return lax.map(jax.checkpoint(one_row), (inputs_all, doc_ids))
    result, pullback = jax.vjp(forward, layer_input, weights)
    masked_grad = jnp.where((doc_ids >= 0)[..., None], cotangent, 0.0)
    input_grad, grads = pullback(masked_grad)
    return (result, input_grad, grads[0], grads[1], grads[2], grads[3], grads[4], grads[5], grads[6], grads[7], grads[8], grads[9], grads[10], grads[11], grads[12], grads[13], grads[14])
```

```python
import functools
import math

import jax
import jax.numpy as jnp
from jax import lax
from jax.experimental import pallas as pl
from jax.experimental.pallas import tpu as pltpu
from jax.sharding import PartitionSpec as P

HEADS = 12
HEAD_DIM = 64
GROUP = 4
FIRST_DILATION = 1
SECOND_DILATION = 2
THIRD_DILATION = 4
FOURTH_DILATION = 6
FIFTH_DILATION = 12


EPS = 1e-05
NEG = -1e30
HIGH = lax.Precision.HIGHEST


def swapped(array, axis, apart):
    return lax.ppermute(array, axis, [(i, i ^ 1 << apart) for i in range(lax.axis_size(axis))])


def for_sending(array):

    def short(part):
        return part.astype(jnp.bfloat16) if part.dtype == jnp.float32 else part

    return jax.tree.map(short, array)


def layer_norm(values, gain, bias):
    center = values - jnp.mean(values, axis=-1, keepdims=True)
    spread = jnp.mean(center * center, axis=-1, keepdims=True)
    return center * lax.rsqrt(spread + EPS) * gain + bias


def project(inputs, weight):
    return jnp.einsum("ntd,df->ntf", inputs, weight, preferred_element_type=jnp.float32)


def project_back(grads, weight):
    return jnp.einsum("ntf,df->ntd", grads, weight, preferred_element_type=jnp.float32)


def weight_grad(inputs, grads):
    return jnp.einsum("ntd,ntf->df", inputs, grads, preferred_element_type=jnp.float32)


def column_sum(grads):
    return jnp.sum(grads.astype(jnp.float32), axis=(0, 1))


def pick_pairs(values, stride, picker):
    sequences, tokens, kinds, model_width = values.shape
    head_count = picker.shape[1]
    shaped = values.reshape(
        sequences, tokens // stride, stride, kinds, head_count, model_width // head_count
    )
    picked = jnp.einsum(
        "nsrche,rh->nsche", shaped, picker.astype(jnp.bfloat16), preferred_element_type=jnp.float32
    )
    return picked.astype(jnp.bfloat16).reshape(sequences, tokens // stride, kinds, model_width)


def spread_grads(values, stride, picker):
    sequences, slot_count, kinds, model_width = values.shape
    head_count = picker.shape[1]
    shaped = values.reshape(sequences, slot_count, kinds, head_count, model_width // head_count)
    spread = jnp.einsum("nsche,rh->nsrche", shaped, picker.astype(jnp.float32), precision=HIGH)
    return spread.reshape(sequences, slot_count * stride, kinds, model_width)


def group_gather(pieces, depth_list, device):
    gathered = list(pieces)
    for bit_index in range(max(depth_list)):
        active = [branch for branch in range(len(pieces)) if depth_list[branch] > bit_index]
        packed = jnp.concatenate([gathered[branch] for branch in active], 1)
        partner = swapped(packed, "seq", bit_index)
        lower = device // 2**bit_index % 2 == 0
        start = 0
        for branch in active:
            count = gathered[branch].shape[1]
            other = partner[:, start : start + count]
            start = start + count
            gathered[branch] = jnp.where(
                lower,
                jnp.concatenate((gathered[branch], other), 1),
                jnp.concatenate((other, gathered[branch]), 1),
            )
    return gathered


def group_return(pieces, depth_list, device):
    held = list(pieces)
    for bit_index in range(max(depth_list)):
        active = [branch for branch in range(len(pieces)) if depth_list[branch] > bit_index]
        lower = device // 2**bit_index % 2 == 0
        keep_parts = []
        send_parts = []
        for branch in active:
            sequences, count, kinds, model_width = held[branch].shape
            devices_left = 2 ** (depth_list[branch] - bit_index)
            slot_count = count // devices_left
            shaped = held[branch].reshape(
                sequences, devices_left // 2, 2, slot_count, kinds, model_width
            )
            even_part = shaped[:, :, 0].reshape(sequences, count // 2, kinds, model_width)
            odd_part = shaped[:, :, 1].reshape(sequences, count // 2, kinds, model_width)
            keep_parts.append(jnp.where(lower, even_part, odd_part))
            send_parts.append(jnp.where(lower, odd_part, even_part))
        received = swapped(for_sending(jnp.concatenate(send_parts, 1)), "seq", bit_index)
        start = 0
        for branch, kept in zip(active, keep_parts):
            count = kept.shape[1]
            held[branch] = kept + received[:, start : start + count]
            start = start + count
    return held


def per_device(
    layer_input,
    doc_ids,
    cotangent,
    attn_norm_gain,
    attn_norm_bias,
    query_weight,
    query_bias,
    key_weight,
    value_weight,
    value_bias,
    output_weight,
    output_bias,
    feed_norm_gain,
    feed_norm_bias,
    up_weight,
    up_bias,
    down_weight,
    down_bias,
):
    sequences, tokens, model_width = layer_input.shape
    head_count = HEADS
    head_size = HEAD_DIM
    score_scale = head_size ** (-0.5)
    device = lax.axis_index("seq")
    axis_count = lax.axis_size("seq")
    branch_strides = (
        FIRST_DILATION,
        SECOND_DILATION,
        THIRD_DILATION,
        FOURTH_DILATION,
        FIFTH_DILATION,
    )
    group_sizes = tuple((min(GROUP * 2**branch, axis_count) for branch in range(5)))
    depth_list = tuple((group_size.bit_length() - 1 for group_size in group_sizes))
    slot_counts = tuple((tokens // stride for stride in branch_strides))
    pickers = tuple(
        (
            jnp.arange(stride)[:, None] == jnp.arange(head_count)[None, :] % stride
            for stride in branch_strides
        )
    )
    docs_all = lax.all_gather(doc_ids, "seq", axis=1, tiled=True)
    segment_docs = []
    for branch in range(5):
        group_size = group_sizes[branch]
        group_start = device // group_size * group_size * tokens
        segment_docs.append(lax.dynamic_slice_in_dim(docs_all, group_start, group_size * tokens, 1))
    masked_grad = jnp.where((doc_ids >= 0)[..., None], cotangent, 0.0)
    h_first = layer_norm(layer_input, attn_norm_gain, attn_norm_bias).astype(jnp.bfloat16)
    query_low = (project(h_first, query_weight) + query_bias).astype(jnp.bfloat16)
    key_low = project(h_first, key_weight).astype(jnp.bfloat16)
    value_low = (project(h_first, value_weight) + value_bias).astype(jnp.bfloat16)
    pairs_low = jnp.stack((key_low, value_low), 2)
    own_sets = [
        pick_pairs(pairs_low, branch_strides[branch], pickers[branch]) for branch in range(5)
    ]
    gathered_sets = group_gather(own_sets, depth_list, device)

    def branch_scores(head_index, branch):
        stride = branch_strides[branch]
        group_size = group_sizes[branch]
        slot_count = slot_counts[branch]
        offset = head_index % stride
        chosen = jnp.arange(stride) == offset
        query_head = lax.dynamic_slice_in_dim(query_low, head_index * head_size, head_size, 2)
        query_sel = lax.dynamic_index_in_dim(
            query_head.reshape(sequences, slot_count, stride, head_size), offset, 2, keepdims=False
        )
        key_sel = lax.dynamic_slice_in_dim(
            gathered_sets[branch][:, :, 0], head_index * head_size, head_size, 2
        )
        value_sel = lax.dynamic_slice_in_dim(
            gathered_sets[branch][:, :, 1], head_index * head_size, head_size, 2
        )
        key_docs = lax.dynamic_index_in_dim(
            segment_docs[branch].reshape(sequences, group_size * slot_count, stride),
            offset,
            2,
            keepdims=False,
        )
        query_docs = lax.dynamic_index_in_dim(
            doc_ids.reshape(sequences, slot_count, stride), offset, 2, keepdims=False
        )
        key_index = jnp.arange(group_size * slot_count, dtype=jnp.int32)
        query_index = device % group_size * slot_count + jnp.arange(slot_count, dtype=jnp.int32)
        mask = (key_index[None, None, :] <= query_index[None, :, None]) & (
            key_docs[:, None, :] == query_docs[:, :, None]
        )
        score = jnp.where(
            mask,
            score_scale
            * jnp.einsum("nqe,nke->nqk", query_sel, key_sel, preferred_element_type=jnp.float32),
            NEG,
        )
        return (chosen, offset, query_sel, key_sel, value_sel, score)

    def head_forward(head_index):
        found = [branch_scores(head_index, branch) for branch in range(5)]
        total = jnp.full((sequences, tokens), NEG, dtype=jnp.float32)
        for branch in range(5):
            chosen, offset, query_sel, key_sel, value_sel, score = found[branch]
            part_total = jax.nn.logsumexp(score, axis=-1)
            spread = jnp.where(chosen, part_total[..., None], NEG).reshape(sequences, tokens)
            total = jnp.logaddexp(total, spread)
        result = jnp.zeros((sequences, tokens, head_size), dtype=jnp.float32)
        for branch in range(5):
            chosen, offset, query_sel, key_sel, value_sel, score = found[branch]
            stride = branch_strides[branch]
            total_sel = lax.dynamic_index_in_dim(
                total.reshape(sequences, slot_counts[branch], stride), offset, 2, keepdims=False
            )
            prob = jnp.exp(score - total_sel[..., None]).astype(jnp.bfloat16)
            part = jnp.einsum("nqk,nke->nqe", prob, value_sel, preferred_element_type=jnp.float32)
            result = result + jnp.where(chosen[:, None], part[:, :, None, :], 0.0).reshape(
                sequences, tokens, head_size
            )
        return (result, total)

    head_outs, totals = lax.map(head_forward, jnp.arange(head_count, dtype=jnp.int32))
    attended = (
        head_outs.transpose(1, 2, 0, 3).reshape(sequences, tokens, model_width).astype(jnp.bfloat16)
    )
    middle = layer_input + project(attended, output_weight) + output_bias
    h_second = layer_norm(middle, feed_norm_gain, feed_norm_bias).astype(jnp.bfloat16)
    hidden = project(h_second, up_weight) + up_bias
    active_full, gelu_pull = jax.vjp(jax.nn.gelu, hidden)
    active = active_full.astype(jnp.bfloat16)
    result_out = middle + project(active, down_weight) + down_bias
    down_grad = masked_grad.astype(jnp.bfloat16)
    grad_down_weight = weight_grad(active, down_grad)
    grad_down_bias = column_sum(down_grad)
    active_grad = jnp.einsum(
        "ntd,fd->ntf", down_grad, down_weight, preferred_element_type=jnp.float32
    )
    hidden_grad = gelu_pull(active_grad)[0].astype(jnp.bfloat16)
    grad_up_weight = weight_grad(h_second, hidden_grad)
    grad_up_bias = column_sum(hidden_grad)
    norm_input_grad = project_back(hidden_grad, up_weight)
    norm_pull = jax.vjp(layer_norm, middle, feed_norm_gain, feed_norm_bias)[1]
    middle_part, grad_feed_norm_gain, grad_feed_norm_bias = norm_pull(norm_input_grad)
    middle_grad = masked_grad + middle_part
    branch_grad = middle_grad.astype(jnp.bfloat16)
    grad_output_weight = weight_grad(attended, branch_grad)
    grad_output_bias = column_sum(branch_grad)
    attended_grad = project_back(branch_grad, output_weight).astype(jnp.bfloat16)

    def head_backward(item):
        head_index, total = item
        found = [branch_scores(head_index, branch) for branch in range(5)]
        out_grad = lax.dynamic_slice_in_dim(attended_grad, head_index * head_size, head_size, 2)
        balance = jnp.zeros((sequences, tokens), dtype=jnp.float32)
        kept = []
        for branch in range(5):
            chosen, offset, query_sel, key_sel, value_sel, score = found[branch]
            stride = branch_strides[branch]
            slot_count = slot_counts[branch]
            total_sel = lax.dynamic_index_in_dim(
                total.reshape(sequences, slot_count, stride), offset, 2, keepdims=False
            )
            grad_sel = lax.dynamic_index_in_dim(
                out_grad.reshape(sequences, slot_count, stride, head_size),
                offset,
                2,
                keepdims=False,
            )
            prob = jnp.exp(score - total_sel[..., None])
            flow = jnp.einsum(
                "nqe,nke->nqk", grad_sel, value_sel, preferred_element_type=jnp.float32
            )
            balance = balance + jnp.where(
                chosen, jnp.sum(prob * flow, axis=-1)[..., None], 0.0
            ).reshape(sequences, tokens)
            kept.append((prob, flow, grad_sel))
        query_part = jnp.zeros((sequences, tokens, head_size), dtype=jnp.float32)
        key_parts = []
        for branch in range(5):
            chosen, offset, query_sel, key_sel, value_sel, score = found[branch]
            prob, flow, grad_sel = kept[branch]
            stride = branch_strides[branch]
            balance_sel = lax.dynamic_index_in_dim(
                balance.reshape(sequences, slot_counts[branch], stride), offset, 2, keepdims=False
            )
            slope = (prob * (flow - balance_sel[..., None])).astype(jnp.bfloat16)
            part = score_scale * jnp.einsum(
                "nqk,nke->nqe", slope, key_sel, preferred_element_type=jnp.float32
            )
            query_part = query_part + jnp.where(chosen[:, None], part[:, :, None, :], 0.0).reshape(
                sequences, tokens, head_size
            )
            key_term = score_scale * jnp.einsum(
                "nqk,nqe->nke", slope, query_sel, preferred_element_type=jnp.float32
            )
            value_term = jnp.einsum(
                "nqk,nqe->nke",
                prob.astype(jnp.bfloat16),
                grad_sel,
                preferred_element_type=jnp.float32,
            )
            key_parts.append(jnp.stack((key_term, value_term), 2))
        return (query_part, balance, tuple(key_parts))

    query_heads, balances, far_parts = lax.map(
        head_backward, (jnp.arange(head_count, dtype=jnp.int32), totals)
    )
    returned_sets = []
    for branch in range(5):
        shaped = far_parts[branch].transpose(1, 2, 3, 0, 4)
        returned_sets.append(shaped.reshape(sequences, shaped.shape[1], 2, model_width))
    owned = group_return(returned_sets, depth_list, device)
    pair_grad = spread_grads(owned[0], branch_strides[0], pickers[0])
    for branch in range(1, 5):
        pair_grad = pair_grad + spread_grads(owned[branch], branch_strides[branch], pickers[branch])
    key_grad = pair_grad[:, :, 0].astype(jnp.bfloat16)
    value_grad = pair_grad[:, :, 1].astype(jnp.bfloat16)
    query_grad = (
        query_heads.transpose(1, 2, 0, 3)
        .reshape(sequences, tokens, model_width)
        .astype(jnp.bfloat16)
    )
    grad_query_weight = weight_grad(h_first, query_grad)
    grad_query_bias = column_sum(query_grad)
    grad_key_weight = weight_grad(h_first, key_grad)
    grad_value_weight = weight_grad(h_first, value_grad)
    grad_value_bias = column_sum(value_grad)
    first_grad = (
        project_back(query_grad, query_weight)
        + project_back(key_grad, key_weight)
        + project_back(value_grad, value_weight)
    )
    first_pull = jax.vjp(layer_norm, layer_input, attn_norm_gain, attn_norm_bias)[1]
    input_part, grad_attn_norm_gain, grad_attn_norm_bias = first_pull(first_grad)
    input_grad = middle_grad + input_part
    summed = (
        lax.psum_scatter(grad_attn_norm_gain, "seq", scatter_dimension=0, tiled=True),
        lax.psum_scatter(grad_attn_norm_bias, "seq", scatter_dimension=0, tiled=True),
        lax.psum_scatter(grad_query_weight, "seq", scatter_dimension=0, tiled=True),
        lax.psum_scatter(grad_query_bias, "seq", scatter_dimension=0, tiled=True),
        lax.psum_scatter(grad_key_weight, "seq", scatter_dimension=0, tiled=True),
        lax.psum_scatter(grad_value_weight, "seq", scatter_dimension=0, tiled=True),
        lax.psum_scatter(grad_value_bias, "seq", scatter_dimension=0, tiled=True),
        lax.psum_scatter(grad_output_weight, "seq", scatter_dimension=0, tiled=True),
        lax.psum_scatter(grad_output_bias, "seq", scatter_dimension=0, tiled=True),
        lax.psum_scatter(grad_feed_norm_gain, "seq", scatter_dimension=0, tiled=True),
        lax.psum_scatter(grad_feed_norm_bias, "seq", scatter_dimension=0, tiled=True),
        lax.psum_scatter(grad_up_weight, "seq", scatter_dimension=0, tiled=True),
        lax.psum_scatter(grad_up_bias, "seq", scatter_dimension=0, tiled=True),
        lax.psum_scatter(grad_down_weight, "seq", scatter_dimension=0, tiled=True),
        lax.psum_scatter(grad_down_bias, "seq", scatter_dimension=0, tiled=True),
    )
    final = (
        lax.psum(summed[0].astype(jnp.bfloat16), "row").astype(jnp.float32),
        lax.psum(summed[1].astype(jnp.bfloat16), "row").astype(jnp.float32),
        lax.psum(summed[2].astype(jnp.bfloat16), "row").astype(jnp.float32),
        lax.psum(summed[3].astype(jnp.bfloat16), "row").astype(jnp.float32),
        lax.psum(summed[4].astype(jnp.bfloat16), "row").astype(jnp.float32),
        lax.psum(summed[5].astype(jnp.bfloat16), "row").astype(jnp.float32),
        lax.psum(summed[6].astype(jnp.bfloat16), "row").astype(jnp.float32),
        lax.psum(summed[7].astype(jnp.bfloat16), "row").astype(jnp.float32),
        lax.psum(summed[8].astype(jnp.bfloat16), "row").astype(jnp.float32),
        lax.psum(summed[9].astype(jnp.bfloat16), "row").astype(jnp.float32),
        lax.psum(summed[10].astype(jnp.bfloat16), "row").astype(jnp.float32),
        lax.psum(summed[11].astype(jnp.bfloat16), "row").astype(jnp.float32),
        lax.psum(summed[12].astype(jnp.bfloat16), "row").astype(jnp.float32),
        lax.psum(summed[13].astype(jnp.bfloat16), "row").astype(jnp.float32),
        lax.psum(summed[14].astype(jnp.bfloat16), "row").astype(jnp.float32),
    )
    return (
        result_out,
        input_grad,
        final[0],
        final[1],
        final[2],
        final[3],
        final[4],
        final[5],
        final[6],
        final[7],
        final[8],
        final[9],
        final[10],
        final[11],
        final[12],
        final[13],
        final[14],
    )


TOK = 384
HALF = TOK // 2
BLOCKS = 8
LEN = TOK * BLOCKS
SEG = LEN // 2
PAR = SEG // 2
TILE = 256
TILES = PAR // TILE
OWN_HEADS = 3
WIDTH = OWN_HEADS * HEAD_DIM
FAR = -1e9
LOG2E = math.log2(math.e)
BOTH = ("row", "seq")
VMEM_LIMIT = 56 * 1024 * 1024


def permutation(move):
    pairs = []
    for x in range(2):
        for core in range(2):
            for z in range(4):
                for y in range(2):
                    core_to, z_to, y_to, x_to = move(core, z, y, x)
                    source = (2 * x + core) * 8 + 2 * z + y
                    pairs.append((source, (2 * x_to + core_to) * 8 + 2 * z_to + y_to))
    return pairs


def inverse(pairs):
    return sorted((b, a) for a, b in pairs)


def send(array, pairs):
    return lax.ppermute(array, BOTH, pairs)


def to_row(slot):
    return permutation(lambda core, z, y, x: (z >> 1, 2 * core + (slot ^ (z & 1)), y, x))


SWAP_CORE = permutation(lambda core, z, y, x: (1 - core, z, y, x))
SWAP_X = permutation(lambda core, z, y, x: (core, z, y, 1 - x))
SWAP_Y = permutation(lambda core, z, y, x: (core, z, 1 - y, x))
SWAP_Z_LOW = permutation(lambda core, z, y, x: (core, z ^ 1, y, x))
SWAP_Z_HIGH = permutation(lambda core, z, y, x: (core, z ^ 2, y, x))


def to_owner(delta):
    high, low, side = delta >> 2, delta >> 1 & 1, delta & 1
    return permutation(
        lambda core, z, y, x: (z >> 1, 2 * (core ^ high) + ((z & 1) ^ low), y ^ side, x)
    )


def pick(bit, zero, one):
    return jnp.where(bit == 0, zero, one)


def halves(array, bit, axis=0):
    first, second = jnp.split(array, 2, axis)
    return pick(bit, first, second), pick(bit, second, first)


def joined(mine, other, bit, axis=0):
    return jnp.concatenate((pick(bit, mine, other), pick(bit, other, mine)), axis)


def columns(width):
    return [(part, slice(128 * part, 128 * (part + 1))) for part in range(width // 128)]


def read_sorted(in_ref, lanes):
    for part, column in columns(in_ref.shape[-1]):
        lanes[part] = in_ref[0, :, column]
    return [
        jnp.concatenate(
            [
                lanes[part, pl.ds(parity, HALF, stride=2), :]
                for part, _ in columns(in_ref.shape[-1])
            ],
            -1,
        )
        for parity in range(2)
    ]


def write_unsorted(out_ref, lanes, found):
    for part, column in columns(out_ref.shape[-1]):
        for parity in range(2):
            lanes[part, pl.ds(parity, HALF, stride=2), :] = found[parity][:, column]
        out_ref[0, :, column] = lanes[part]


def lanes_of(width):
    return [pltpu.VMEM((width // 128, TOK, 128), jnp.float32)]


def norm_kernel(swap_ref, in_ref, gain_ref, bias_ref, sorted_ref, out_ref, lanes):
    for parity, values in enumerate(read_sorted(in_ref, lanes)):
        rows = pl.ds(parity * HALF, HALF)
        sorted_ref[0, rows, :] = values
        out_ref[0, rows, :] = layer_norm(values, gain_ref[...], bias_ref[...]).astype(jnp.bfloat16)


def first_norm(swap, inputs, gain, bias):
    width = inputs.shape[-1]
    block = (1, TOK, width)
    vector = pl.BlockSpec((1, width), lambda slot, swap: (0, 0))
    own = pl.BlockSpec(block, lambda slot, swap: (slot, 0, 0))
    return pl.pallas_call(
        norm_kernel,
        grid_spec=pltpu.PrefetchScalarGridSpec(
            num_scalar_prefetch=1,
            grid=(2,),
            in_specs=[
                pl.BlockSpec(block, lambda slot, swap: (slot ^ swap[0], 0, 0)),
                vector,
                vector,
            ],
            out_specs=[own, own],
            scratch_shapes=lanes_of(width),
        ),
        out_shape=[
            jax.ShapeDtypeStruct(inputs.shape, jnp.float32),
            jax.ShapeDtypeStruct(inputs.shape, jnp.bfloat16),
        ],
        name="first_norm",
    )(swap, inputs, gain[None], bias[None])


def sort_kernel(swap_ref, in_ref, out_ref, lanes):
    for parity, values in enumerate(read_sorted(in_ref, lanes)):
        out_ref[0, pl.ds(parity * HALF, HALF), :] = values


def unsort_kernel(swap_ref, in_ref, out_ref, lanes):
    found = [in_ref[0, pl.ds(parity * HALF, HALF), :] for parity in range(2)]
    write_unsorted(out_ref, lanes, found)


def moved(kernel, swap, array):
    block = (1, TOK, array.shape[-1])
    return pl.pallas_call(
        kernel,
        grid_spec=pltpu.PrefetchScalarGridSpec(
            num_scalar_prefetch=1,
            grid=(2,),
            in_specs=[pl.BlockSpec(block, lambda slot, swap: (slot ^ swap[0], 0, 0))],
            out_specs=pl.BlockSpec(block, lambda slot, swap: (slot, 0, 0)),
            scratch_shapes=lanes_of(block[-1]),
        ),
        out_shape=jax.ShapeDtypeStruct(array.shape, array.dtype),
        name=kernel.__name__,
    )(swap, array)


def norm_back(values, grads, gain):
    center = values - jnp.mean(values, axis=-1, keepdims=True)
    scale = lax.rsqrt(jnp.mean(center * center, axis=-1, keepdims=True) + EPS)
    unit = center * scale
    scaled = grads * gain
    mean_scaled = jnp.mean(scaled, axis=-1, keepdims=True)
    mean_both = jnp.mean(scaled * unit, axis=-1, keepdims=True)
    return scale * (scaled - mean_scaled - unit * mean_both)


def last_kernel(swap_ref, values_ref, grads_ref, through_ref, gain_ref, out_ref, lanes):
    found = []
    for parity in range(2):
        rows = pl.ds(parity * HALF, HALF)
        grads = grads_ref[0, rows, :].astype(jnp.float32)
        part = norm_back(values_ref[0, rows, :], grads, gain_ref[...])
        found.append(through_ref[0, rows, :] + part)
    write_unsorted(out_ref, lanes, found)


def last_norm(swap, values, grads, through, gain):
    width = values.shape[-1]
    block = (1, TOK, width)
    own = pl.BlockSpec(block, lambda slot, swap: (slot ^ swap[0], 0, 0))
    return pl.pallas_call(
        last_kernel,
        grid_spec=pltpu.PrefetchScalarGridSpec(
            num_scalar_prefetch=1,
            grid=(2,),
            in_specs=[own, own, own, pl.BlockSpec((1, width), lambda slot, swap: (0, 0))],
            out_specs=pl.BlockSpec(block, lambda slot, swap: (slot, 0, 0)),
            scratch_shapes=lanes_of(block[-1]),
        ),
        out_shape=jax.ShapeDtypeStruct(values.shape, jnp.float32),
        name="last_norm",
    )(swap, values, grads, through, gain[None])


NT = (((1,), (1,)), ((), ()))
NN = (((1,), (0,)), ((), ()))


def dot(left, right, dims):
    return lax.dot_general(left, right, dims, preferred_element_type=jnp.float32)


def pieces():
    for block in range(BLOCKS):
        for parity in range(2):
            place = block // 4 * SEG + parity * PAR + block % 4 * HALF
            yield block, parity, place


def load_row(place, parity_of_head, triple_ref, query_mark, key_mark, far_mark, query, far, key):
    for block, parity, start in pieces():
        rows = pl.ds(parity * HALF, HALF)
        delta = place ^ block
        query[pl.ds(start, HALF), :] = (
            triple_ref[delta, rows, 0:128] + query_mark[0, pl.ds(start, HALF), :]
        )
        key[pl.ds(start, HALF), :] = (
            triple_ref[delta, rows, 128:256] + key_mark[0, pl.ds(start, HALF), :]
        )
    for block in range(4):
        rows = pl.ds(pl.multiple_of(parity_of_head * HALF, HALF), HALF)
        far[pl.ds(block * HALF, HALF), :] = (
            triple_ref[place ^ (block + 4), rows, 0:128]
            + far_mark[0, pl.ds(block * HALF, HALF), :]
        )


def causal(parts, later):
    keys = lax.broadcasted_iota(jnp.int32, parts.shape, 0)
    queries = lax.broadcasted_iota(jnp.int32, parts.shape, 1)
    return jnp.where(keys <= queries + later, parts, NEG)


def aligned(start):
    return pl.multiple_of(start, TILE)


def groups(index):
    segment, query_parity, key_parity = index >> 2, index >> 1 & 1, index & 1
    query_base = segment * SEG + query_parity * PAR
    key_base = segment * SEG + key_parity * PAR
    later = jnp.where(query_parity < key_parity, -1, 0)
    return query_base, key_base, later


def forward_kernel(
    info, triple_ref, query_mark, key_mark, far_mark, send_ref, result_ref, total_ref,
    query, far, key, value, value_t, most, acc,
):
    head = pl.program_id(0)
    place = info[0]
    parity_of_head = (info[1] + head) & 1
    load_row(
        place, parity_of_head, triple_ref, query_mark, key_mark, far_mark, query, far, key
    )
    ones = jnp.where(lax.broadcasted_iota(jnp.int32, (HALF, 128), 1) == HEAD_DIM, 1.0, 0.0)
    for block, parity, start in pieces():
        rows = pl.ds(parity * HALF, HALF)
        value[pl.ds(start, HALF), :] = (
            triple_ref[place ^ block, rows, 256:384].astype(jnp.float32) + ones
        )
    for tile in range(LEN // TILE):
        cols = pl.ds(tile * TILE, TILE)
        value_t[:, cols] = value[cols, :].T.astype(jnp.bfloat16)
    most[...] = jnp.full(most.shape, NEG, jnp.float32)
    acc[...] = jnp.zeros(acc.shape, jnp.float32)

    def update(column, parts):
        cols = pl.ds(column, TILE)
        old = most[0:1, cols]
        new = old
        for scores, _, _ in parts:
            new = jnp.maximum(new, jnp.max(scores, axis=0, keepdims=True))
        total = acc[:, cols] * jnp.exp2(old - new)
        for scores, start, count in parts:
            prob = jnp.exp2(scores - new).astype(jnp.bfloat16)
            total = total + dot(value_t[0:80, pl.ds(start, count)], prob, NN)
        acc[:, cols] = total
        most[0:1, cols] = new

    def near(index, carry):
        query_base, key_base, later = groups(index)
        for tile in range(TILES):
            column = aligned(query_base + tile * TILE)
            queries = query[pl.ds(column, TILE), :]
            parts = []
            if tile:
                start = aligned(key_base)
                scores = dot(key[pl.ds(start, tile * TILE), :], queries, NT)
                parts.append((scores, start, tile * TILE))
            start = aligned(key_base + tile * TILE)
            scores = causal(dot(key[pl.ds(start, TILE), :], queries, NT), later)
            parts.append((scores, start, TILE))
            update(column, parts)
        return carry

    lax.fori_loop(0, 8, near, 0)
    start = aligned(parity_of_head * PAR)
    for tile in range(TILES):
        queries = far[pl.ds(tile * TILE, TILE), :]
        scores = dot(key[pl.ds(start, PAR), :], queries, NT)
        update(aligned(SEG + parity_of_head * PAR + tile * TILE), [(scores, start, PAR)])

    weight = acc[HEAD_DIM : HEAD_DIM + 1, :]
    result = acc[0:HEAD_DIM, :] / weight
    result_ref[0] = result
    total_ref[0] = jnp.broadcast_to(most[0:1, :] + jnp.log2(weight), (8, LEN))
    heads = pl.ds(pl.multiple_of(head * HEAD_DIM, HEAD_DIM), HEAD_DIM)
    for block, parity, start in pieces():
        send_ref[place ^ block, heads, parity * HALF : (parity + 1) * HALF] = result[
            :, start : start + HALF
        ].astype(jnp.bfloat16)


def backward_kernel(
    info, triple_ref, query_mark, key_mark, far_mark, grad_ref, result_ref, total_ref, out_ref,
    query, far, key, value, key_t, grad_t, balance, query_grad, key_grad, value_grad, turned,
):
    head = pl.program_id(0)
    place = info[0]
    parity_of_head = (info[1] + head) & 1
    load_row(
        place, parity_of_head, triple_ref, query_mark, key_mark, far_mark, query, far, key
    )
    heads = pl.ds(pl.multiple_of(head * HEAD_DIM, HEAD_DIM), HEAD_DIM)
    grad_t[HEAD_DIM:128, :] = jnp.zeros((128 - HEAD_DIM, LEN), jnp.bfloat16)
    for block, parity, start in pieces():
        rows = pl.ds(parity * HALF, HALF)
        delta = place ^ block
        value[pl.ds(start, HALF), :] = triple_ref[delta, rows, 256:384]
        grad_t[0:HEAD_DIM, start : start + HALF] = grad_ref[
            delta, heads, parity * HALF : (parity + 1) * HALF
        ]
    for tile in range(LEN // TILE):
        cols = pl.ds(tile * TILE, TILE)
        key_t[:, cols] = key[cols, :].astype(jnp.float32).T.astype(jnp.bfloat16)
    balance[...] = jnp.sum(
        grad_t[0:HEAD_DIM, :].astype(jnp.float32) * result_ref[0], axis=0, keepdims=True
    )
    query_grad[...] = jnp.zeros(query_grad.shape, jnp.float32)
    key_grad[...] = jnp.zeros(key_grad.shape, jnp.float32)
    value_grad[...] = jnp.zeros(value_grad.shape, jnp.float32)

    def update(column, queries, start, count, later):
        cols = pl.ds(column, TILE)
        rows = pl.ds(start, count)
        scores = dot(key[rows, :], queries, NT)
        if later is not None:
            scores = causal(scores, later)
        prob = jnp.exp2(scores - total_ref[0, 0:1, cols])
        grads = grad_t[:, cols]
        flow = dot(value[rows, :], grads, NN)
        slope = (prob * (flow - balance[0:1, cols])).astype(jnp.bfloat16)
        value_grad[rows, :] += dot(prob.astype(jnp.bfloat16), grads, NT)
        key_grad[rows, :] += dot(slope, queries, NN)
        query_grad[0:HEAD_DIM, cols] += dot(key_t[0:HEAD_DIM, rows], slope, NN)

    def near(index, carry):
        query_base, key_base, later = groups(index)
        for tile in range(TILES):
            column = aligned(query_base + tile * TILE)
            queries = query[pl.ds(column, TILE), :]
            if tile:
                update(column, queries, aligned(key_base), tile * TILE, None)
            update(column, queries, aligned(key_base + tile * TILE), TILE, later)
        return carry

    lax.fori_loop(0, 8, near, 0)
    start = aligned(parity_of_head * PAR)
    for tile in range(TILES):
        queries = far[pl.ds(tile * TILE, TILE), :]
        column = aligned(SEG + parity_of_head * PAR + tile * TILE)
        update(column, queries, start, PAR, None)

    for tile in range(LEN // TILE):
        cols = pl.ds(tile * TILE, TILE)
        turned[cols, :] = query_grad[:, cols].T
    first = lax.broadcasted_iota(jnp.int32, (HALF, 128), 1) < HEAD_DIM
    for block, parity, start in pieces():
        rows = pl.ds(parity * HALF, HALF)
        delta = place ^ block
        own = pl.ds(start, HALF)
        pair = jnp.where(
            first,
            turned[own, :] * HEAD_DIM**-0.5,
            pltpu.roll(key_grad[own, :], HEAD_DIM, axis=1) * (1 / LOG2E),
        )
        out_ref[delta, rows, 0:128] = pair.astype(jnp.bfloat16)
        out_ref[delta, rows, 128:256] = jnp.where(first, value_grad[own, :], 0.0).astype(
            jnp.bfloat16
        )


def whole(*shape):
    return pl.BlockSpec(shape, lambda head, info: (0,) * len(shape))


def per_head(*shape):
    return pl.BlockSpec((1, *shape), lambda head, info: (head, *(0,) * len(shape)))


def triple_spec():
    return pl.BlockSpec((BLOCKS, TOK, 384), lambda head, info: (0, 0, head))


def attention(info, triples, query_mark, key_mark, far_mark):
    return pl.pallas_call(
        forward_kernel,
        grid_spec=pltpu.PrefetchScalarGridSpec(
            num_scalar_prefetch=1,
            grid=(OWN_HEADS,),
            in_specs=[
                triple_spec(),
                per_head(LEN, 128),
                per_head(LEN, 128),
                per_head(PAR, 128),
            ],
            out_specs=[whole(BLOCKS, WIDTH, TOK), per_head(HEAD_DIM, LEN), per_head(8, LEN)],
            scratch_shapes=[
                pltpu.VMEM((LEN, 128), jnp.bfloat16),
                pltpu.VMEM((PAR, 128), jnp.bfloat16),
                pltpu.VMEM((LEN, 128), jnp.bfloat16),
                pltpu.VMEM((LEN, 128), jnp.float32),
                pltpu.VMEM((128, LEN), jnp.bfloat16),
                pltpu.VMEM((8, LEN), jnp.float32),
                pltpu.VMEM((80, LEN), jnp.float32),
            ],
        ),
        out_shape=[
            jax.ShapeDtypeStruct((BLOCKS, WIDTH, TOK), jnp.bfloat16),
            jax.ShapeDtypeStruct((OWN_HEADS, HEAD_DIM, LEN), jnp.float32),
            jax.ShapeDtypeStruct((OWN_HEADS, 8, LEN), jnp.float32),
        ],
        compiler_params=pltpu.CompilerParams(vmem_limit_bytes=VMEM_LIMIT),
        name="attention",
    )(info, triples, query_mark, key_mark, far_mark)


def attention_back(info, triples, query_mark, key_mark, far_mark, grads, result, total):
    return pl.pallas_call(
        backward_kernel,
        grid_spec=pltpu.PrefetchScalarGridSpec(
            num_scalar_prefetch=1,
            grid=(OWN_HEADS,),
            in_specs=[
                triple_spec(),
                per_head(LEN, 128),
                per_head(LEN, 128),
                per_head(PAR, 128),
                whole(BLOCKS, WIDTH, TOK),
                per_head(HEAD_DIM, LEN),
                per_head(8, LEN),
            ],
            out_specs=pl.BlockSpec((BLOCKS, TOK, 256), lambda head, info: (0, 0, head)),
            scratch_shapes=[
                pltpu.VMEM((LEN, 128), jnp.bfloat16),
                pltpu.VMEM((PAR, 128), jnp.bfloat16),
                pltpu.VMEM((LEN, 128), jnp.bfloat16),
                pltpu.VMEM((LEN, 128), jnp.bfloat16),
                pltpu.VMEM((128, LEN), jnp.bfloat16),
                pltpu.VMEM((128, LEN), jnp.bfloat16),
                pltpu.VMEM((1, LEN), jnp.float32),
                pltpu.VMEM((128, LEN), jnp.float32),
                pltpu.VMEM((LEN, 128), jnp.float32),
                pltpu.VMEM((LEN, 128), jnp.float32),
                pltpu.VMEM((LEN, 128), jnp.float32),
            ],
        ),
        out_shape=jax.ShapeDtypeStruct((BLOCKS, TOK, OWN_HEADS * 256), jnp.bfloat16),
        compiler_params=pltpu.CompilerParams(vmem_limit_bytes=VMEM_LIMIT),
        name="attention_back",
    )(info, triples, query_mark, key_mark, far_mark, grads, result, total)


def marks(first_head, first_doc, padding):
    heads = first_head + jnp.arange(OWN_HEADS, dtype=jnp.int32)[:, None, None]
    column = jnp.arange(128, dtype=jnp.int32)[None, None, :] - HEAD_DIM

    def members(place, dilation):
        return (place - heads) % dilation == 0

    def kind(place):
        fifth, fourth, third, second = (
            members(place, dilation)
            for dilation in (FIFTH_DILATION, FOURTH_DILATION, THIRD_DILATION, SECOND_DILATION)
        )
        found = jnp.where(fifth, 0, jnp.where(fourth, 1, jnp.where(third, 2, 3)))
        return jnp.where(second, found, 4)

    def document(place):
        return jnp.where(place < first_doc, 0, jnp.where(place >= LEN - padding, 2, 1))

    index = jnp.arange(LEN, dtype=jnp.int32)
    place = (index // SEG * SEG + index % PAR * 2 + index // PAR % 2)[None, :, None]
    own, doc = kind(place), document(place)
    query = (
        ((column >= 0) & (column < 4) & (own == column))
        | ((column >= 4) & (column < 8) & (own == column - 4))
        | ((column >= 8) & (column < 11) & (doc == column - 8))
    ).astype(jnp.bfloat16)

    far_place = SEG + 2 * jnp.arange(PAR, dtype=jnp.int32)[None, :, None] + heads % 2
    far_own, far_doc = kind(far_place), document(far_place)
    far = (
        ((column >= 8) & (column < 11) & (far_doc == column - 8))
        | ((column >= 12) & (column < 16) & (far_own == column - 12))
    ).astype(jnp.bfloat16)

    row = column & 3
    count = (
        2
        + ((row % 2 == 0) & (own % 2 == 0)).astype(jnp.int32)
        + ((row < 2) & (own < 2)).astype(jnp.int32)
        + ((row == 0) & (own == 0)).astype(jnp.int32)
    )

    def rounded(value):
        return round(value * 64) / 64

    log3, log5 = math.log2(3), math.log2(5)
    high = jnp.where(count == 2, 1.0, jnp.where(count == 3, rounded(log3), rounded(log5)))
    low = jnp.where(
        count == 2,
        0.0,
        jnp.where(count == 3, log3 - rounded(log3), log5 - rounded(log5)),
    )
    across = jnp.where(count == 2, 0.0, jnp.where(count == 3, 1.0, 2.0))
    even = own < 4
    key = jnp.where((column >= 0) & (column < 4) & even, high, 0.0)
    key = jnp.where((column >= 4) & (column < 8) & even, low, key)
    key = jnp.where((column >= 8) & (column < 11) & (doc != column - 8), FAR, key)
    key = jnp.where((column >= 12) & (column < 16) & even, across, key)
    return query, key.astype(jnp.bfloat16), far


def flipped(array, axis, bit):
    zero, one = (lax.index_in_dim(array, i, axis, keepdims=False) for i in range(2))
    return jnp.stack((pick(bit, zero, one), pick(bit, one, zero)), axis)


def summed(array, core, x, y, z):
    def add(parts, pairs):
        keep, away = parts
        return (keep.astype(jnp.float32) + send(away, pairs).astype(jnp.float32)).astype(
            jnp.bfloat16
        )

    array = add(halves(array, core, 1), SWAP_CORE)
    array = add(halves(array, x, 1), SWAP_X)
    count, width = array.shape[1:]
    array = add(halves(array.reshape(2, 2, 2, count, width), y, 2), SWAP_Y)
    array = add(halves(array, z >> 1, 0), SWAP_Z_HIGH)
    array = add(halves(array, z & 1, 1), SWAP_Z_LOW)
    array = array.reshape(count, width)
    array = joined(array, send(array, SWAP_X), x)
    return joined(array, send(array, SWAP_CORE), core)


def summed_heads(array, core, x, y, z):
    def add(parts, pairs):
        keep, away = parts
        return (keep.astype(jnp.float32) + send(away, pairs).astype(jnp.float32)).astype(
            jnp.bfloat16
        )

    array = add(halves(array, x, 1), SWAP_X)
    count, width = array.shape[1:]
    array = array.reshape(2, 2, 2, count, width)
    array = add(halves(array, z >> 1, 0), SWAP_Z_HIGH)
    array = add(halves(array, z & 1, 1), SWAP_Z_LOW)
    keep, away = halves(array.reshape(2, count, width), y)
    array = joined(keep, send(away, SWAP_Y), y)
    array = jnp.stack((array, send(array, SWAP_CORE)), 1)
    array = flipped(array, 1, core)
    return joined(array, send(array, SWAP_X), x, 2)


def packed_rows(
    layer_input, doc_ids, cotangent, attn_norm_gain, attn_norm_bias, query_weight, query_bias,
    key_weight, value_weight, value_bias, output_weight, output_bias, feed_norm_gain,
    feed_norm_bias, up_weight, up_bias, down_weight, down_bias,
):
    bf16, f32 = jnp.bfloat16, jnp.float32
    model = layer_input.shape[-1]
    hidden_width = up_weight.shape[-1]
    row, seq = lax.axis_index("row"), lax.axis_index("seq")
    x, core, z, y = row >> 1, row & 1, seq >> 1, seq & 1
    swap = (z & 1)[None].astype(jnp.int32)
    place = 4 * core + 2 * (z & 1) + y
    group = 2 * y + core
    info = jnp.stack((place, OWN_HEADS * group)).astype(jnp.int32)

    ordered, first = first_norm(swap, layer_input, attn_norm_gain, attn_norm_bias)

    held = []
    for slot in range(2):
        block = send(first[slot], to_row(slot))
        held.extend((block, send(block, SWAP_Y)))
    held.extend([send(block, SWAP_CORE) for block in held])
    normed = jnp.stack(held)

    counts = jnp.stack((jnp.sum(doc_ids == 0, axis=1), jnp.sum(doc_ids < 0, axis=1)), 1)
    counts = lax.all_gather(counts.astype(jnp.int32).reshape(1, 4), BOTH, tiled=True)
    counts = jnp.sum(counts.reshape(4, 8, 2, 2), axis=1).reshape(2, 4, 2)
    counts = lax.dynamic_index_in_dim(counts, x, 0, keepdims=False)
    counts = lax.dynamic_index_in_dim(counts, z, 0, keepdims=False)
    query_mark, key_mark, far_mark = marks(OWN_HEADS * group, counts[0], counts[1])

    def own_columns(weight):
        own = lax.dynamic_slice_in_dim(weight, group * WIDTH, WIDTH, weight.ndim - 1)
        return own.reshape(*weight.shape[:-1], OWN_HEADS, HEAD_DIM)

    query_own, key_own, value_own = map(own_columns, (query_weight, key_weight, value_weight))
    triple_weight = jnp.stack((query_own, key_own, value_own), 2)
    triple_weight = jnp.pad(triple_weight, ((0, 0),) * 3 + ((0, 128 - HEAD_DIM),))
    triple_weight = triple_weight.reshape(model, OWN_HEADS * 384)
    query_row, value_row = own_columns(query_bias), own_columns(value_bias)
    triple_bias = jnp.stack((query_row, jnp.zeros_like(query_row), value_row), 1)
    triple_bias = jnp.pad(triple_bias, ((0, 0), (0, 0), (0, 128 - HEAD_DIM))).reshape(-1)
    scale = jnp.where(jnp.arange(OWN_HEADS * 384) % 384 < 128, LOG2E * HEAD_DIM**-0.5, 1.0)
    triples = jnp.einsum("btd,df->btf", normed, triple_weight, preferred_element_type=f32)
    triples = ((triples + triple_bias) * scale).astype(bf16)

    sends, result, total = attention(info, triples, query_mark, key_mark, far_mark)
    slabs = [send(sends[delta], to_owner(delta)) for delta in range(8)]
    attended = jnp.stack(
        [
            jnp.concatenate([slabs[4 * high + 2 * slot + side] for side in (0, 1) for high in (0, 1)])
            for slot in range(2)
        ]
    )

    def other_order(array):
        array = array.reshape(2, 2, WIDTH, model)
        return flipped(flipped(array, 0, y), 1, z >> 1).reshape(4 * WIDTH, model)

    output_own = other_order(output_weight)
    docs = doc_ids.reshape(2, HALF, 2).transpose(0, 2, 1).reshape(2, TOK)
    docs = flipped(docs, 0, z & 1)
    masked_grad = jnp.where((docs >= 0)[..., None], moved(sort_kernel, swap, cotangent), 0.0)
    down_grad = masked_grad.astype(bf16)
    active_grad = project_back(down_grad, down_weight)

    middle = ordered + output_bias
    middle = middle + jnp.einsum("nft,fd->ntd", attended, output_own, preferred_element_type=f32)
    second = layer_norm(middle, feed_norm_gain, feed_norm_bias).astype(bf16)
    hidden = project(second, up_weight) + up_bias
    active_full, gelu_pull = jax.vjp(jax.nn.gelu, hidden)
    active = active_full.astype(bf16)
    hidden_grad = gelu_pull(active_grad)[0].astype(bf16)
    middle_part = norm_back(middle, project_back(hidden_grad, up_weight), feed_norm_gain)
    middle_grad = masked_grad + middle_part
    branch_grad = middle_grad.astype(bf16)
    attended_grad = jnp.einsum("fd,ntd->nft", output_own, branch_grad, preferred_element_type=f32)
    attended_grad = attended_grad.astype(bf16).reshape(2, 2, 2, WIDTH, TOK)
    grads = jnp.stack(
        [
            send(attended_grad[delta >> 1 & 1, delta & 1, delta >> 2], inverse(to_owner(delta)))
            for delta in range(8)
        ]
    )

    out = moved(unsort_kernel, swap, middle + project(active, down_weight) + down_bias)
    grad_down = weight_grad(active, down_grad)
    grad_up = weight_grad(second, hidden_grad)
    grad_output = jnp.einsum("nft,ntd->fd", attended, branch_grad, preferred_element_type=f32)
    grad_output = other_order(grad_output)
    early = jnp.concatenate(
        (
            grad_output.astype(bf16).reshape(8, -1, model),
            grad_up.astype(bf16).reshape(8, -1, model),
            grad_down.astype(bf16).reshape(8, -1, model),
        ),
        1,
    )
    early = summed(early, core, x, y, z).astype(f32)
    output_rows = model // 8
    up_rows = output_rows * hidden_width // model
    grad_output = early[:output_rows]
    grad_up = early[output_rows : output_rows + up_rows].reshape(model // 8, hidden_width)
    grad_down = early[output_rows + up_rows :]

    triple_grad = attention_back(
        info, triples, query_mark, key_mark, far_mark, grads, result, total
    )
    back_weight = jnp.stack((query_own, key_own, value_own, jnp.zeros_like(key_own)), 2)
    back_weight = back_weight.reshape(model, OWN_HEADS * 256)
    first_grad = jnp.einsum("btf,df->btd", triple_grad, back_weight, preferred_element_type=f32)
    far_half = send(first_grad[4:].astype(bf16), SWAP_CORE)
    near_half = first_grad[:4] + far_half.astype(f32)
    near_half = near_half.reshape(2, 2, TOK, model)
    returned = []
    for slot in range(2):
        other = send(near_half[slot, 1].astype(bf16), SWAP_Y)
        both = (near_half[slot, 0] + other.astype(f32)).astype(bf16)
        returned.append(send(both, inverse(to_row(slot))))
    input_grad = last_norm(swap, ordered, jnp.stack(returned), middle_grad, attn_norm_gain)

    triple_sum = jnp.sum(triple_grad.astype(f32), axis=(0, 1)).reshape(OWN_HEADS, 4, HEAD_DIM)
    triple_sum = triple_sum[:, :3].transpose(1, 0, 2).reshape(3, 1, WIDTH)
    triple_sum = jnp.where(jnp.arange(4)[:, None] == group, triple_sum, 0.0).reshape(-1)
    sums = jnp.concatenate(
        (triple_sum, column_sum(branch_grad), column_sum(hidden_grad), column_sum(down_grad))
    )
    sums = lax.psum(sums, BOTH)
    query_sum, key_sum, value_sum, output_sum, up_sum, down_sum = jnp.split(
        sums, (model, 2 * model, 3 * model, 4 * model, 4 * model + hidden_width)
    )

    late = jnp.einsum("btd,btf->df", normed, triple_grad, preferred_element_type=f32)
    late = late.reshape(model, OWN_HEADS, 4, HEAD_DIM)[:, :, :3].transpose(0, 2, 1, 3)
    late = late.astype(bf16).reshape(8, model // 8, 3 * WIDTH)
    late = summed_heads(late, core, x, y, z).astype(f32)
    late = late.reshape(4, model // 8, 3, WIDTH).transpose(2, 1, 0, 3)
    grad_query, grad_key, grad_value = late.reshape(3, model // 8, model)

    def own_rows(array):
        count = array.shape[0] // 8
        return lax.dynamic_slice_in_dim(array, seq * count, count, 0)

    def norm_grads(gain, bias, parts):
        bias_grad = jnp.zeros((model // 8,), f32)
        both = bias_grad
        for weight, grad, total in parts:
            mine = own_rows(weight).astype(f32)
            bias_grad = bias_grad + jnp.sum(mine * total, axis=1)
            both = both + jnp.sum(mine * grad, axis=1)
        return (both - own_rows(bias) * bias_grad) / own_rows(gain), bias_grad

    grad_feed_gain, grad_feed_bias = norm_grads(
        feed_norm_gain, feed_norm_bias, ((up_weight, grad_up, up_sum),)
    )
    grad_attn_gain, grad_attn_bias = norm_grads(
        attn_norm_gain,
        attn_norm_bias,
        (
            (query_weight, grad_query, query_sum),
            (key_weight, grad_key, key_sum),
            (value_weight, grad_value, value_sum),
        ),
    )
    return (
        out,
        input_grad,
        grad_attn_gain,
        grad_attn_bias,
        grad_query,
        own_rows(query_sum),
        grad_key,
        grad_value,
        own_rows(value_sum),
        grad_output,
        own_rows(output_sum),
        grad_feed_gain,
        grad_feed_bias,
        grad_up,
        own_rows(up_sum),
        grad_down,
        own_rows(down_sum),
    )


def solution(mesh):
    placed = (
        P("row", "seq", None),
        P("row", "seq"),
        P("row", "seq", None),
        P(),
        P(),
        P(),
        P(),
        P(),
        P(),
        P(),
        P(),
        P(),
        P(),
        P(),
        P(),
        P(),
        P(),
        P(),
    )
    chosen = packed_rows if dict(mesh.shape) == {"row": 4, "seq": 8} else per_device
    return jax.shard_map(
        chosen,
        mesh=mesh,
        in_specs=placed,
        out_specs=(
            P("row", "seq", None),
            P("row", "seq", None),
            P("seq"),
            P("seq"),
            P("seq", None),
            P("seq"),
            P("seq", None),
            P("seq", None),
            P("seq"),
            P("seq", None),
            P("seq"),
            P("seq"),
            P("seq"),
            P("seq", None),
            P("seq"),
            P("seq", None),
            P("seq"),
        ),
        check_vma=False,
    )
```

```python
import functools
import math

import jax
import jax.numpy as jnp
from jax import lax
from jax.experimental import pallas as pl
from jax.experimental.pallas import tpu as pltpu
from jax.sharding import PartitionSpec as P

HEADS = 12
HEAD_DIM = 64
GROUP = 4
FIRST_DILATION = 1
SECOND_DILATION = 2
THIRD_DILATION = 4
FOURTH_DILATION = 6
FIFTH_DILATION = 12


EPS = 1e-05
NEG = -1e30
HIGH = lax.Precision.HIGHEST


def swapped(array, axis, apart):
    return lax.ppermute(array, axis, [(i, i ^ 1 << apart) for i in range(lax.axis_size(axis))])


def for_sending(array):

    def short(part):
        return part.astype(jnp.bfloat16) if part.dtype == jnp.float32 else part

    return jax.tree.map(short, array)


def layer_norm(values, gain, bias):
    center = values - jnp.mean(values, axis=-1, keepdims=True)
    spread = jnp.mean(center * center, axis=-1, keepdims=True)
    return center * lax.rsqrt(spread + EPS) * gain + bias


def project(inputs, weight):
    return jnp.einsum("ntd,df->ntf", inputs, weight, preferred_element_type=jnp.float32)


def project_back(grads, weight):
    return jnp.einsum("ntf,df->ntd", grads, weight, preferred_element_type=jnp.float32)


def weight_grad(inputs, grads):
    return jnp.einsum("ntd,ntf->df", inputs, grads, preferred_element_type=jnp.float32)


def column_sum(grads):
    return jnp.sum(grads.astype(jnp.float32), axis=(0, 1))


def pick_pairs(values, stride, picker):
    sequences, tokens, kinds, model_width = values.shape
    head_count = picker.shape[1]
    shaped = values.reshape(
        sequences, tokens // stride, stride, kinds, head_count, model_width // head_count
    )
    picked = jnp.einsum(
        "nsrche,rh->nsche", shaped, picker.astype(jnp.bfloat16), preferred_element_type=jnp.float32
    )
    return picked.astype(jnp.bfloat16).reshape(sequences, tokens // stride, kinds, model_width)


def spread_grads(values, stride, picker):
    sequences, slot_count, kinds, model_width = values.shape
    head_count = picker.shape[1]
    shaped = values.reshape(sequences, slot_count, kinds, head_count, model_width // head_count)
    spread = jnp.einsum("nsche,rh->nsrche", shaped, picker.astype(jnp.float32), precision=HIGH)
    return spread.reshape(sequences, slot_count * stride, kinds, model_width)


def group_gather(pieces, depth_list, device):
    gathered = list(pieces)
    for bit_index in range(max(depth_list)):
        active = [branch for branch in range(len(pieces)) if depth_list[branch] > bit_index]
        packed = jnp.concatenate([gathered[branch] for branch in active], 1)
        partner = swapped(packed, "seq", bit_index)
        lower = device // 2**bit_index % 2 == 0
        start = 0
        for branch in active:
            count = gathered[branch].shape[1]
            other = partner[:, start : start + count]
            start = start + count
            gathered[branch] = jnp.where(
                lower,
                jnp.concatenate((gathered[branch], other), 1),
                jnp.concatenate((other, gathered[branch]), 1),
            )
    return gathered


def group_return(pieces, depth_list, device):
    held = list(pieces)
    for bit_index in range(max(depth_list)):
        active = [branch for branch in range(len(pieces)) if depth_list[branch] > bit_index]
        lower = device // 2**bit_index % 2 == 0
        keep_parts = []
        send_parts = []
        for branch in active:
            sequences, count, kinds, model_width = held[branch].shape
            devices_left = 2 ** (depth_list[branch] - bit_index)
            slot_count = count // devices_left
            shaped = held[branch].reshape(
                sequences, devices_left // 2, 2, slot_count, kinds, model_width
            )
            even_part = shaped[:, :, 0].reshape(sequences, count // 2, kinds, model_width)
            odd_part = shaped[:, :, 1].reshape(sequences, count // 2, kinds, model_width)
            keep_parts.append(jnp.where(lower, even_part, odd_part))
            send_parts.append(jnp.where(lower, odd_part, even_part))
        received = swapped(for_sending(jnp.concatenate(send_parts, 1)), "seq", bit_index)
        start = 0
        for branch, kept in zip(active, keep_parts):
            count = kept.shape[1]
            held[branch] = kept + received[:, start : start + count]
            start = start + count
    return held


def per_device(
    layer_input,
    doc_ids,
    cotangent,
    attn_norm_gain,
    attn_norm_bias,
    query_weight,
    query_bias,
    key_weight,
    value_weight,
    value_bias,
    output_weight,
    output_bias,
    feed_norm_gain,
    feed_norm_bias,
    up_weight,
    up_bias,
    down_weight,
    down_bias,
):
    sequences, tokens, model_width = layer_input.shape
    head_count = HEADS
    head_size = HEAD_DIM
    score_scale = head_size ** (-0.5)
    device = lax.axis_index("seq")
    axis_count = lax.axis_size("seq")
    branch_strides = (
        FIRST_DILATION,
        SECOND_DILATION,
        THIRD_DILATION,
        FOURTH_DILATION,
        FIFTH_DILATION,
    )
    group_sizes = tuple((min(GROUP * 2**branch, axis_count) for branch in range(5)))
    depth_list = tuple((group_size.bit_length() - 1 for group_size in group_sizes))
    slot_counts = tuple((tokens // stride for stride in branch_strides))
    pickers = tuple(
        (
            jnp.arange(stride)[:, None] == jnp.arange(head_count)[None, :] % stride
            for stride in branch_strides
        )
    )
    docs_all = lax.all_gather(doc_ids, "seq", axis=1, tiled=True)
    segment_docs = []
    for branch in range(5):
        group_size = group_sizes[branch]
        group_start = device // group_size * group_size * tokens
        segment_docs.append(lax.dynamic_slice_in_dim(docs_all, group_start, group_size * tokens, 1))
    masked_grad = jnp.where((doc_ids >= 0)[..., None], cotangent, 0.0)
    h_first = layer_norm(layer_input, attn_norm_gain, attn_norm_bias).astype(jnp.bfloat16)
    query_low = (project(h_first, query_weight) + query_bias).astype(jnp.bfloat16)
    key_low = project(h_first, key_weight).astype(jnp.bfloat16)
    value_low = (project(h_first, value_weight) + value_bias).astype(jnp.bfloat16)
    pairs_low = jnp.stack((key_low, value_low), 2)
    own_sets = [
        pick_pairs(pairs_low, branch_strides[branch], pickers[branch]) for branch in range(5)
    ]
    gathered_sets = group_gather(own_sets, depth_list, device)

    def branch_scores(head_index, branch):
        stride = branch_strides[branch]
        group_size = group_sizes[branch]
        slot_count = slot_counts[branch]
        offset = head_index % stride
        chosen = jnp.arange(stride) == offset
        query_head = lax.dynamic_slice_in_dim(query_low, head_index * head_size, head_size, 2)
        query_sel = lax.dynamic_index_in_dim(
            query_head.reshape(sequences, slot_count, stride, head_size), offset, 2, keepdims=False
        )
        key_sel = lax.dynamic_slice_in_dim(
            gathered_sets[branch][:, :, 0], head_index * head_size, head_size, 2
        )
        value_sel = lax.dynamic_slice_in_dim(
            gathered_sets[branch][:, :, 1], head_index * head_size, head_size, 2
        )
        key_docs = lax.dynamic_index_in_dim(
            segment_docs[branch].reshape(sequences, group_size * slot_count, stride),
            offset,
            2,
            keepdims=False,
        )
        query_docs = lax.dynamic_index_in_dim(
            doc_ids.reshape(sequences, slot_count, stride), offset, 2, keepdims=False
        )
        key_index = jnp.arange(group_size * slot_count, dtype=jnp.int32)
        query_index = device % group_size * slot_count + jnp.arange(slot_count, dtype=jnp.int32)
        mask = (key_index[None, None, :] <= query_index[None, :, None]) & (
            key_docs[:, None, :] == query_docs[:, :, None]
        )
        score = jnp.where(
            mask,
            score_scale
            * jnp.einsum("nqe,nke->nqk", query_sel, key_sel, preferred_element_type=jnp.float32),
            NEG,
        )
        return (chosen, offset, query_sel, key_sel, value_sel, score)

    def head_forward(head_index):
        found = [branch_scores(head_index, branch) for branch in range(5)]
        total = jnp.full((sequences, tokens), NEG, dtype=jnp.float32)
        for branch in range(5):
            chosen, offset, query_sel, key_sel, value_sel, score = found[branch]
            part_total = jax.nn.logsumexp(score, axis=-1)
            spread = jnp.where(chosen, part_total[..., None], NEG).reshape(sequences, tokens)
            total = jnp.logaddexp(total, spread)
        result = jnp.zeros((sequences, tokens, head_size), dtype=jnp.float32)
        for branch in range(5):
            chosen, offset, query_sel, key_sel, value_sel, score = found[branch]
            stride = branch_strides[branch]
            total_sel = lax.dynamic_index_in_dim(
                total.reshape(sequences, slot_counts[branch], stride), offset, 2, keepdims=False
            )
            prob = jnp.exp(score - total_sel[..., None]).astype(jnp.bfloat16)
            part = jnp.einsum("nqk,nke->nqe", prob, value_sel, preferred_element_type=jnp.float32)
            result = result + jnp.where(chosen[:, None], part[:, :, None, :], 0.0).reshape(
                sequences, tokens, head_size
            )
        return (result, total)

    head_outs, totals = lax.map(head_forward, jnp.arange(head_count, dtype=jnp.int32))
    attended = (
        head_outs.transpose(1, 2, 0, 3).reshape(sequences, tokens, model_width).astype(jnp.bfloat16)
    )
    middle = layer_input + project(attended, output_weight) + output_bias
    h_second = layer_norm(middle, feed_norm_gain, feed_norm_bias).astype(jnp.bfloat16)
    hidden = project(h_second, up_weight) + up_bias
    active_full, gelu_pull = jax.vjp(jax.nn.gelu, hidden)
    active = active_full.astype(jnp.bfloat16)
    result_out = middle + project(active, down_weight) + down_bias
    down_grad = masked_grad.astype(jnp.bfloat16)
    grad_down_weight = weight_grad(active, down_grad)
    grad_down_bias = column_sum(down_grad)
    active_grad = jnp.einsum(
        "ntd,fd->ntf", down_grad, down_weight, preferred_element_type=jnp.float32
    )
    hidden_grad = gelu_pull(active_grad)[0].astype(jnp.bfloat16)
    grad_up_weight = weight_grad(h_second, hidden_grad)
    grad_up_bias = column_sum(hidden_grad)
    norm_input_grad = project_back(hidden_grad, up_weight)
    norm_pull = jax.vjp(layer_norm, middle, feed_norm_gain, feed_norm_bias)[1]
    middle_part, grad_feed_norm_gain, grad_feed_norm_bias = norm_pull(norm_input_grad)
    middle_grad = masked_grad + middle_part
    branch_grad = middle_grad.astype(jnp.bfloat16)
    grad_output_weight = weight_grad(attended, branch_grad)
    grad_output_bias = column_sum(branch_grad)
    attended_grad = project_back(branch_grad, output_weight).astype(jnp.bfloat16)

    def head_backward(item):
        head_index, total = item
        found = [branch_scores(head_index, branch) for branch in range(5)]
        out_grad = lax.dynamic_slice_in_dim(attended_grad, head_index * head_size, head_size, 2)
        balance = jnp.zeros((sequences, tokens), dtype=jnp.float32)
        kept = []
        for branch in range(5):
            chosen, offset, query_sel, key_sel, value_sel, score = found[branch]
            stride = branch_strides[branch]
            slot_count = slot_counts[branch]
            total_sel = lax.dynamic_index_in_dim(
                total.reshape(sequences, slot_count, stride), offset, 2, keepdims=False
            )
            grad_sel = lax.dynamic_index_in_dim(
                out_grad.reshape(sequences, slot_count, stride, head_size),
                offset,
                2,
                keepdims=False,
            )
            prob = jnp.exp(score - total_sel[..., None])
            flow = jnp.einsum(
                "nqe,nke->nqk", grad_sel, value_sel, preferred_element_type=jnp.float32
            )
            balance = balance + jnp.where(
                chosen, jnp.sum(prob * flow, axis=-1)[..., None], 0.0
            ).reshape(sequences, tokens)
            kept.append((prob, flow, grad_sel))
        query_part = jnp.zeros((sequences, tokens, head_size), dtype=jnp.float32)
        key_parts = []
        for branch in range(5):
            chosen, offset, query_sel, key_sel, value_sel, score = found[branch]
            prob, flow, grad_sel = kept[branch]
            stride = branch_strides[branch]
            balance_sel = lax.dynamic_index_in_dim(
                balance.reshape(sequences, slot_counts[branch], stride), offset, 2, keepdims=False
            )
            slope = (prob * (flow - balance_sel[..., None])).astype(jnp.bfloat16)
            part = score_scale * jnp.einsum(
                "nqk,nke->nqe", slope, key_sel, preferred_element_type=jnp.float32
            )
            query_part = query_part + jnp.where(chosen[:, None], part[:, :, None, :], 0.0).reshape(
                sequences, tokens, head_size
            )
            key_term = score_scale * jnp.einsum(
                "nqk,nqe->nke", slope, query_sel, preferred_element_type=jnp.float32
            )
            value_term = jnp.einsum(
                "nqk,nqe->nke",
                prob.astype(jnp.bfloat16),
                grad_sel,
                preferred_element_type=jnp.float32,
            )
            key_parts.append(jnp.stack((key_term, value_term), 2))
        return (query_part, balance, tuple(key_parts))

    query_heads, balances, far_parts = lax.map(
        head_backward, (jnp.arange(head_count, dtype=jnp.int32), totals)
    )
    returned_sets = []
    for branch in range(5):
        shaped = far_parts[branch].transpose(1, 2, 3, 0, 4)
        returned_sets.append(shaped.reshape(sequences, shaped.shape[1], 2, model_width))
    owned = group_return(returned_sets, depth_list, device)
    pair_grad = spread_grads(owned[0], branch_strides[0], pickers[0])
    for branch in range(1, 5):
        pair_grad = pair_grad + spread_grads(owned[branch], branch_strides[branch], pickers[branch])
    key_grad = pair_grad[:, :, 0].astype(jnp.bfloat16)
    value_grad = pair_grad[:, :, 1].astype(jnp.bfloat16)
    query_grad = (
        query_heads.transpose(1, 2, 0, 3)
        .reshape(sequences, tokens, model_width)
        .astype(jnp.bfloat16)
    )
    grad_query_weight = weight_grad(h_first, query_grad)
    grad_query_bias = column_sum(query_grad)
    grad_key_weight = weight_grad(h_first, key_grad)
    grad_value_weight = weight_grad(h_first, value_grad)
    grad_value_bias = column_sum(value_grad)
    first_grad = (
        project_back(query_grad, query_weight)
        + project_back(key_grad, key_weight)
        + project_back(value_grad, value_weight)
    )
    first_pull = jax.vjp(layer_norm, layer_input, attn_norm_gain, attn_norm_bias)[1]
    input_part, grad_attn_norm_gain, grad_attn_norm_bias = first_pull(first_grad)
    input_grad = middle_grad + input_part
    summed = (
        lax.psum_scatter(grad_attn_norm_gain, "seq", scatter_dimension=0, tiled=True),
        lax.psum_scatter(grad_attn_norm_bias, "seq", scatter_dimension=0, tiled=True),
        lax.psum_scatter(grad_query_weight, "seq", scatter_dimension=0, tiled=True),
        lax.psum_scatter(grad_query_bias, "seq", scatter_dimension=0, tiled=True),
        lax.psum_scatter(grad_key_weight, "seq", scatter_dimension=0, tiled=True),
        lax.psum_scatter(grad_value_weight, "seq", scatter_dimension=0, tiled=True),
        lax.psum_scatter(grad_value_bias, "seq", scatter_dimension=0, tiled=True),
        lax.psum_scatter(grad_output_weight, "seq", scatter_dimension=0, tiled=True),
        lax.psum_scatter(grad_output_bias, "seq", scatter_dimension=0, tiled=True),
        lax.psum_scatter(grad_feed_norm_gain, "seq", scatter_dimension=0, tiled=True),
        lax.psum_scatter(grad_feed_norm_bias, "seq", scatter_dimension=0, tiled=True),
        lax.psum_scatter(grad_up_weight, "seq", scatter_dimension=0, tiled=True),
        lax.psum_scatter(grad_up_bias, "seq", scatter_dimension=0, tiled=True),
        lax.psum_scatter(grad_down_weight, "seq", scatter_dimension=0, tiled=True),
        lax.psum_scatter(grad_down_bias, "seq", scatter_dimension=0, tiled=True),
    )
    final = (
        lax.psum(summed[0].astype(jnp.bfloat16), "row").astype(jnp.float32),
        lax.psum(summed[1].astype(jnp.bfloat16), "row").astype(jnp.float32),
        lax.psum(summed[2].astype(jnp.bfloat16), "row").astype(jnp.float32),
        lax.psum(summed[3].astype(jnp.bfloat16), "row").astype(jnp.float32),
        lax.psum(summed[4].astype(jnp.bfloat16), "row").astype(jnp.float32),
        lax.psum(summed[5].astype(jnp.bfloat16), "row").astype(jnp.float32),
        lax.psum(summed[6].astype(jnp.bfloat16), "row").astype(jnp.float32),
        lax.psum(summed[7].astype(jnp.bfloat16), "row").astype(jnp.float32),
        lax.psum(summed[8].astype(jnp.bfloat16), "row").astype(jnp.float32),
        lax.psum(summed[9].astype(jnp.bfloat16), "row").astype(jnp.float32),
        lax.psum(summed[10].astype(jnp.bfloat16), "row").astype(jnp.float32),
        lax.psum(summed[11].astype(jnp.bfloat16), "row").astype(jnp.float32),
        lax.psum(summed[12].astype(jnp.bfloat16), "row").astype(jnp.float32),
        lax.psum(summed[13].astype(jnp.bfloat16), "row").astype(jnp.float32),
        lax.psum(summed[14].astype(jnp.bfloat16), "row").astype(jnp.float32),
    )
    return (
        result_out,
        input_grad,
        final[0],
        final[1],
        final[2],
        final[3],
        final[4],
        final[5],
        final[6],
        final[7],
        final[8],
        final[9],
        final[10],
        final[11],
        final[12],
        final[13],
        final[14],
    )


TOK = 384
HALF = TOK // 2
BLOCKS = 8
LEN = TOK * BLOCKS
SEG = LEN // 2
PAR = SEG // 2
TILE = 256
TILES = PAR // TILE
OWN_HEADS = 3
WIDTH = OWN_HEADS * HEAD_DIM
FAR = -1e9
LOG2E = math.log2(math.e)
BOTH = ("row", "seq")
CHEAP = pl.CostEstimate(flops=0, bytes_accessed=0, transcendentals=0)
VMEM_LIMIT = 56 * 1024 * 1024
VMEM_LESS = 32 * 1024 * 1024


def permutation(move):
    pairs = []
    for x in range(2):
        for core in range(2):
            for z in range(4):
                for y in range(2):
                    core_to, z_to, y_to, x_to = move(core, z, y, x)
                    source = (2 * x + core) * 8 + 2 * z + y
                    pairs.append((source, (2 * x_to + core_to) * 8 + 2 * z_to + y_to))
    return pairs


def inverse(pairs):
    return sorted((b, a) for a, b in pairs)


def send(array, pairs):
    return lax.ppermute(array, BOTH, pairs)


def to_row(slot):
    return permutation(lambda core, z, y, x: (z >> 1, 2 * core + (slot ^ (z & 1)), y, x))


SWAP_CORE = permutation(lambda core, z, y, x: (1 - core, z, y, x))
SWAP_X = permutation(lambda core, z, y, x: (core, z, y, 1 - x))
SWAP_Y = permutation(lambda core, z, y, x: (core, z, 1 - y, x))
SWAP_Z_LOW = permutation(lambda core, z, y, x: (core, z ^ 1, y, x))
SWAP_Z_HIGH = permutation(lambda core, z, y, x: (core, z ^ 2, y, x))


def to_owner(delta):
    high, low, side = delta >> 2, delta >> 1 & 1, delta & 1
    return permutation(
        lambda core, z, y, x: (z >> 1, 2 * (core ^ high) + ((z & 1) ^ low), y ^ side, x)
    )


def pick(bit, zero, one):
    return jnp.where(bit == 0, zero, one)


def tied(values):
    return lax.optimization_barrier(values)


def columns(width):
    return [(part, slice(128 * part, 128 * (part + 1))) for part in range(width // 128)]


def read_sorted(in_ref, lanes):
    for part, column in columns(in_ref.shape[-1]):
        lanes[part] = in_ref[0, :, column]
    return [
        jnp.concatenate(
            [
                lanes[part, pl.ds(parity, in_ref.shape[1] // 2, stride=2), :]
                for part, _ in columns(in_ref.shape[-1])
            ],
            -1,
        )
        for parity in range(2)
    ]


def write_unsorted(out_ref, lanes, found):
    for part, column in columns(out_ref.shape[-1]):
        for parity in range(2):
            lanes[part, pl.ds(parity, HALF, stride=2), :] = found[parity][:, column]
        out_ref[0, :, column] = lanes[part]


def lanes_of(width, rows=TOK):
    return [pltpu.VMEM((width // 128, rows, 128), jnp.float32)]


SENT = TOK + 16


def norm_kernel(slot, swap_ref, in_ref, docs_ref, gain_ref, bias_ref, sorted_ref, out_ref, lanes):
    step = pl.program_id(0)
    gain, bias = gain_ref[...].reshape(1, -1), bias_ref[...].reshape(1, -1)
    count = in_ref.shape[1] // 2
    for parity, values in enumerate(read_sorted(in_ref, lanes)):
        rows = pl.ds(pl.multiple_of(parity * HALF + step * count, count), count)
        sorted_ref[rows, :] = values
        out_ref[rows, :] = layer_norm(values, gain, bias).astype(jnp.bfloat16)

    @pl.when(step == 0)
    def _():
        docs = docs_ref[pl.ds(slot ^ swap_ref[0], 1), :]
        lines = [
            jnp.broadcast_to(
                jnp.sum(jnp.where(found, 1.0, 0.0), axis=1, keepdims=True), (8, out_ref.shape[1])
            )
            for found in (docs == 0, docs < 0)
        ]
        out_ref[TOK:SENT, :] = jnp.concatenate(lines, 0).astype(jnp.bfloat16)


def first_norm(slot, swap, inputs, docs, gain, bias):
    width = inputs.shape[-1]
    steps = 2
    vector = pl.BlockSpec((width,), lambda step, swap: (0,))
    return pl.pallas_call(
        functools.partial(norm_kernel, slot),
        grid_spec=pltpu.PrefetchScalarGridSpec(
            num_scalar_prefetch=1,
            grid=(steps,),
            in_specs=[
                pl.BlockSpec(
                    (1, TOK // steps, width), lambda step, swap: (slot ^ swap[0], step, 0)
                ),
                pl.BlockSpec((2, TOK), lambda step, swap: (0, 0)),
                vector,
                vector,
            ],
            out_specs=[
                pl.BlockSpec((TOK, width), lambda step, swap: (0, 0)),
                pl.BlockSpec((SENT, width), lambda step, swap: (0, 0)),
            ],
            scratch_shapes=lanes_of(width, TOK // steps),
        ),
        out_shape=[
            jax.ShapeDtypeStruct((TOK, width), jnp.float32),
            jax.ShapeDtypeStruct((SENT, width), jnp.bfloat16),
        ],
        cost_estimate=CHEAP,
        name="first_norm",
    )(swap, inputs, docs, gain, bias)


def sort_kernel(swap_ref, in_ref, out_ref, lanes):
    for parity, values in enumerate(read_sorted(in_ref, lanes)):
        out_ref[0, pl.ds(parity * HALF, HALF), :] = values


def unsort_kernel(swap_ref, in_ref, out_ref, lanes):
    found = [in_ref[0, pl.ds(parity * HALF, HALF), :] for parity in range(2)]
    write_unsorted(out_ref, lanes, found)


def moved(kernel, swap, array):
    block = (1, TOK, array.shape[-1])
    return pl.pallas_call(
        kernel,
        grid_spec=pltpu.PrefetchScalarGridSpec(
            num_scalar_prefetch=1,
            grid=(2,),
            in_specs=[pl.BlockSpec(block, lambda slot, swap: (slot ^ swap[0], 0, 0))],
            out_specs=pl.BlockSpec(block, lambda slot, swap: (slot, 0, 0)),
            scratch_shapes=lanes_of(block[-1]),
        ),
        out_shape=jax.ShapeDtypeStruct(array.shape, array.dtype),
        name=kernel.__name__,
    )(swap, array)


def norm_back(values, grads, gain):
    center = values - jnp.mean(values, axis=-1, keepdims=True)
    scale = lax.rsqrt(jnp.mean(center * center, axis=-1, keepdims=True) + EPS)
    unit = center * scale
    scaled = grads * gain
    mean_scaled = jnp.mean(scaled, axis=-1, keepdims=True)
    mean_both = jnp.mean(scaled * unit, axis=-1, keepdims=True)
    return scale * (scaled - mean_scaled - unit * mean_both)


def last_kernel(swap_ref, values_ref, first_ref, second_ref, through_ref, gain_ref, out_ref, lanes):
    slot = pl.program_id(0) ^ swap_ref[0]
    found = []
    for parity in range(2):
        rows = pl.ds(parity * HALF, HALF)
        grads = jnp.where(slot == 0, first_ref[rows, :], second_ref[rows, :])
        part = norm_back(
            values_ref[0, rows, :], grads.astype(jnp.float32), gain_ref[...].reshape(1, -1)
        )
        found.append(through_ref[0, rows, :] + part)
    write_unsorted(out_ref, lanes, found)


def last_norm(swap, values, grads, through, gain):
    width = values.shape[-1]
    block = (1, TOK, width)
    own = pl.BlockSpec(block, lambda slot, swap: (slot ^ swap[0], 0, 0))
    whole_slot = pl.BlockSpec((TOK, width), lambda slot, swap: (0, 0))
    return pl.pallas_call(
        last_kernel,
        grid_spec=pltpu.PrefetchScalarGridSpec(
            num_scalar_prefetch=1,
            grid=(2,),
            in_specs=[
                own,
                whole_slot,
                whole_slot,
                own,
                pl.BlockSpec((width,), lambda slot, swap: (0,)),
            ],
            out_specs=pl.BlockSpec(block, lambda slot, swap: (slot, 0, 0)),
            scratch_shapes=lanes_of(width),
        ),
        out_shape=jax.ShapeDtypeStruct(values.shape, jnp.float32),
        cost_estimate=CHEAP,
        name="last_norm",
    )(swap, values, *grads, through, gain)


NT = (((1,), (1,)), ((), ()))
NN = (((1,), (0,)), ((), ()))


def dot(left, right, dims):
    return lax.dot_general(left, right, dims, preferred_element_type=jnp.float32)


def pieces():
    for block in range(BLOCKS):
        for parity in range(2):
            place = block // 4 * SEG + parity * PAR + block % 4 * HALF
            yield block, parity, place


def causal(parts, later):
    keys = lax.broadcasted_iota(jnp.int32, parts.shape, 0)
    queries = lax.broadcasted_iota(jnp.int32, parts.shape, 1)
    return jnp.where(keys <= queries + later, parts, NEG)


def aligned(start):
    return pl.multiple_of(start, TILE)


def groups(index):
    segment, query_parity, key_parity = index >> 2, index >> 1 & 1, index & 1
    query_base = segment * SEG + query_parity * PAR
    key_base = segment * SEG + key_parity * PAR
    later = jnp.where(query_parity < key_parity, -1, 0)
    return query_base, key_base, later


class Tile:
    def __init__(self, segment, parity, tile):
        self.rows = pl.ds(segment * SEG + parity * PAR + tile * TILE, TILE)
        self.parts = []
        for key_parity in range(2):
            start = segment * SEG + key_parity * PAR
            if tile:
                self.parts.append((start, tile * TILE, None))
            later = -1 if parity < key_parity else 0
            self.parts.append((start + tile * TILE, TILE, later))


def near_tiles():
    return [
        Tile(segment, parity, tile)
        for segment in range(2)
        for parity in range(2)
        for tile in range(TILES)
    ]


def in_turn(tiles, first, second):
    held = None
    for tile in tiles:
        found = first(tile)
        if held is not None:
            second(*held)
        held = tile, found
    second(*held)


def marks(head, place, first_doc, padding):
    row = lax.broadcasted_iota(jnp.int32, (16, place.shape[1]), 0)
    turn = lax.rem(place + (FIFTH_DILATION - head), FIFTH_DILATION)

    def members(dilation):
        return lax.rem(turn, dilation) == 0

    found = jnp.where(members(THIRD_DILATION), 2, 3)
    found = jnp.where(members(FOURTH_DILATION), 1, found)
    found = jnp.where(members(FIFTH_DILATION), 0, found)
    kind = jnp.broadcast_to(jnp.where(members(SECOND_DILATION), found, 4), row.shape)
    spot = place.astype(jnp.float32)
    doc = jnp.where(spot < first_doc, 0, jnp.where(spot >= LEN - padding, 2, 1))
    doc = jnp.broadcast_to(doc, row.shape)

    def chosen(condition):
        return jnp.where(condition, 1.0, 0.0)

    same_doc = chosen((row >= 8) & (row < 11) & (doc == row - 8))
    near = same_doc + chosen((row < 8) & (kind == (row & 3)))
    far = same_doc + chosen((row >= 12) & (kind == row - 12))
    other = row & 3
    count = (
        2
        + jnp.where(((other & 1) == 0) & ((kind & 1) == 0), 1, 0)
        + jnp.where((other < 2) & (kind < 2), 1, 0)
        + jnp.where((other == 0) & (kind == 0), 1, 0)
    )
    log3, log5 = math.log2(3), math.log2(5)
    high3, high5 = round(log3 * 64) / 64, round(log5 * 64) / 64

    def by_count(two, three, five):
        return jnp.where(count == 2, two, jnp.where(count == 3, three, five))

    key = jnp.where(
        row < 4,
        by_count(1.0, high3, high5),
        jnp.where(row < 8, by_count(0.0, log3 - high3, log5 - high5), by_count(0.0, 1.0, 2.0)),
    )
    key = jnp.where((kind < 4) & ((row < 8) | (row >= 12)), key, 0.0)
    key = jnp.where((row >= 8) & (row < 11) & (doc != row - 8), FAR, key)
    return near, far, key


def beside(mark):
    count = mark.shape[1]
    mark = jnp.concatenate(
        (jnp.zeros((HEAD_DIM, count)), mark, jnp.zeros((128 - HEAD_DIM - 16, count))), 0
    )
    return mark.T.astype(jnp.bfloat16)


def forward_kernel(info, *refs):
    normed, refs = refs[:BLOCKS], refs[BLOCKS:]
    (
        weight_ref, bias_ref, send_ref, away_ref, result_ref, total_ref, query_ref, far_ref, key_ref, key_t_ref, value_ref, value_t, most, acc, parted,
    ) = refs
    query, far, key, value, key_t = (
        each.at[0] for each in (query_ref, far_ref, key_ref, value_ref, key_t_ref)
    )
    bf16 = jnp.bfloat16
    head = pl.program_id(0)
    place = info[0]
    parity_of_head = (info[1] + head) & 1
    for delta in range(BLOCKS):
        block = place ^ delta
        found = dot(normed[delta][0:TOK, :], weight_ref[...], NT) + bias_ref[...]
        for parity in range(2):
            start = (block >> 2) * SEG + parity * PAR + (block & 3) * HALF
            rows = pl.ds(pl.multiple_of(start, HALF), HALF)
            part = found[parity * HALF : (parity + 1) * HALF]
            query[rows, :] = (part[:, 0:128] * (LOG2E * HEAD_DIM**-0.5)).astype(bf16)
            key[rows, :] = part[:, 128:256].astype(bf16)
            value[rows, :] = part[:, 256:384].astype(bf16)
    counts = sum(each[TOK:SENT, 0:128].astype(jnp.float32) for each in normed)
    first_doc, padding = counts[0:1, 0:1], counts[8:9, 0:1]
    global_head = info[1] + head
    index = lax.broadcasted_iota(jnp.int32, (1, TILE), 1)
    for tile in range(TILES):
        own = query[pl.ds(aligned(SEG + parity_of_head * PAR + tile * TILE), TILE), :]
        spot = SEG + parity_of_head + 2 * (tile * TILE + index)
        mark = marks(global_head, spot, first_doc, padding)[1]
        far[tile * TILE : (tile + 1) * TILE, :] = own + beside(mark)
    for tile in range(LEN // TILE):
        rows = pl.ds(tile * TILE, TILE)
        segment, parity, start = tile * TILE // SEG, tile * TILE // PAR % 2, tile * TILE % PAR
        spot = segment * SEG + parity + 2 * (start + index)
        near, _, key_mark = marks(global_head, spot, first_doc, padding)
        query[rows, :] += beside(near)
        key[rows, :] += beside(key_mark)

    row = lax.broadcasted_iota(jnp.int32, (128, TILE), 0)
    for tile in range(LEN // TILE):
        cols = pl.ds(tile * TILE, TILE)
        turned = value[cols, :].T
        value_t[:, cols] = jnp.where(row == HEAD_DIM, jnp.ones_like(turned), turned)
        key_t[:, cols] = key[cols, :].T[0:HEAD_DIM]

    def scores(tile):
        return [
            (dot(key[pl.ds(start, count), :], query[tile.rows, :], NT), start, count, later)
            for start, count, later in tile.parts
        ]

    def finish(tile, parts):
        parts = [
            (each if later is None else causal(each, later), start, count)
            for each, start, count, later in parts
        ]
        new = functools.reduce(
            jnp.maximum, [jnp.max(each, axis=0, keepdims=True) for each, _, _ in parts]
        )
        total = None
        for each, start, count in parts:
            prob = jnp.exp2(each - new).astype(jnp.bfloat16)
            part = dot(value_t[0:80, pl.ds(start, count)], prob, NN)
            total = part if total is None else total + part
        acc[:, tile.rows] = total
        most[0:1, tile.rows] = new

    in_turn(near_tiles(), scores, finish)

    def far_scores(tile):
        rows = pl.ds(aligned(parity_of_head * PAR), PAR)
        return dot(key[rows, :], far[pl.ds(tile * TILE, TILE), :], NT)

    def far_finish(tile, parts):
        cols = pl.ds(aligned(SEG + parity_of_head * PAR + tile * TILE), TILE)
        old = most[0:1, cols]
        new = jnp.maximum(old, jnp.max(parts, axis=0, keepdims=True))
        prob = jnp.exp2(parts - new).astype(jnp.bfloat16)
        part = dot(value_t[0:80, pl.ds(aligned(parity_of_head * PAR), PAR)], prob, NN)
        acc[:, cols] = acc[:, cols] * jnp.exp2(old - new) + part
        most[0:1, cols] = new

    in_turn(range(TILES), far_scores, far_finish)

    weight = acc[HEAD_DIM : HEAD_DIM + 1, :]
    result = acc[0:HEAD_DIM, :] / weight
    result_ref[0] = result
    total_ref[0] = jnp.broadcast_to(most[0:1, :] + jnp.log2(weight), (8, LEN))
    heads = pl.ds(pl.multiple_of(head * HEAD_DIM, HEAD_DIM), HEAD_DIM)
    for block, parity, start in pieces():
        part = result[:, start : start + HALF].astype(bf16)
        parted[place ^ block, :, parity * HALF : (parity + 1) * HALF] = part
    send_ref[:, heads, :] = parted[0:4]
    away_ref[:, heads, :] = parted[4:8]


def backward_kernel(
    first_head, info, query_ref, far_ref, key_ref, key_t_ref, value_ref, near0, near1, near2,
    near3, away_ref, result_ref, total_ref, out_ref, grad_ref, grad_t, balance, query_grad,
    key_grad, value_grad, turned,
):
    query, far, key, value, key_t = (
        each.at[0] for each in (query_ref, far_ref, key_ref, value_ref, key_t_ref)
    )
    head = first_head + pl.program_id(0)
    place = info[0]
    parity_of_head = (info[1] + head) & 1
    heads = pl.ds(pl.multiple_of(head * HEAD_DIM, HEAD_DIM), HEAD_DIM)
    grad_t[HEAD_DIM:128, :] = jnp.zeros((128 - HEAD_DIM, LEN), jnp.bfloat16)
    for index, near in enumerate((near0, near1, near2, near3)):
        grad_ref[index] = near[0, heads, :]
        grad_ref[4 + index] = away_ref[index, heads, :]
    for block, parity, start in pieces():
        part = grad_ref[place ^ block, :, parity * HALF : (parity + 1) * HALF]
        grad_t[0:HEAD_DIM, start : start + HALF] = part
    balance[...] = jnp.sum(
        grad_t[0:HEAD_DIM, :].astype(jnp.float32) * result_ref[0], axis=0, keepdims=True
    )
    query_grad[HEAD_DIM:128, :] = jnp.zeros((128 - HEAD_DIM, LEN), jnp.float32)
    key_grad[...] = jnp.zeros(key_grad.shape, jnp.float32)
    value_grad[...] = jnp.zeros(value_grad.shape, jnp.float32)

    def products(tile):
        found = []
        for start, count, later in tile.parts:
            rows = pl.ds(start, count)
            found.append(
                (
                    dot(key[rows, :], query[tile.rows, :], NT),
                    dot(value[rows, :], grad_t[:, tile.rows], NN),
                )
            )
        return found

    def spread(rows, queries, grads, scores, flow, total, level):
        prob = jnp.exp2(scores - total)
        slope = (prob * (flow - level)).astype(jnp.bfloat16)
        value_grad[rows, :] += dot(prob.astype(jnp.bfloat16), grads, NT)
        key_grad[rows, :] += dot(slope, queries, NN)
        return dot(key_t[0:HEAD_DIM, rows], slope, NN)

    def finish(tile, found):
        total, level = total_ref[0, 0:1, tile.rows], balance[0:1, tile.rows]
        result = None
        for (start, count, later), (scores, flow) in zip(tile.parts, found):
            if later is not None:
                scores = causal(scores, later)
            part = spread(
                pl.ds(start, count), query[tile.rows, :], grad_t[:, tile.rows], scores, flow,
                total, level,
            )
            result = part if result is None else result + part
        query_grad[0:HEAD_DIM, tile.rows] = result

    in_turn(near_tiles(), products, finish)
    far_rows = pl.ds(aligned(parity_of_head * PAR), PAR)

    def far_columns(tile):
        return pl.ds(aligned(SEG + parity_of_head * PAR + tile * TILE), TILE)

    def far_products(tile):
        return (
            dot(key[far_rows, :], far[pl.ds(tile * TILE, TILE), :], NT),
            dot(value[far_rows, :], grad_t[:, far_columns(tile)], NN),
        )

    def far_finish(tile, found):
        cols = far_columns(tile)
        query_grad[0:HEAD_DIM, cols] += spread(
            far_rows, far[pl.ds(tile * TILE, TILE), :], grad_t[:, cols], *found,
            total_ref[0, 0:1, cols], balance[0:1, cols],
        )

    in_turn(range(TILES), far_products, far_finish)

    for tile in range(LEN // TILE):
        cols = pl.ds(tile * TILE, TILE)
        turned[cols, :] = query_grad[:, cols].T
    first = lax.broadcasted_iota(jnp.int32, (HALF, 128), 1) < HEAD_DIM
    for block, parity, start in pieces():
        rows = pl.ds(parity * HALF, HALF)
        delta = place ^ block
        own = pl.ds(start, HALF)
        pair = jnp.where(
            first,
            turned[own, :] * HEAD_DIM**-0.5,
            pltpu.roll(key_grad[own, :], HEAD_DIM, axis=1) * (1 / LOG2E),
        )
        out_ref[delta, rows, 0:128] = pair.astype(jnp.bfloat16)
        out_ref[delta, rows, 128:256] = jnp.where(first, value_grad[own, :], 0.0).astype(
            jnp.bfloat16
        )


TN = (((0,), (0,)), ((), ()))
HIDDEN_STEP = 768
ROOT = math.sqrt(2 / math.pi)
CUBE = 0.044715


def feed_kernel(
    *refs,
):
    slabs, refs = refs[:4], refs[4:]
    (
        output_ref, ordered0, ordered1, masked_ref, down_ref, output_bias, gain_ref, bias_ref,
        up_bias, up_ref, weight_ref, middle_ref, active_ref, turned_ref, grad_ref, second_t,
        attended_ref, branch_ref, through_ref, sums_ref, hidden_sum,
    ), refs = refs[:21], refs[21:]
    sends, (second, back) = refs[:4], refs[4:]
    step = pl.program_id(0)
    bf16, f32 = jnp.bfloat16, jnp.float32

    @pl.when(step == 0)
    def _():
        back[...] = jnp.zeros(back.shape, f32)
        for slot, ordered in enumerate((ordered0, ordered1)):
            rows = pl.ds(slot * TOK, TOK)
            found = ordered[...] + output_bias[...].reshape(1, -1)
            for side in range(2):
                for high in range(2):
                    index = 2 * side + high
                    slab = slabs[2 * slot + side][high]
                    attended_ref[index, :, slot * TOK : (slot + 1) * TOK] = slab
                    found = found + dot(slab, output_ref[pl.ds(index * WIDTH, WIDTH), :], TN)
            middle_ref[rows, :] = found
            normed = layer_norm(found, gain_ref[...].reshape(1, -1), bias_ref[...].reshape(1, -1))
            second[rows, :] = normed.astype(bf16)
            second_t[:, slot * TOK : (slot + 1) * TOK] = normed.T.astype(bf16)

    sums = jnp.zeros((1, HIDDEN_STEP), f32)
    for part in range(3):
        rows = pl.ds(part * TILE, TILE)
        hidden = dot(second[rows, :], up_ref[...], NN) + up_bias[...]
        active_grad = dot(down_ref[rows, :], weight_ref[...], NT)
        square = hidden * hidden
        bent = jnp.tanh(hidden * (ROOT + ROOT * CUBE * square))
        half = 0.5 + 0.5 * bent
        active = hidden * half
        slope = half + hidden * (half * (1.0 - bent)) * (ROOT + 3 * ROOT * CUBE * square)
        active_ref[rows, :] = active.astype(bf16)
        turned_ref[:, part * TILE : (part + 1) * TILE] = active.T.astype(bf16)
        grad = (slope * active_grad).astype(bf16)
        grad_ref[rows, :] = grad
        sums = sums + jnp.sum(grad.astype(f32), axis=0, keepdims=True)
        back[rows, :] += dot(grad, up_ref[...], NT)
    hidden_sum[...] = jnp.broadcast_to(sums, hidden_sum.shape)

    @pl.when(step == pl.num_programs(0) - 1)
    def _():
        sums_ref[...] = jnp.zeros(sums_ref.shape, f32)
        gain = gain_ref[...].reshape(1, -1)
        for slot in range(2):
            rows = pl.ds(slot * TOK, TOK)
            middle, grads = middle_ref[rows, :], back[rows, :]
            center = middle - jnp.mean(middle, axis=-1, keepdims=True)
            scale = lax.rsqrt(jnp.mean(center * center, axis=-1, keepdims=True) + EPS)
            unit = center * scale
            scaled = grads * gain
            mean_scaled = jnp.mean(scaled, axis=-1, keepdims=True)
            mean_both = jnp.mean(scaled * unit, axis=-1, keepdims=True)
            through = masked_ref[rows, :] + scale * (scaled - mean_scaled - unit * mean_both)
            through_ref[rows, :] = through
            branch = through.astype(bf16)
            branch_ref[rows, :] = branch
            for index, each in enumerate(
                (branch.astype(f32), down_ref[rows, :].astype(f32), grads * unit, grads)
            ):
                sums_ref[index : index + 1, :] += jnp.sum(each, axis=0, keepdims=True)
            for side in range(2):
                for high in range(2):
                    index = 2 * side + high
                    found = dot(output_ref[pl.ds(index * WIDTH, WIDTH), :], branch, NT)
                    sends[2 * slot + side][high] = found.astype(bf16)


def feed(slabs, output_own, ordered, masked, down, output_bias, gain, bias, up_bias, up, weight):
    bf16, f32 = jnp.bfloat16, jnp.float32
    model, hidden = up.shape
    tokens = 2 * TOK

    slab = fixed(2, WIDTH, TOK)
    table = fixed(tokens, model)
    vector = fixed(model)
    wide = along(tokens, HIDDEN_STEP, axis=1)
    tall = along(HIDDEN_STEP, tokens, axis=0)
    out = jax.ShapeDtypeStruct
    return pl.pallas_call(
        feed_kernel,
        grid=(hidden // HIDDEN_STEP,),
        in_specs=[slab] * 4
        + [fixed(model, model), fixed(TOK, model), fixed(TOK, model), table, table]
        + [vector] * 3
        + [along(1, HIDDEN_STEP, axis=1), along(model, HIDDEN_STEP, axis=1)]
        + [along(HIDDEN_STEP, model, axis=0)],
        out_specs=[table, wide, tall, wide, fixed(model, tokens), fixed(4, WIDTH, tokens)]
        + [table, table, fixed(8, model), along(8, HIDDEN_STEP, axis=1)]
        + [slab] * 4,
        out_shape=[
            out((tokens, model), f32),
            out((tokens, hidden), bf16),
            out((hidden, tokens), bf16),
            out((tokens, hidden), bf16),
            out((model, tokens), bf16),
            out((4, WIDTH, tokens), bf16),
            out((tokens, model), bf16),
            out((tokens, model), f32),
            out((8, model), f32),
            out((8, hidden), f32),
        ]
        + [out((2, WIDTH, TOK), bf16)] * 4,
        scratch_shapes=[pltpu.VMEM((tokens, model), bf16), pltpu.VMEM((tokens, model), f32)],
        compiler_params=pltpu.CompilerParams(vmem_limit_bytes=VMEM_LIMIT),
        cost_estimate=CHEAP,
        name="feed",
    )(*slabs, output_own, *ordered, masked, down, output_bias, gain, bias, up_bias, up, weight)


def halved(found, own, keep_ref, away_ref, place):
    zero, one = found[:, 0].astype(jnp.bfloat16), found[:, 1].astype(jnp.bfloat16)
    keep_ref[place] = jnp.where(own == 0, zero, one)
    away_ref[place] = jnp.where(own == 0, one, zero)


def wide_kernel(
    info, attended_ref, branch_ref, turned_ref, down_ref, vector_ref, keep_ref, away_ref
):
    rows = HIDDEN_STEP // 8
    found = dot(turned_ref[...], down_ref[...], NN)
    found = found.reshape(2, 2, 2, rows, found.shape[-1])
    every = slice(None)
    halved(found, info[1], keep_ref, away_ref, (every, every, slice(0, rows)))
    found = dot(attended_ref[0], branch_ref[...], NN).reshape(2, 4, WIDTH // 8, -1)
    found = jnp.concatenate((found, vector_ref[...]), 2)
    found = found.reshape(2, 2, 2, 32, found.shape[-1])
    halved(found, info[1], keep_ref, away_ref, (every, every, slice(rows, rows + 32)))


def tall_kernel(info, second_t, grad_ref, keep_ref, away_ref):
    found = dot(second_t[...], grad_ref[...], NN)
    found = found.reshape(8, 2, -1, found.shape[-1])
    every = slice(None)
    halved(found, info[1], keep_ref, away_ref, (every, 0))


def out_kernel(swap_ref, active_ref, weight_ref, middle_ref, bias_ref, out_ref, acc, lanes):
    step = pl.program_id(0)
    found = dot(active_ref[...], weight_ref[...], NN)

    @pl.when(step == 0)
    def _():
        acc[...] = middle_ref[...] + bias_ref[...].reshape(1, -1) + found

    @pl.when(step > 0)
    def _():
        acc[...] += found

    @pl.when(step == pl.num_programs(0) - 1)
    def _():
        for slot in range(2):
            for part, column in columns(out_ref.shape[-1]):
                for parity in range(2):
                    lanes[part, pl.ds(parity, HALF, stride=2), :] = acc[
                        pl.ds(slot * TOK + parity * HALF, HALF), column
                    ]
                out_ref[slot ^ swap_ref[0], :, column] = lanes[part]


def fixed(*shape):
    return pl.BlockSpec(shape, lambda step, *info: (0,) * len(shape))


def along(*shape, axis):
    return pl.BlockSpec(
        shape, lambda step, *info: tuple(step if i == axis else 0 for i in range(len(shape)))
    )


def stepped(kernel, name, steps, info, operands, in_specs, out_specs, out_shape, scratch=()):
    return pl.pallas_call(
        kernel,
        grid_spec=pltpu.PrefetchScalarGridSpec(
            num_scalar_prefetch=1,
            grid=(steps,),
            in_specs=in_specs,
            out_specs=out_specs,
            scratch_shapes=list(scratch),
        ),
        out_shape=out_shape,
        compiler_params=pltpu.CompilerParams(vmem_limit_bytes=VMEM_LESS),
        cost_estimate=CHEAP,
        name=name,
    )(info, *operands)


def wide_shares(info, attended, branch, turned, down, vectors):
    hidden, tokens = turned.shape
    model = branch.shape[-1]
    return stepped(
        wide_kernel,
        "wide_shares",
        hidden // HIDDEN_STEP,
        info,
        (attended, branch, turned, down, vectors),
        [
            pl.BlockSpec((1, WIDTH, tokens), lambda step, info: (step ^ info[0], 0, 0)),
            fixed(tokens, model),
            along(HIDDEN_STEP, tokens, axis=0),
            fixed(tokens, model),
            along(2, 4, 8, model, axis=0),
        ],
        [along(2, 2, 128, model, axis=0)] * 2,
        [jax.ShapeDtypeStruct((8, 2, 128, model), jnp.bfloat16)] * 2,
    )


def tall_shares(info, second_t, grad):
    tokens, hidden = grad.shape
    model = second_t.shape[0]
    return stepped(
        tall_kernel,
        "tall_shares",
        hidden // HIDDEN_STEP,
        info,
        (second_t, grad),
        [fixed(model, tokens), along(tokens, HIDDEN_STEP, axis=1)],
        [along(8, 1, model // 16, HIDDEN_STEP, axis=1)] * 2,
        [
            jax.ShapeDtypeStruct((8, hidden // HIDDEN_STEP, model // 16, HIDDEN_STEP), jnp.bfloat16)
        ]
        * 2,
    )


def layer_out(swap, active, weight, middle, bias):
    tokens, hidden = active.shape
    model = weight.shape[-1]
    return stepped(
        out_kernel,
        "layer_out",
        hidden // HIDDEN_STEP,
        swap,
        (active, weight, middle, bias),
        [
            along(tokens, HIDDEN_STEP, axis=1),
            along(HIDDEN_STEP, model, axis=0),
            fixed(tokens, model),
            fixed(model),
        ],
        fixed(2, TOK, model),
        jax.ShapeDtypeStruct((2, TOK, model), jnp.float32),
        [pltpu.VMEM((tokens, model), jnp.float32), *lanes_of(model)],
    )


def project_triples(grads, weights):
    grads = jnp.concatenate([each[0] for each in grads], -1)
    return dot(grads, weights[...], NN)


def far_kernel(head0, heads, weights, out_ref):
    out_ref[0] = project_triples((head0, heads), weights).astype(jnp.bfloat16)


def near_kernel(head0, heads, weights, far_ref, keep_ref, away_ref):
    found = project_triples((head0, heads), weights) + far_ref[0].astype(jnp.float32)

    @pl.when(pl.program_id(0) % 2 == 0)
    def _():
        keep_ref[0] = found

    @pl.when(pl.program_id(0) % 2 == 1)
    def _():
        away_ref[0] = found.astype(jnp.bfloat16)


def back_specs(grads, weights, first):
    def block(width):
        return pl.BlockSpec((1, TOK, width), lambda step: (first + step, 0, 0))

    return [block(each.shape[-1]) for each in grads] + [
        pl.BlockSpec(weights.shape, lambda step: (0, 0))
    ]


def far_projection(grads, weights):
    model = weights.shape[-1]
    return pl.pallas_call(
        far_kernel,
        grid=(4,),
        in_specs=back_specs(grads, weights, 4),
        out_specs=pl.BlockSpec((1, TOK, model), lambda step: (step, 0, 0)),
        out_shape=jax.ShapeDtypeStruct((4, TOK, model), jnp.bfloat16),
        compiler_params=pltpu.CompilerParams(vmem_limit_bytes=VMEM_LESS),
        cost_estimate=CHEAP,
        name="far_projection",
    )(*grads, weights)


def near_projection(grads, weights, far):
    model = weights.shape[-1]
    own = pl.BlockSpec((1, TOK, model), lambda step: (step, 0, 0))
    pair = pl.BlockSpec((1, TOK, model), lambda step: (step // 2, 0, 0))
    return pl.pallas_call(
        near_kernel,
        grid=(4,),
        in_specs=[*back_specs(grads, weights, 0), own],
        out_specs=[pair, pair],
        out_shape=[
            jax.ShapeDtypeStruct((2, TOK, model), jnp.float32),
            jax.ShapeDtypeStruct((2, TOK, model), jnp.bfloat16),
        ],
        compiler_params=pltpu.CompilerParams(vmem_limit_bytes=VMEM_LESS),
        cost_estimate=CHEAP,
        name="near_projection",
    )(*grads, weights, far)


LATE_ROWS = 64


def late_kernel(info, *refs):
    normed, (head0, heads, keep_ref, away_ref) = refs[:BLOCKS], refs[BLOCKS:]
    total, acc = 0.0, None
    for delta in range(BLOCKS):
        grads = jnp.concatenate((head0[delta], heads[delta]), -1)
        found = dot(normed[delta][0:TOK, :], grads, TN)
        acc = found if acc is None else acc + found
        total = total + jnp.sum(grads.astype(jnp.float32), axis=0, keepdims=True)
    rows, width = acc.shape
    found = acc.reshape(8, rows // 8, width)
    sums = jnp.broadcast_to(total, (8, 2 * LATE_ROWS - rows // 8, width))
    found = jnp.concatenate((found, sums), 1).reshape(2, 2, 2, 2 * LATE_ROWS, width)
    zero, one = found[:, 0].astype(jnp.bfloat16), found[:, 1].astype(jnp.bfloat16)
    keep_ref[...] = jnp.where(info[0] == 0, zero, one)
    away_ref[...] = jnp.where(info[0] == 0, one, zero)


def late_shares(info, normed, grads):
    model, width = normed[0].shape[-1], sum(each.shape[-1] for each in grads)
    return stepped(
        late_kernel,
        "late_shares",
        1,
        info,
        (*normed, *grads),
        [fixed(*each.shape) for each in (*normed, *grads)],
        [fixed(2, 2, 2 * LATE_ROWS, width)] * 2,
        [jax.ShapeDtypeStruct((2, 2, 2 * LATE_ROWS, width), jnp.bfloat16)] * 2,
    )


def ordered_by(bits, refs):
    found = [ref[...].astype(jnp.float32) for ref in refs]
    for bit in range(2):
        flip = (bits >> bit & 1) == 1
        found = [
            jnp.where(flip, found[i ^ (1 << bit)], found[i]) for i in range(len(found))
        ]
    return found


def early_end_kernel(info, *refs):
    early, (down_ref, output_ref, up_ref, sums_ref) = refs[:4], refs[4:]
    rows = down_ref.shape[0] // 4
    more = output_ref.shape[0] // 4
    model = output_ref.shape[1]
    below = rows + more + 8
    for index, each in enumerate(ordered_by(info[0], early)):
        down_ref[index * rows : (index + 1) * rows, :] = each[0:rows]
        output_ref[index * more : (index + 1) * more, :] = each[rows : rows + more]
        if index == 0:
            sums_ref[...] = each[rows + more : below]
        for part, column in enumerate(range(0, up_ref.shape[1], model)):
            up_ref[index * more : (index + 1) * more, column : column + model] = each[
                below + part * more : below + (part + 1) * more
            ]


def early_end(info, early, hidden):
    model = early[0].shape[-1]
    part = model // 8
    return pl.pallas_call(
        early_end_kernel,
        in_specs=[pl.BlockSpec(memory_space=pltpu.SMEM)]
        + [pl.BlockSpec(memory_space=pltpu.VMEM)] * 4,
        out_specs=[pl.BlockSpec(memory_space=pltpu.VMEM)] * 4,
        out_shape=[
            jax.ShapeDtypeStruct((hidden // 8, model), jnp.float32),
            jax.ShapeDtypeStruct((part, model), jnp.float32),
            jax.ShapeDtypeStruct((part, hidden), jnp.float32),
            jax.ShapeDtypeStruct((8, model), jnp.float32),
        ],
        compiler_params=pltpu.CompilerParams(vmem_limit_bytes=VMEM_LESS),
        cost_estimate=CHEAP,
        name="early_end",
    )(info, *early)


def late_end_kernel(info, *refs):
    pieces_in, refs = refs[:4], refs[4:]
    weights, (gain_ref, bias_ref), refs = refs[:3], refs[3:5], refs[5:]
    outs, (sums_ref, norm_ref) = refs[:3], refs[3:]
    part = outs[0].shape[0]
    pieces_in = ordered_by(info[0], pieces_in)
    groups_in = [
        jnp.concatenate((pieces_in[2 * core][side], pieces_in[2 * core + 1][side]), 0)
        for side in range(2)
        for core in range(2)
    ]
    both = bias_grad = jnp.zeros((8, part), jnp.float32)
    ones = jnp.ones((8, outs[0].shape[1]), jnp.float32)
    for kind, (weight, out) in enumerate(zip(weights, outs)):
        found = jnp.concatenate(
            [
                each[:, 256 * head + HEAD_DIM * kind : 256 * head + HEAD_DIM * (kind + 1)]
                for each in groups_in
                for head in range(OWN_HEADS)
            ],
            1,
        )
        out[...] = found[0:part]
        sums_ref[8 * kind : 8 * kind + 8, :] = found[part : part + 8]
        mine = weight[...].astype(jnp.float32)

        def across(values):
            return lax.dot_general(ones, values, NT, precision=HIGH)

        bias_grad = bias_grad + across(mine * found[part : part + 1])
        both = both + across(mine * found[0:part])
    norm_ref[0:8, :] = (both - bias_ref[0] * bias_grad) / gain_ref[0]
    norm_ref[8:16, :] = bias_grad


def late_end(info, late, weights, gain, bias):
    model = weights[0].shape[0]
    part = model // 8
    own = pl.BlockSpec((part, model), lambda step, info: (info[1], 0))
    vector = pl.BlockSpec((1, 1, part), lambda step, info: (info[1], 0, 0))
    return stepped(
        late_end_kernel,
        "late_end",
        1,
        info,
        (*late, *weights, gain.reshape(8, 1, part), bias.reshape(8, 1, part)),
        [*[fixed(*late[0].shape)] * 4, own, own, own, vector, vector],
        [*[fixed(part, model)] * 3, fixed(24, model), fixed(16, part)],
        [
            *[jax.ShapeDtypeStruct((part, model), jnp.float32)] * 3,
            jax.ShapeDtypeStruct((24, model), jnp.float32),
            jax.ShapeDtypeStruct((16, part), jnp.float32),
        ],
    )


def whole(*shape):
    return pl.BlockSpec(shape, lambda head, info: (0,) * len(shape))


def per_head(*shape, first=0):
    return pl.BlockSpec((1, *shape), lambda head, info: (first + head, *(0,) * len(shape)))


def attention(info, normed, weight, bias):
    bf16, f32 = jnp.bfloat16, jnp.float32
    model = weight.shape[1]

    def out(dtype, *shape):
        return jax.ShapeDtypeStruct(shape, dtype)

    return pl.pallas_call(
        forward_kernel,
        grid_spec=pltpu.PrefetchScalarGridSpec(
            num_scalar_prefetch=1,
            grid=(OWN_HEADS,),
            in_specs=[
                *[whole(SENT, model)] * BLOCKS,
                pl.BlockSpec((384, model), lambda head, info: (head, 0)),
                pl.BlockSpec((1, 384), lambda head, info: (0, head)),
            ],
            out_specs=[
                *[whole(4, WIDTH, TOK)] * 2,
                per_head(HEAD_DIM, LEN),
                per_head(8, LEN),
                per_head(LEN, 128),
                per_head(PAR, 128),
                per_head(LEN, 128),
                per_head(HEAD_DIM, LEN),
                per_head(LEN, 128),
            ],
            scratch_shapes=[
                pltpu.VMEM((128, LEN), bf16),
                pltpu.VMEM((8, LEN), f32),
                pltpu.VMEM((80, LEN), f32),
                pltpu.VMEM((BLOCKS, HEAD_DIM, TOK), bf16),
            ],
        ),
        out_shape=[
            *[out(bf16, 4, WIDTH, TOK)] * 2,
            out(f32, OWN_HEADS, HEAD_DIM, LEN),
            out(f32, OWN_HEADS, 8, LEN),
            out(bf16, OWN_HEADS, LEN, 128),
            out(bf16, OWN_HEADS, PAR, 128),
            out(bf16, OWN_HEADS, LEN, 128),
            out(bf16, OWN_HEADS, HEAD_DIM, LEN),
            out(bf16, OWN_HEADS, LEN, 128),
        ],
        compiler_params=pltpu.CompilerParams(vmem_limit_bytes=VMEM_LIMIT),
        name="attention",
    )(info, *normed, weight, bias)


def attention_back(heads, info, held, grads, result, total):
    first, count = heads
    bf16, f32 = jnp.bfloat16, jnp.float32
    return pl.pallas_call(
        functools.partial(backward_kernel, first),
        grid_spec=pltpu.PrefetchScalarGridSpec(
            num_scalar_prefetch=1,
            grid=(count,),
            in_specs=[
                per_head(LEN, 128, first=first),
                per_head(PAR, 128, first=first),
                per_head(LEN, 128, first=first),
                per_head(HEAD_DIM, LEN, first=first),
                per_head(LEN, 128, first=first),
                *[whole(1, WIDTH, TOK)] * 4,
                whole(4, WIDTH, TOK),
                per_head(HEAD_DIM, LEN, first=first),
                per_head(8, LEN, first=first),
            ],
            out_specs=pl.BlockSpec((BLOCKS, TOK, 256), lambda head, info: (0, 0, head)),
            scratch_shapes=[
                pltpu.VMEM((BLOCKS, HEAD_DIM, TOK), bf16),
                pltpu.VMEM((128, LEN), bf16),
                pltpu.VMEM((1, LEN), f32),
                pltpu.VMEM((128, LEN), f32),
                pltpu.VMEM((LEN, 128), f32),
                pltpu.VMEM((LEN, 128), f32),
                pltpu.VMEM((LEN, 128), f32),
            ],
        ),
        out_shape=jax.ShapeDtypeStruct((BLOCKS, TOK, count * 256), bf16),
        compiler_params=pltpu.CompilerParams(vmem_limit_bytes=VMEM_LESS),
        cost_estimate=CHEAP,
        name="attention_back",
    )(info, *held, *grads, result, total)


def flipped(array, axis, bit):
    zero, one = (lax.index_in_dim(array, i, axis, keepdims=False) for i in range(2))
    return jnp.stack((pick(bit, zero, one), pick(bit, one, zero)), axis)


def entry(array, axis, index):
    return lax.dynamic_index_in_dim(array, index, axis, keepdims=False)


def reduced(array, axis, bit, pairs):
    return plus(entry(array, axis, bit), send(entry(array, axis, 1 - bit), pairs))


def plus(left, right):
    return (left.astype(jnp.float32) + right.astype(jnp.float32)).astype(jnp.bfloat16)


def collected(array, bit, pairs):
    other = send(array, pairs)
    return jnp.stack((pick(bit, array, other), pick(bit, other, array)))


def packed_rows(
    layer_input, doc_ids, cotangent, attn_norm_gain, attn_norm_bias, query_weight, query_bias,
    key_weight, value_weight, value_bias, output_weight, output_bias, feed_norm_gain,
    feed_norm_bias, up_weight, up_bias, down_weight, down_bias,
):
    bf16, f32 = jnp.bfloat16, jnp.float32
    model = layer_input.shape[-1]
    hidden_width = up_weight.shape[-1]
    row, seq = lax.axis_index("row"), lax.axis_index("seq")
    x, core, z, y = row >> 1, row & 1, seq >> 1, seq & 1
    swap = (z & 1)[None].astype(jnp.int32)
    place = 4 * core + 2 * (z & 1) + y
    group = 2 * y + core
    info = jnp.stack((place, OWN_HEADS * group)).astype(jnp.int32)

    ordered, blocks = [], []
    for slot in range(2):
        values, block = first_norm(
            slot, swap, layer_input, doc_ids, attn_norm_gain, attn_norm_bias
        )
        ordered.append(values)
        blocks.append(block)
    first = send(blocks[0], to_row(0))
    docs = doc_ids.reshape(2, HALF, 2).transpose(0, 2, 1).reshape(2, TOK)
    docs = flipped(docs, 0, z & 1)
    masked_grad = jnp.where((docs >= 0)[..., None], moved(sort_kernel, swap, cotangent), 0.0)
    down_grad = masked_grad.astype(bf16)
    first, blocks[1], masked_grad, down_grad = tied((first, blocks[1], masked_grad, down_grad))
    normed = [first, send(first, SWAP_Y)]
    second = send(blocks[1], to_row(1))

    def other_order(array):
        array = array.reshape(2, 2, WIDTH, model)
        return flipped(flipped(array, 0, y), 1, z >> 1).reshape(4 * WIDTH, model)

    def own_columns(weight):
        own = lax.dynamic_slice_in_dim(weight, group * WIDTH, WIDTH, weight.ndim - 1)
        return own.reshape(*weight.shape[:-1], OWN_HEADS, HEAD_DIM)

    query_own, key_own, value_own = map(own_columns, (query_weight, key_weight, value_weight))
    triple_weight = jnp.stack((query_own, key_own, value_own), 2)
    triple_weight = jnp.pad(triple_weight, ((0, 0),) * 3 + ((0, 128 - HEAD_DIM),))
    triple_weight = triple_weight.reshape(model, OWN_HEADS * 384).T
    query_row, value_row = own_columns(query_bias), own_columns(value_bias)
    triple_bias = jnp.stack((query_row, jnp.zeros_like(query_row), value_row), 1)
    triple_bias = jnp.pad(triple_bias, ((0, 0), (0, 0), (0, 128 - HEAD_DIM))).reshape(-1)
    output_own = other_order(output_weight)
    back_weight = jnp.stack((query_own, key_own, value_own, jnp.zeros_like(key_own)), 2)
    back_weight = back_weight.reshape(model, OWN_HEADS * 256).T
    normed, second, output_own, back_weight, triple_weight, triple_bias, ordered_rows = tied(
        (
            normed, second, output_own, back_weight, triple_weight, triple_bias,
            jnp.stack(ordered),
        )
    )
    normed.extend((second, send(second, SWAP_Y)))
    normed.extend([send(block, SWAP_CORE) for block in normed])
    sends, far_sends, result, total, *kept = attention(
        info, normed, triple_weight, triple_bias[None]
    )
    far_sends = send(far_sends, SWAP_CORE)
    slabs = [
        send(jnp.stack((sends[index], far_sends[index])), to_owner(index)) for index in range(4)
    ]
    (
        middle, active, turned, hidden_grad, second_t, attended, branch_grad, middle_grad, sums,
        hidden_sum, *slabs,
    ) = feed(
        slabs, output_own, ordered, masked_grad.reshape(2 * TOK, model),
        down_grad.reshape(2 * TOK, model), output_bias, feed_norm_gain, feed_norm_bias,
        up_bias[None], up_weight, down_weight,
    )
    grads = [send(slabs[index], inverse(to_owner(index))) for index in range(4)]

    vectors = [each.reshape(8, -1) for each in (*sums[:4], hidden_sum[0])]
    vectors = jnp.concatenate(vectors, 1)[:, None, None]
    vectors = jnp.pad(vectors, ((0, 0), (0, 3), (0, 7), (0, 0)))
    share_info = jnp.stack((2 * y + (z >> 1), core)).astype(jnp.int32)
    wide, wide_away = wide_shares(
        share_info, attended, branch_grad, turned, down_grad.reshape(2 * TOK, model), vectors
    )
    wide_away, second_t, hidden_grad, grads[0], grads[1] = tied(
        (wide_away, second_t, hidden_grad, grads[0], grads[1])
    )
    wide_away = send(wide_away, SWAP_CORE)
    tall, tall_away = tall_shares(share_info, second_t, hidden_grad)
    grads, wide, wide_away, tall, tall_away = tied((grads, wide, wide_away, tall, tall_away))
    grads.append(send(jnp.stack([pair[1] for pair in grads]), SWAP_CORE))
    tall_away = send(tall_away, SWAP_CORE)
    wide = plus(wide, wide_away).reshape(2, 2, 2, 2, -1, model)
    grads, wide = tied((grads, wide))
    wide_away = send(entry(wide, 3, 1 - x), SWAP_X)

    def back(heads):
        return attention_back(heads, info, kept, grads, result, total)

    head0 = back((0, 1))
    head0, grads, tall_away = tied((head0, grads, tall_away))
    tall = plus(tall, tall_away).reshape(2, 2, 2, hidden_width // model, 2, -1, model)
    tall, grads = tied((tall, grads))
    tall_away = send(entry(tall, 2, 1 - y), SWAP_Y)
    heads = back((1, 2))
    triple_grads = (head0, heads)
    far_half = far_projection(triple_grads, back_weight)
    far_half, triple_grads, wide_away, tall_away = tied(
        (far_half, triple_grads, wide_away, tall_away)
    )
    far_half = send(far_half, SWAP_CORE)
    late, late_away = late_shares((z & 1)[None].astype(jnp.int32), normed, triple_grads)
    far_half, late, late_away = tied((far_half, late, late_away))
    wide, tall = plus(entry(wide, 3, x), wide_away), plus(entry(tall, 2, y), tall_away)
    wide_away = send(entry(wide, 2, 1 - y), SWAP_Y)
    tall_away = send(entry(tall, 3, 1 - x), SWAP_X)
    late_away = send(late_away, SWAP_Z_LOW)
    near_keep, near_away = near_projection(triple_grads, back_weight, far_half)
    pieces_away = (near_away[0, :96], near_away[0, 96:], near_away[1])
    near_away = [send(each, SWAP_Y) for each in pieces_away]
    near_keep, near_away[0], wide_away, tall_away, late_away, active, middle = tied(
        (near_keep, near_away[0], wide_away, tall_away, late_away, active, middle)
    )
    tall = plus(entry(tall, 3, x), tall_away).reshape(2, 2, -1, model)
    early = jnp.concatenate((plus(entry(wide, 2, y), wide_away), tall), 2)
    late = plus(late, late_away)
    early_away = send(entry(early, 1, 1 - (z & 1)), SWAP_Z_LOW)
    late_away = send(entry(late, 0, 1 - (z >> 1)), SWAP_Z_HIGH)
    near_away, early_away, late_away, active, middle = tied(
        (near_away, early_away, late_away, active, middle)
    )
    early = plus(entry(early, 1, z & 1), early_away)
    early_away = send(entry(early, 0, 1 - (z >> 1)), SWAP_Z_HIGH)
    near_away = (jnp.concatenate(near_away[:2], 0), near_away[2])
    returned = []
    for slot in range(2):
        both = (near_keep[slot] + near_away[slot].astype(f32)).astype(bf16)
        returned.append(send(both, inverse(to_row(slot))))
    late = plus(entry(late, 0, z >> 1), late_away).reshape(2, 2, -1, late.shape[-1])
    late = reduced(late, 1, x, SWAP_X)
    other = send(entry(late, 0, 1 - y), SWAP_Y)
    out = layer_out(swap, active, down_weight, middle, down_bias)
    other, out, early_away = tied((other, out, early_away))
    early = plus(entry(early, 0, z >> 1), early_away)
    early = [early, send(early, SWAP_X)]
    late = entry(late, 0, y)
    late = jnp.stack((pick(y, late, other), pick(y, other, late)))
    late = [late, send(late, SWAP_X)]

    def all_four(pair):
        return [*pair, *(send(each, SWAP_CORE) for each in pair)]

    input_grad = last_norm(
        swap, ordered_rows, returned, middle_grad.reshape(2, TOK, model), attn_norm_gain
    )
    end_info = jnp.stack((2 * core + x, seq)).astype(jnp.int32)
    grad_down, grad_output, grad_up, sums = early_end(
        end_info, all_four(early), hidden_width
    )
    part = model // 8
    output_sum, down_sum, grad_feed_gain, grad_feed_bias, up_sum = jnp.split(
        sums[0], (part, 2 * part, 3 * part, 4 * part)
    )
    grad_query, grad_key, grad_value, sums, norm = late_end(
        end_info,
        all_four(late),
        (query_weight, key_weight, value_weight),
        attn_norm_gain,
        attn_norm_bias,
    )

    def own_part(array):
        return lax.dynamic_slice_in_dim(array, seq * part, part, 0)

    query_sum, value_sum = own_part(sums[0]), own_part(sums[16])
    grad_attn_gain, grad_attn_bias = norm[0], norm[8]
    return (
        out,
        input_grad,
        grad_attn_gain,
        grad_attn_bias,
        grad_query,
        query_sum,
        grad_key,
        grad_value,
        value_sum,
        grad_output,
        output_sum,
        grad_feed_gain,
        grad_feed_bias,
        grad_up,
        up_sum,
        grad_down,
        down_sum,
    )


def solution(mesh):
    placed = (
        P("row", "seq", None),
        P("row", "seq"),
        P("row", "seq", None),
        P(),
        P(),
        P(),
        P(),
        P(),
        P(),
        P(),
        P(),
        P(),
        P(),
        P(),
        P(),
        P(),
        P(),
        P(),
    )
    chosen = packed_rows if dict(mesh.shape) == {"row": 4, "seq": 8} else per_device
    return jax.shard_map(
        chosen,
        mesh=mesh,
        in_specs=placed,
        out_specs=(
            P("row", "seq", None),
            P("row", "seq", None),
            P("seq"),
            P("seq"),
            P("seq", None),
            P("seq"),
            P("seq", None),
            P("seq", None),
            P("seq"),
            P("seq", None),
            P("seq"),
            P("seq"),
            P("seq"),
            P("seq", None),
            P("seq"),
            P("seq", None),
            P("seq"),
        ),
        check_vma=False,
    )
```

```python
import functools
import math

import jax
import jax.numpy as jnp
from jax import lax
from jax.experimental import pallas as pl
from jax.experimental.pallas import tpu as pltpu
from jax.sharding import PartitionSpec as P

HEADS = 12
HEAD_DIM = 64
GROUP = 4
FIRST_DILATION = 1
SECOND_DILATION = 2
THIRD_DILATION = 4
FOURTH_DILATION = 6
FIFTH_DILATION = 12


EPS = 1e-05
NEG = -1e30
HIGH = lax.Precision.HIGHEST


def swapped(array, axis, apart):
    return lax.ppermute(array, axis, [(i, i ^ 1 << apart) for i in range(lax.axis_size(axis))])


def for_sending(array):

    def short(part):
        return part.astype(jnp.bfloat16) if part.dtype == jnp.float32 else part

    return jax.tree.map(short, array)


def layer_norm(values, gain, bias):
    center = values - jnp.mean(values, axis=-1, keepdims=True)
    spread = jnp.mean(center * center, axis=-1, keepdims=True)
    return center * lax.rsqrt(spread + EPS) * gain + bias


def project(inputs, weight):
    return jnp.einsum("ntd,df->ntf", inputs, weight, preferred_element_type=jnp.float32)


def project_back(grads, weight):
    return jnp.einsum("ntf,df->ntd", grads, weight, preferred_element_type=jnp.float32)


def weight_grad(inputs, grads):
    return jnp.einsum("ntd,ntf->df", inputs, grads, preferred_element_type=jnp.float32)


def column_sum(grads):
    return jnp.sum(grads.astype(jnp.float32), axis=(0, 1))


def pick_pairs(values, stride, picker):
    sequences, tokens, kinds, model_width = values.shape
    head_count = picker.shape[1]
    shaped = values.reshape(
        sequences, tokens // stride, stride, kinds, head_count, model_width // head_count
    )
    picked = jnp.einsum(
        "nsrche,rh->nsche", shaped, picker.astype(jnp.bfloat16), preferred_element_type=jnp.float32
    )
    return picked.astype(jnp.bfloat16).reshape(sequences, tokens // stride, kinds, model_width)


def spread_grads(values, stride, picker):
    sequences, slot_count, kinds, model_width = values.shape
    head_count = picker.shape[1]
    shaped = values.reshape(sequences, slot_count, kinds, head_count, model_width // head_count)
    spread = jnp.einsum("nsche,rh->nsrche", shaped, picker.astype(jnp.float32), precision=HIGH)
    return spread.reshape(sequences, slot_count * stride, kinds, model_width)


def group_gather(pieces, depth_list, device):
    gathered = list(pieces)
    for bit_index in range(max(depth_list)):
        active = [branch for branch in range(len(pieces)) if depth_list[branch] > bit_index]
        packed = jnp.concatenate([gathered[branch] for branch in active], 1)
        partner = swapped(packed, "seq", bit_index)
        lower = device // 2**bit_index % 2 == 0
        start = 0
        for branch in active:
            count = gathered[branch].shape[1]
            other = partner[:, start : start + count]
            start = start + count
            gathered[branch] = jnp.where(
                lower,
                jnp.concatenate((gathered[branch], other), 1),
                jnp.concatenate((other, gathered[branch]), 1),
            )
    return gathered


def group_return(pieces, depth_list, device):
    held = list(pieces)
    for bit_index in range(max(depth_list)):
        active = [branch for branch in range(len(pieces)) if depth_list[branch] > bit_index]
        lower = device // 2**bit_index % 2 == 0
        keep_parts = []
        send_parts = []
        for branch in active:
            sequences, count, kinds, model_width = held[branch].shape
            devices_left = 2 ** (depth_list[branch] - bit_index)
            slot_count = count // devices_left
            shaped = held[branch].reshape(
                sequences, devices_left // 2, 2, slot_count, kinds, model_width
            )
            even_part = shaped[:, :, 0].reshape(sequences, count // 2, kinds, model_width)
            odd_part = shaped[:, :, 1].reshape(sequences, count // 2, kinds, model_width)
            keep_parts.append(jnp.where(lower, even_part, odd_part))
            send_parts.append(jnp.where(lower, odd_part, even_part))
        received = swapped(for_sending(jnp.concatenate(send_parts, 1)), "seq", bit_index)
        start = 0
        for branch, kept in zip(active, keep_parts):
            count = kept.shape[1]
            held[branch] = kept + received[:, start : start + count]
            start = start + count
    return held


def per_device(
    layer_input,
    doc_ids,
    cotangent,
    attn_norm_gain,
    attn_norm_bias,
    query_weight,
    query_bias,
    key_weight,
    value_weight,
    value_bias,
    output_weight,
    output_bias,
    feed_norm_gain,
    feed_norm_bias,
    up_weight,
    up_bias,
    down_weight,
    down_bias,
):
    sequences, tokens, model_width = layer_input.shape
    head_count = HEADS
    head_size = HEAD_DIM
    score_scale = head_size ** (-0.5)
    device = lax.axis_index("seq")
    axis_count = lax.axis_size("seq")
    branch_strides = (
        FIRST_DILATION,
        SECOND_DILATION,
        THIRD_DILATION,
        FOURTH_DILATION,
        FIFTH_DILATION,
    )
    group_sizes = tuple((min(GROUP * 2**branch, axis_count) for branch in range(5)))
    depth_list = tuple((group_size.bit_length() - 1 for group_size in group_sizes))
    slot_counts = tuple((tokens // stride for stride in branch_strides))
    pickers = tuple(
        (
            jnp.arange(stride)[:, None] == jnp.arange(head_count)[None, :] % stride
            for stride in branch_strides
        )
    )
    docs_all = lax.all_gather(doc_ids, "seq", axis=1, tiled=True)
    segment_docs = []
    for branch in range(5):
        group_size = group_sizes[branch]
        group_start = device // group_size * group_size * tokens
        segment_docs.append(lax.dynamic_slice_in_dim(docs_all, group_start, group_size * tokens, 1))
    masked_grad = jnp.where((doc_ids >= 0)[..., None], cotangent, 0.0)
    h_first = layer_norm(layer_input, attn_norm_gain, attn_norm_bias).astype(jnp.bfloat16)
    query_low = (project(h_first, query_weight) + query_bias).astype(jnp.bfloat16)
    key_low = project(h_first, key_weight).astype(jnp.bfloat16)
    value_low = (project(h_first, value_weight) + value_bias).astype(jnp.bfloat16)
    pairs_low = jnp.stack((key_low, value_low), 2)
    own_sets = [
        pick_pairs(pairs_low, branch_strides[branch], pickers[branch]) for branch in range(5)
    ]
    gathered_sets = group_gather(own_sets, depth_list, device)

    def branch_scores(head_index, branch):
        stride = branch_strides[branch]
        group_size = group_sizes[branch]
        slot_count = slot_counts[branch]
        offset = head_index % stride
        chosen = jnp.arange(stride) == offset
        query_head = lax.dynamic_slice_in_dim(query_low, head_index * head_size, head_size, 2)
        query_sel = lax.dynamic_index_in_dim(
            query_head.reshape(sequences, slot_count, stride, head_size), offset, 2, keepdims=False
        )
        key_sel = lax.dynamic_slice_in_dim(
            gathered_sets[branch][:, :, 0], head_index * head_size, head_size, 2
        )
        value_sel = lax.dynamic_slice_in_dim(
            gathered_sets[branch][:, :, 1], head_index * head_size, head_size, 2
        )
        key_docs = lax.dynamic_index_in_dim(
            segment_docs[branch].reshape(sequences, group_size * slot_count, stride),
            offset,
            2,
            keepdims=False,
        )
        query_docs = lax.dynamic_index_in_dim(
            doc_ids.reshape(sequences, slot_count, stride), offset, 2, keepdims=False
        )
        key_index = jnp.arange(group_size * slot_count, dtype=jnp.int32)
        query_index = device % group_size * slot_count + jnp.arange(slot_count, dtype=jnp.int32)
        mask = (key_index[None, None, :] <= query_index[None, :, None]) & (
            key_docs[:, None, :] == query_docs[:, :, None]
        )
        score = jnp.where(
            mask,
            score_scale
            * jnp.einsum("nqe,nke->nqk", query_sel, key_sel, preferred_element_type=jnp.float32),
            NEG,
        )
        return (chosen, offset, query_sel, key_sel, value_sel, score)

    def head_forward(head_index):
        found = [branch_scores(head_index, branch) for branch in range(5)]
        total = jnp.full((sequences, tokens), NEG, dtype=jnp.float32)
        for branch in range(5):
            chosen, offset, query_sel, key_sel, value_sel, score = found[branch]
            part_total = jax.nn.logsumexp(score, axis=-1)
            spread = jnp.where(chosen, part_total[..., None], NEG).reshape(sequences, tokens)
            total = jnp.logaddexp(total, spread)
        result = jnp.zeros((sequences, tokens, head_size), dtype=jnp.float32)
        for branch in range(5):
            chosen, offset, query_sel, key_sel, value_sel, score = found[branch]
            stride = branch_strides[branch]
            total_sel = lax.dynamic_index_in_dim(
                total.reshape(sequences, slot_counts[branch], stride), offset, 2, keepdims=False
            )
            prob = jnp.exp(score - total_sel[..., None]).astype(jnp.bfloat16)
            part = jnp.einsum("nqk,nke->nqe", prob, value_sel, preferred_element_type=jnp.float32)
            result = result + jnp.where(chosen[:, None], part[:, :, None, :], 0.0).reshape(
                sequences, tokens, head_size
            )
        return (result, total)

    head_outs, totals = lax.map(head_forward, jnp.arange(head_count, dtype=jnp.int32))
    attended = (
        head_outs.transpose(1, 2, 0, 3).reshape(sequences, tokens, model_width).astype(jnp.bfloat16)
    )
    middle = layer_input + project(attended, output_weight) + output_bias
    h_second = layer_norm(middle, feed_norm_gain, feed_norm_bias).astype(jnp.bfloat16)
    hidden = project(h_second, up_weight) + up_bias
    active_full, gelu_pull = jax.vjp(jax.nn.gelu, hidden)
    active = active_full.astype(jnp.bfloat16)
    result_out = middle + project(active, down_weight) + down_bias
    down_grad = masked_grad.astype(jnp.bfloat16)
    grad_down_weight = weight_grad(active, down_grad)
    grad_down_bias = column_sum(down_grad)
    active_grad = jnp.einsum(
        "ntd,fd->ntf", down_grad, down_weight, preferred_element_type=jnp.float32
    )
    hidden_grad = gelu_pull(active_grad)[0].astype(jnp.bfloat16)
    grad_up_weight = weight_grad(h_second, hidden_grad)
    grad_up_bias = column_sum(hidden_grad)
    norm_input_grad = project_back(hidden_grad, up_weight)
    norm_pull = jax.vjp(layer_norm, middle, feed_norm_gain, feed_norm_bias)[1]
    middle_part, grad_feed_norm_gain, grad_feed_norm_bias = norm_pull(norm_input_grad)
    middle_grad = masked_grad + middle_part
    branch_grad = middle_grad.astype(jnp.bfloat16)
    grad_output_weight = weight_grad(attended, branch_grad)
    grad_output_bias = column_sum(branch_grad)
    attended_grad = project_back(branch_grad, output_weight).astype(jnp.bfloat16)

    def head_backward(item):
        head_index, total = item
        found = [branch_scores(head_index, branch) for branch in range(5)]
        out_grad = lax.dynamic_slice_in_dim(attended_grad, head_index * head_size, head_size, 2)
        balance = jnp.zeros((sequences, tokens), dtype=jnp.float32)
        kept = []
        for branch in range(5):
            chosen, offset, query_sel, key_sel, value_sel, score = found[branch]
            stride = branch_strides[branch]
            slot_count = slot_counts[branch]
            total_sel = lax.dynamic_index_in_dim(
                total.reshape(sequences, slot_count, stride), offset, 2, keepdims=False
            )
            grad_sel = lax.dynamic_index_in_dim(
                out_grad.reshape(sequences, slot_count, stride, head_size),
                offset,
                2,
                keepdims=False,
            )
            prob = jnp.exp(score - total_sel[..., None])
            flow = jnp.einsum(
                "nqe,nke->nqk", grad_sel, value_sel, preferred_element_type=jnp.float32
            )
            balance = balance + jnp.where(
                chosen, jnp.sum(prob * flow, axis=-1)[..., None], 0.0
            ).reshape(sequences, tokens)
            kept.append((prob, flow, grad_sel))
        query_part = jnp.zeros((sequences, tokens, head_size), dtype=jnp.float32)
        key_parts = []
        for branch in range(5):
            chosen, offset, query_sel, key_sel, value_sel, score = found[branch]
            prob, flow, grad_sel = kept[branch]
            stride = branch_strides[branch]
            balance_sel = lax.dynamic_index_in_dim(
                balance.reshape(sequences, slot_counts[branch], stride), offset, 2, keepdims=False
            )
            slope = (prob * (flow - balance_sel[..., None])).astype(jnp.bfloat16)
            part = score_scale * jnp.einsum(
                "nqk,nke->nqe", slope, key_sel, preferred_element_type=jnp.float32
            )
            query_part = query_part + jnp.where(chosen[:, None], part[:, :, None, :], 0.0).reshape(
                sequences, tokens, head_size
            )
            key_term = score_scale * jnp.einsum(
                "nqk,nqe->nke", slope, query_sel, preferred_element_type=jnp.float32
            )
            value_term = jnp.einsum(
                "nqk,nqe->nke",
                prob.astype(jnp.bfloat16),
                grad_sel,
                preferred_element_type=jnp.float32,
            )
            key_parts.append(jnp.stack((key_term, value_term), 2))
        return (query_part, balance, tuple(key_parts))

    query_heads, balances, far_parts = lax.map(
        head_backward, (jnp.arange(head_count, dtype=jnp.int32), totals)
    )
    returned_sets = []
    for branch in range(5):
        shaped = far_parts[branch].transpose(1, 2, 3, 0, 4)
        returned_sets.append(shaped.reshape(sequences, shaped.shape[1], 2, model_width))
    owned = group_return(returned_sets, depth_list, device)
    pair_grad = spread_grads(owned[0], branch_strides[0], pickers[0])
    for branch in range(1, 5):
        pair_grad = pair_grad + spread_grads(owned[branch], branch_strides[branch], pickers[branch])
    key_grad = pair_grad[:, :, 0].astype(jnp.bfloat16)
    value_grad = pair_grad[:, :, 1].astype(jnp.bfloat16)
    query_grad = (
        query_heads.transpose(1, 2, 0, 3)
        .reshape(sequences, tokens, model_width)
        .astype(jnp.bfloat16)
    )
    grad_query_weight = weight_grad(h_first, query_grad)
    grad_query_bias = column_sum(query_grad)
    grad_key_weight = weight_grad(h_first, key_grad)
    grad_value_weight = weight_grad(h_first, value_grad)
    grad_value_bias = column_sum(value_grad)
    first_grad = (
        project_back(query_grad, query_weight)
        + project_back(key_grad, key_weight)
        + project_back(value_grad, value_weight)
    )
    first_pull = jax.vjp(layer_norm, layer_input, attn_norm_gain, attn_norm_bias)[1]
    input_part, grad_attn_norm_gain, grad_attn_norm_bias = first_pull(first_grad)
    input_grad = middle_grad + input_part
    summed = (
        lax.psum_scatter(grad_attn_norm_gain, "seq", scatter_dimension=0, tiled=True),
        lax.psum_scatter(grad_attn_norm_bias, "seq", scatter_dimension=0, tiled=True),
        lax.psum_scatter(grad_query_weight, "seq", scatter_dimension=0, tiled=True),
        lax.psum_scatter(grad_query_bias, "seq", scatter_dimension=0, tiled=True),
        lax.psum_scatter(grad_key_weight, "seq", scatter_dimension=0, tiled=True),
        lax.psum_scatter(grad_value_weight, "seq", scatter_dimension=0, tiled=True),
        lax.psum_scatter(grad_value_bias, "seq", scatter_dimension=0, tiled=True),
        lax.psum_scatter(grad_output_weight, "seq", scatter_dimension=0, tiled=True),
        lax.psum_scatter(grad_output_bias, "seq", scatter_dimension=0, tiled=True),
        lax.psum_scatter(grad_feed_norm_gain, "seq", scatter_dimension=0, tiled=True),
        lax.psum_scatter(grad_feed_norm_bias, "seq", scatter_dimension=0, tiled=True),
        lax.psum_scatter(grad_up_weight, "seq", scatter_dimension=0, tiled=True),
        lax.psum_scatter(grad_up_bias, "seq", scatter_dimension=0, tiled=True),
        lax.psum_scatter(grad_down_weight, "seq", scatter_dimension=0, tiled=True),
        lax.psum_scatter(grad_down_bias, "seq", scatter_dimension=0, tiled=True),
    )
    final = (
        lax.psum(summed[0].astype(jnp.bfloat16), "row").astype(jnp.float32),
        lax.psum(summed[1].astype(jnp.bfloat16), "row").astype(jnp.float32),
        lax.psum(summed[2].astype(jnp.bfloat16), "row").astype(jnp.float32),
        lax.psum(summed[3].astype(jnp.bfloat16), "row").astype(jnp.float32),
        lax.psum(summed[4].astype(jnp.bfloat16), "row").astype(jnp.float32),
        lax.psum(summed[5].astype(jnp.bfloat16), "row").astype(jnp.float32),
        lax.psum(summed[6].astype(jnp.bfloat16), "row").astype(jnp.float32),
        lax.psum(summed[7].astype(jnp.bfloat16), "row").astype(jnp.float32),
        lax.psum(summed[8].astype(jnp.bfloat16), "row").astype(jnp.float32),
        lax.psum(summed[9].astype(jnp.bfloat16), "row").astype(jnp.float32),
        lax.psum(summed[10].astype(jnp.bfloat16), "row").astype(jnp.float32),
        lax.psum(summed[11].astype(jnp.bfloat16), "row").astype(jnp.float32),
        lax.psum(summed[12].astype(jnp.bfloat16), "row").astype(jnp.float32),
        lax.psum(summed[13].astype(jnp.bfloat16), "row").astype(jnp.float32),
        lax.psum(summed[14].astype(jnp.bfloat16), "row").astype(jnp.float32),
    )
    return (
        result_out,
        input_grad,
        final[0],
        final[1],
        final[2],
        final[3],
        final[4],
        final[5],
        final[6],
        final[7],
        final[8],
        final[9],
        final[10],
        final[11],
        final[12],
        final[13],
        final[14],
    )


TOK = 384
HALF = TOK // 2
BLOCKS = 8
LEN = TOK * BLOCKS
SEG = LEN // 2
PAR = SEG // 2
TILE = 256
TILES = PAR // TILE
OWN_HEADS = 3
WIDTH = OWN_HEADS * HEAD_DIM
FAR = -1e9
LOG2E = math.log2(math.e)
BOTH = ("row", "seq")
CHEAP = pl.CostEstimate(flops=0, bytes_accessed=0, transcendentals=0)
VMEM_LIMIT = 56 * 1024 * 1024
VMEM_LESS = 32 * 1024 * 1024


def permutation(move):
    pairs = []
    for x in range(2):
        for core in range(2):
            for z in range(4):
                for y in range(2):
                    core_to, z_to, y_to, x_to = move(core, z, y, x)
                    source = (2 * x + core) * 8 + 2 * z + y
                    pairs.append((source, (2 * x_to + core_to) * 8 + 2 * z_to + y_to))
    return pairs


def inverse(pairs):
    return sorted((b, a) for a, b in pairs)


def send(array, pairs):
    return lax.ppermute(array, BOTH, pairs)


def to_row(slot):
    return permutation(lambda core, z, y, x: (z >> 1, 2 * core + (slot ^ (z & 1)), y, x))


SWAP_CORE = permutation(lambda core, z, y, x: (1 - core, z, y, x))
SWAP_X = permutation(lambda core, z, y, x: (core, z, y, 1 - x))
SWAP_Y = permutation(lambda core, z, y, x: (core, z, 1 - y, x))
SWAP_Z_LOW = permutation(lambda core, z, y, x: (core, z ^ 1, y, x))
SWAP_Z_HIGH = permutation(lambda core, z, y, x: (core, z ^ 2, y, x))


def to_owner(delta):
    high, low, side = delta >> 2, delta >> 1 & 1, delta & 1
    return permutation(
        lambda core, z, y, x: (z >> 1, 2 * (core ^ high) + ((z & 1) ^ low), y ^ side, x)
    )


def pick(bit, zero, one):
    return jnp.where(bit == 0, zero, one)


def tied(values):
    return lax.optimization_barrier(values)


def columns(width):
    return [(part, slice(128 * part, 128 * (part + 1))) for part in range(width // 128)]


def read_sorted(in_ref, lanes):
    for part, column in columns(in_ref.shape[-1]):
        lanes[part] = in_ref[0, :, column]
    return [
        jnp.concatenate(
            [
                lanes[part, pl.ds(parity, in_ref.shape[1] // 2, stride=2), :]
                for part, _ in columns(in_ref.shape[-1])
            ],
            -1,
        )
        for parity in range(2)
    ]


def write_unsorted(out_ref, lanes, found):
    for part, column in columns(out_ref.shape[-1]):
        for parity in range(2):
            lanes[part, pl.ds(parity, HALF, stride=2), :] = found[parity][:, column]
        out_ref[0, :, column] = lanes[part]


def lanes_of(width, rows=TOK):
    return [pltpu.VMEM((width // 128, rows, 128), jnp.float32)]


SENT = TOK + 16


def norm_kernel(slot, swap_ref, in_ref, docs_ref, gain_ref, bias_ref, sorted_ref, out_ref, lanes):
    step = pl.program_id(0)
    gain, bias = gain_ref[...].reshape(1, -1), bias_ref[...].reshape(1, -1)
    count = in_ref.shape[1] // 2
    for parity, values in enumerate(read_sorted(in_ref, lanes)):
        rows = pl.ds(pl.multiple_of(parity * HALF + step * count, count), count)
        sorted_ref[rows, :] = values
        out_ref[rows, :] = layer_norm(values, gain, bias).astype(jnp.bfloat16)

    @pl.when(step == 0)
    def _():
        docs = docs_ref[pl.ds(slot ^ swap_ref[0], 1), :]
        lines = [
            jnp.broadcast_to(
                jnp.sum(jnp.where(found, 1.0, 0.0), axis=1, keepdims=True), (8, out_ref.shape[1])
            )
            for found in (docs == 0, docs < 0)
        ]
        out_ref[TOK:SENT, :] = jnp.concatenate(lines, 0).astype(jnp.bfloat16)


def first_norm(slot, swap, inputs, docs, gain, bias):
    width = inputs.shape[-1]
    steps = 2
    vector = pl.BlockSpec((width,), lambda step, swap: (0,))
    return pl.pallas_call(
        functools.partial(norm_kernel, slot),
        grid_spec=pltpu.PrefetchScalarGridSpec(
            num_scalar_prefetch=1,
            grid=(steps,),
            in_specs=[
                pl.BlockSpec(
                    (1, TOK // steps, width), lambda step, swap: (slot ^ swap[0], step, 0)
                ),
                pl.BlockSpec((2, TOK), lambda step, swap: (0, 0)),
                vector,
                vector,
            ],
            out_specs=[
                pl.BlockSpec((TOK, width), lambda step, swap: (0, 0)),
                pl.BlockSpec((SENT, width), lambda step, swap: (0, 0)),
            ],
            scratch_shapes=lanes_of(width, TOK // steps),
        ),
        out_shape=[
            jax.ShapeDtypeStruct((TOK, width), jnp.float32),
            jax.ShapeDtypeStruct((SENT, width), jnp.bfloat16),
        ],
        cost_estimate=CHEAP,
        name="first_norm",
    )(swap, inputs, docs, gain, bias)


def sort_kernel(swap_ref, in_ref, out_ref, lanes):
    for parity, values in enumerate(read_sorted(in_ref, lanes)):
        out_ref[0, pl.ds(parity * HALF, HALF), :] = values


def unsort_kernel(swap_ref, in_ref, out_ref, lanes):
    found = [in_ref[0, pl.ds(parity * HALF, HALF), :] for parity in range(2)]
    write_unsorted(out_ref, lanes, found)


def moved(kernel, swap, array):
    block = (1, TOK, array.shape[-1])
    return pl.pallas_call(
        kernel,
        grid_spec=pltpu.PrefetchScalarGridSpec(
            num_scalar_prefetch=1,
            grid=(2,),
            in_specs=[pl.BlockSpec(block, lambda slot, swap: (slot ^ swap[0], 0, 0))],
            out_specs=pl.BlockSpec(block, lambda slot, swap: (slot, 0, 0)),
            scratch_shapes=lanes_of(block[-1]),
        ),
        out_shape=jax.ShapeDtypeStruct(array.shape, array.dtype),
        name=kernel.__name__,
    )(swap, array)


def norm_back(values, grads, gain):
    center = values - jnp.mean(values, axis=-1, keepdims=True)
    scale = lax.rsqrt(jnp.mean(center * center, axis=-1, keepdims=True) + EPS)
    unit = center * scale
    scaled = grads * gain
    mean_scaled = jnp.mean(scaled, axis=-1, keepdims=True)
    mean_both = jnp.mean(scaled * unit, axis=-1, keepdims=True)
    return scale * (scaled - mean_scaled - unit * mean_both)


def last_kernel(swap_ref, values_ref, first_ref, second_ref, through_ref, gain_ref, out_ref, lanes):
    slot = pl.program_id(0) ^ swap_ref[0]
    found = []
    for parity in range(2):
        rows = pl.ds(parity * HALF, HALF)
        grads = jnp.where(slot == 0, first_ref[rows, :], second_ref[rows, :])
        part = norm_back(
            values_ref[0, rows, :], grads.astype(jnp.float32), gain_ref[...].reshape(1, -1)
        )
        found.append(through_ref[0, rows, :] + part)
    write_unsorted(out_ref, lanes, found)


def last_norm(swap, values, grads, through, gain):
    width = values.shape[-1]
    block = (1, TOK, width)
    own = pl.BlockSpec(block, lambda slot, swap: (slot ^ swap[0], 0, 0))
    whole_slot = pl.BlockSpec((TOK, width), lambda slot, swap: (0, 0))
    return pl.pallas_call(
        last_kernel,
        grid_spec=pltpu.PrefetchScalarGridSpec(
            num_scalar_prefetch=1,
            grid=(2,),
            in_specs=[
                own,
                whole_slot,
                whole_slot,
                own,
                pl.BlockSpec((width,), lambda slot, swap: (0,)),
            ],
            out_specs=pl.BlockSpec(block, lambda slot, swap: (slot, 0, 0)),
            scratch_shapes=lanes_of(width),
        ),
        out_shape=jax.ShapeDtypeStruct(values.shape, jnp.float32),
        cost_estimate=CHEAP,
        name="last_norm",
    )(swap, values, *grads, through, gain)


NT = (((1,), (1,)), ((), ()))
NN = (((1,), (0,)), ((), ()))


def dot(left, right, dims):
    return lax.dot_general(left, right, dims, preferred_element_type=jnp.float32)


def pieces():
    for block in range(BLOCKS):
        for parity in range(2):
            place = block // 4 * SEG + parity * PAR + block % 4 * HALF
            yield block, parity, place


def causal(parts, later):
    keys = lax.broadcasted_iota(jnp.int32, parts.shape, 0)
    queries = lax.broadcasted_iota(jnp.int32, parts.shape, 1)
    return jnp.where(keys <= queries + later, parts, NEG)


def aligned(start):
    return pl.multiple_of(start, TILE)


def groups(index):
    segment, query_parity, key_parity = index >> 2, index >> 1 & 1, index & 1
    query_base = segment * SEG + query_parity * PAR
    key_base = segment * SEG + key_parity * PAR
    later = jnp.where(query_parity < key_parity, -1, 0)
    return query_base, key_base, later


class Tile:
    def __init__(self, segment, parity, tile):
        self.rows = pl.ds(segment * SEG + parity * PAR + tile * TILE, TILE)
        self.parts = []
        for key_parity in range(2):
            start = segment * SEG + key_parity * PAR
            if tile:
                self.parts.append((start, tile * TILE, None))
            later = -1 if parity < key_parity else 0
            self.parts.append((start + tile * TILE, TILE, later))


def near_tiles():
    return [
        Tile(segment, parity, tile)
        for segment in range(2)
        for parity in range(2)
        for tile in range(TILES)
    ]


def in_turn(tiles, first, second):
    held = None
    for tile in tiles:
        found = first(tile)
        if held is not None:
            second(*held)
        held = tile, found
    second(*held)


def marks(head, place, first_doc, padding):
    row = lax.broadcasted_iota(jnp.int32, (16, place.shape[1]), 0)
    turn = lax.rem(place + (FIFTH_DILATION - head), FIFTH_DILATION)

    def members(dilation):
        return lax.rem(turn, dilation) == 0

    found = jnp.where(members(THIRD_DILATION), 2, 3)
    found = jnp.where(members(FOURTH_DILATION), 1, found)
    found = jnp.where(members(FIFTH_DILATION), 0, found)
    kind = jnp.broadcast_to(jnp.where(members(SECOND_DILATION), found, 4), row.shape)
    spot = place.astype(jnp.float32)
    doc = jnp.where(spot < first_doc, 0, jnp.where(spot >= LEN - padding, 2, 1))
    doc = jnp.broadcast_to(doc, row.shape)

    def chosen(condition):
        return jnp.where(condition, 1.0, 0.0)

    same_doc = chosen((row >= 8) & (row < 11) & (doc == row - 8))
    near = same_doc + chosen((row < 8) & (kind == (row & 3)))
    far = same_doc + chosen((row >= 12) & (kind == row - 12))
    other = row & 3
    count = (
        2
        + jnp.where(((other & 1) == 0) & ((kind & 1) == 0), 1, 0)
        + jnp.where((other < 2) & (kind < 2), 1, 0)
        + jnp.where((other == 0) & (kind == 0), 1, 0)
    )
    log3, log5 = math.log2(3), math.log2(5)
    high3, high5 = round(log3 * 64) / 64, round(log5 * 64) / 64

    def by_count(two, three, five):
        return jnp.where(count == 2, two, jnp.where(count == 3, three, five))

    key = jnp.where(
        row < 4,
        by_count(1.0, high3, high5),
        jnp.where(row < 8, by_count(0.0, log3 - high3, log5 - high5), by_count(0.0, 1.0, 2.0)),
    )
    key = jnp.where((kind < 4) & ((row < 8) | (row >= 12)), key, 0.0)
    key = jnp.where((row >= 8) & (row < 11) & (doc != row - 8), FAR, key)
    return near, far, key


def beside(mark):
    count = mark.shape[1]
    mark = jnp.concatenate(
        (jnp.zeros((HEAD_DIM, count)), mark, jnp.zeros((128 - HEAD_DIM - 16, count))), 0
    )
    return mark.T.astype(jnp.bfloat16)


def forward_kernel(info, *refs):
    normed, refs = refs[:BLOCKS], refs[BLOCKS:]
    (
        weight_ref, bias_ref, send_ref, away_ref, result_ref, total_ref, query_ref, far_ref, key_ref, key_t_ref, value_ref, value_t, most, acc, parted,
    ) = refs
    query, far, key, value, key_t = (
        each.at[0] for each in (query_ref, far_ref, key_ref, value_ref, key_t_ref)
    )
    bf16 = jnp.bfloat16
    head = pl.program_id(0)
    place = info[0]
    parity_of_head = (info[1] + head) & 1
    for delta in range(BLOCKS):
        block = place ^ delta
        found = dot(normed[delta][0:TOK, :], weight_ref[...], NT) + bias_ref[...]
        for parity in range(2):
            start = (block >> 2) * SEG + parity * PAR + (block & 3) * HALF
            rows = pl.ds(pl.multiple_of(start, HALF), HALF)
            part = found[parity * HALF : (parity + 1) * HALF]
            query[rows, :] = (part[:, 0:128] * (LOG2E * HEAD_DIM**-0.5)).astype(bf16)
            key[rows, :] = part[:, 128:256].astype(bf16)
            value[rows, :] = part[:, 256:384].astype(bf16)
    counts = sum(each[TOK:SENT, 0:128].astype(jnp.float32) for each in normed)
    first_doc, padding = counts[0:1, 0:1], counts[8:9, 0:1]
    global_head = info[1] + head
    index = lax.broadcasted_iota(jnp.int32, (1, TILE), 1)
    for tile in range(TILES):
        own = query[pl.ds(aligned(SEG + parity_of_head * PAR + tile * TILE), TILE), :]
        spot = SEG + parity_of_head + 2 * (tile * TILE + index)
        mark = marks(global_head, spot, first_doc, padding)[1]
        far[tile * TILE : (tile + 1) * TILE, :] = own + beside(mark)
    for tile in range(LEN // TILE):
        rows = pl.ds(tile * TILE, TILE)
        segment, parity, start = tile * TILE // SEG, tile * TILE // PAR % 2, tile * TILE % PAR
        spot = segment * SEG + parity + 2 * (start + index)
        near, _, key_mark = marks(global_head, spot, first_doc, padding)
        query[rows, :] += beside(near)
        key[rows, :] += beside(key_mark)

    row = lax.broadcasted_iota(jnp.int32, (128, TILE), 0)
    for tile in range(LEN // TILE):
        cols = pl.ds(tile * TILE, TILE)
        turned = value[cols, :].T
        value_t[:, cols] = jnp.where(row == HEAD_DIM, jnp.ones_like(turned), turned)
        key_t[:, cols] = key[cols, :].T[0:HEAD_DIM]

    def scores(tile):
        return [
            (dot(key[pl.ds(start, count), :], query[tile.rows, :], NT), start, count, later)
            for start, count, later in tile.parts
        ]

    def finish(tile, parts):
        parts = [
            (each if later is None else causal(each, later), start, count)
            for each, start, count, later in parts
        ]
        new = functools.reduce(
            jnp.maximum, [jnp.max(each, axis=0, keepdims=True) for each, _, _ in parts]
        )
        total = None
        for each, start, count in parts:
            prob = jnp.exp2(each - new).astype(jnp.bfloat16)
            part = dot(value_t[0:80, pl.ds(start, count)], prob, NN)
            total = part if total is None else total + part
        acc[:, tile.rows] = total
        most[0:1, tile.rows] = new

    in_turn(near_tiles(), scores, finish)

    def far_scores(tile):
        rows = pl.ds(aligned(parity_of_head * PAR), PAR)
        return dot(key[rows, :], far[pl.ds(tile * TILE, TILE), :], NT)

    def far_finish(tile, parts):
        cols = pl.ds(aligned(SEG + parity_of_head * PAR + tile * TILE), TILE)
        old = most[0:1, cols]
        new = jnp.maximum(old, jnp.max(parts, axis=0, keepdims=True))
        prob = jnp.exp2(parts - new).astype(jnp.bfloat16)
        part = dot(value_t[0:80, pl.ds(aligned(parity_of_head * PAR), PAR)], prob, NN)
        acc[:, cols] = acc[:, cols] * jnp.exp2(old - new) + part
        most[0:1, cols] = new

    in_turn(range(TILES), far_scores, far_finish)

    weight = acc[HEAD_DIM : HEAD_DIM + 1, :]
    result = acc[0:HEAD_DIM, :] / weight
    result_ref[0] = result
    total_ref[0] = jnp.broadcast_to(most[0:1, :] + jnp.log2(weight), (8, LEN))
    heads = pl.ds(pl.multiple_of(head * HEAD_DIM, HEAD_DIM), HEAD_DIM)
    for block, parity, start in pieces():
        part = result[:, start : start + HALF].astype(bf16)
        parted[place ^ block, :, parity * HALF : (parity + 1) * HALF] = part
    send_ref[:, heads, :] = parted[0:4]
    away_ref[:, heads, :] = parted[4:8]


def backward_kernel(
    first_head, info, query_ref, far_ref, key_ref, key_t_ref, value_ref, near0, near1, near2,
    near3, away_ref, result_ref, total_ref, out_ref, grad_ref, grad_t, balance, query_grad,
    key_grad, value_grad, turned,
):
    query, far, key, value, key_t = (
        each.at[0] for each in (query_ref, far_ref, key_ref, value_ref, key_t_ref)
    )
    head = first_head + pl.program_id(0)
    place = info[0]
    parity_of_head = (info[1] + head) & 1
    heads = pl.ds(pl.multiple_of(head * HEAD_DIM, HEAD_DIM), HEAD_DIM)
    grad_t[HEAD_DIM:128, :] = jnp.zeros((128 - HEAD_DIM, LEN), jnp.bfloat16)
    for index, near in enumerate((near0, near1, near2, near3)):
        grad_ref[index] = near[0, heads, :]
        grad_ref[4 + index] = away_ref[index, heads, :]
    for block, parity, start in pieces():
        part = grad_ref[place ^ block, :, parity * HALF : (parity + 1) * HALF]
        grad_t[0:HEAD_DIM, start : start + HALF] = part
    balance[...] = jnp.sum(
        grad_t[0:HEAD_DIM, :].astype(jnp.float32) * result_ref[0], axis=0, keepdims=True
    )
    query_grad[HEAD_DIM:128, :] = jnp.zeros((128 - HEAD_DIM, LEN), jnp.float32)
    key_grad[...] = jnp.zeros(key_grad.shape, jnp.float32)
    value_grad[...] = jnp.zeros(value_grad.shape, jnp.float32)

    def products(tile):
        found = []
        for start, count, later in tile.parts:
            rows = pl.ds(start, count)
            found.append(
                (
                    dot(key[rows, :], query[tile.rows, :], NT),
                    dot(value[rows, :], grad_t[:, tile.rows], NN),
                )
            )
        return found

    def spread(rows, queries, grads, scores, flow, total, level):
        prob = jnp.exp2(scores - total)
        slope = (prob * (flow - level)).astype(jnp.bfloat16)
        value_grad[rows, :] += dot(prob.astype(jnp.bfloat16), grads, NT)
        key_grad[rows, :] += dot(slope, queries, NN)
        return dot(key_t[0:HEAD_DIM, rows], slope, NN)

    def finish(tile, found):
        total, level = total_ref[0, 0:1, tile.rows], balance[0:1, tile.rows]
        result = None
        for (start, count, later), (scores, flow) in zip(tile.parts, found):
            if later is not None:
                scores = causal(scores, later)
            part = spread(
                pl.ds(start, count), query[tile.rows, :], grad_t[:, tile.rows], scores, flow,
                total, level,
            )
            result = part if result is None else result + part
        query_grad[0:HEAD_DIM, tile.rows] = result

    in_turn(near_tiles(), products, finish)
    far_rows = pl.ds(aligned(parity_of_head * PAR), PAR)

    def far_columns(tile):
        return pl.ds(aligned(SEG + parity_of_head * PAR + tile * TILE), TILE)

    def far_products(tile):
        return (
            dot(key[far_rows, :], far[pl.ds(tile * TILE, TILE), :], NT),
            dot(value[far_rows, :], grad_t[:, far_columns(tile)], NN),
        )

    def far_finish(tile, found):
        cols = far_columns(tile)
        query_grad[0:HEAD_DIM, cols] += spread(
            far_rows, far[pl.ds(tile * TILE, TILE), :], grad_t[:, cols], *found,
            total_ref[0, 0:1, cols], balance[0:1, cols],
        )

    in_turn(range(TILES), far_products, far_finish)

    for tile in range(LEN // TILE):
        cols = pl.ds(tile * TILE, TILE)
        turned[cols, :] = query_grad[:, cols].T
    first = lax.broadcasted_iota(jnp.int32, (HALF, 128), 1) < HEAD_DIM
    for block, parity, start in pieces():
        rows = pl.ds(parity * HALF, HALF)
        delta = place ^ block
        own = pl.ds(start, HALF)
        pair = jnp.where(
            first,
            turned[own, :] * HEAD_DIM**-0.5,
            pltpu.roll(key_grad[own, :], HEAD_DIM, axis=1) * (1 / LOG2E),
        )
        out_ref[delta, rows, 0:128] = pair.astype(jnp.bfloat16)
        out_ref[delta, rows, 128:256] = jnp.where(first, value_grad[own, :], 0.0).astype(
            jnp.bfloat16
        )


TN = (((0,), (0,)), ((), ()))
HIDDEN_STEP = 768
ROOT = math.sqrt(2 / math.pi)
CUBE = 0.044715


def feed_kernel(
    *refs,
):
    slabs, refs = refs[:4], refs[4:]
    (
        output_ref, ordered0, ordered1, masked_ref, down_ref, output_bias, gain_ref, bias_ref,
        up_bias, up_ref, weight_ref, middle_ref, active_ref, turned_ref, grad_ref, second_t,
        attended_ref, branch_ref, through_ref, sums_ref, hidden_sum,
    ), refs = refs[:21], refs[21:]
    sends, (second, back) = refs[:4], refs[4:]
    step = pl.program_id(0)
    bf16, f32 = jnp.bfloat16, jnp.float32

    @pl.when(step == 0)
    def _():
        back[...] = jnp.zeros(back.shape, f32)
        for slot, ordered in enumerate((ordered0, ordered1)):
            rows = pl.ds(slot * TOK, TOK)
            found = ordered[...] + output_bias[...].reshape(1, -1)
            for side in range(2):
                for high in range(2):
                    index = 2 * side + high
                    slab = slabs[2 * slot + side][high]
                    attended_ref[index, :, slot * TOK : (slot + 1) * TOK] = slab
                    found = found + dot(slab, output_ref[pl.ds(index * WIDTH, WIDTH), :], TN)
            middle_ref[rows, :] = found
            normed = layer_norm(found, gain_ref[...].reshape(1, -1), bias_ref[...].reshape(1, -1))
            second[rows, :] = normed.astype(bf16)
            second_t[:, slot * TOK : (slot + 1) * TOK] = normed.T.astype(bf16)

    sums = jnp.zeros((1, HIDDEN_STEP), f32)
    for part in range(3):
        rows = pl.ds(part * TILE, TILE)
        hidden = dot(second[rows, :], up_ref[...], NN) + up_bias[...]
        active_grad = dot(down_ref[rows, :], weight_ref[...], NT)
        square = hidden * hidden
        bent = jnp.tanh(hidden * (ROOT + ROOT * CUBE * square))
        half = 0.5 + 0.5 * bent
        active = hidden * half
        slope = half + hidden * (half * (1.0 - bent)) * (ROOT + 3 * ROOT * CUBE * square)
        active_ref[rows, :] = active.astype(bf16)
        turned_ref[:, part * TILE : (part + 1) * TILE] = active.T.astype(bf16)
        grad = (slope * active_grad).astype(bf16)
        grad_ref[rows, :] = grad
        sums = sums + jnp.sum(grad.astype(f32), axis=0, keepdims=True)
        back[rows, :] += dot(grad, up_ref[...], NT)
    hidden_sum[...] = jnp.broadcast_to(sums, hidden_sum.shape)

    @pl.when(step == pl.num_programs(0) - 1)
    def _():
        sums_ref[...] = jnp.zeros(sums_ref.shape, f32)
        gain = gain_ref[...].reshape(1, -1)
        for slot in range(2):
            rows = pl.ds(slot * TOK, TOK)
            middle, grads = middle_ref[rows, :], back[rows, :]
            center = middle - jnp.mean(middle, axis=-1, keepdims=True)
            scale = lax.rsqrt(jnp.mean(center * center, axis=-1, keepdims=True) + EPS)
            unit = center * scale
            scaled = grads * gain
            mean_scaled = jnp.mean(scaled, axis=-1, keepdims=True)
            mean_both = jnp.mean(scaled * unit, axis=-1, keepdims=True)
            through = masked_ref[rows, :] + scale * (scaled - mean_scaled - unit * mean_both)
            through_ref[rows, :] = through
            branch = through.astype(bf16)
            branch_ref[rows, :] = branch
            for index, each in enumerate(
                (branch.astype(f32), down_ref[rows, :].astype(f32), grads * unit, grads)
            ):
                sums_ref[index : index + 1, :] += jnp.sum(each, axis=0, keepdims=True)
            for side in range(2):
                for high in range(2):
                    index = 2 * side + high
                    found = dot(output_ref[pl.ds(index * WIDTH, WIDTH), :], branch, NT)
                    sends[2 * slot + side][high] = found.astype(bf16)


def feed(slabs, output_own, ordered, masked, down, output_bias, gain, bias, up_bias, up, weight):
    bf16, f32 = jnp.bfloat16, jnp.float32
    model, hidden = up.shape
    tokens = 2 * TOK

    slab = fixed(2, WIDTH, TOK)
    table = fixed(tokens, model)
    vector = fixed(model)
    wide = along(tokens, HIDDEN_STEP, axis=1)
    tall = along(HIDDEN_STEP, tokens, axis=0)
    out = jax.ShapeDtypeStruct
    return pl.pallas_call(
        feed_kernel,
        grid=(hidden // HIDDEN_STEP,),
        in_specs=[slab] * 4
        + [fixed(model, model), fixed(TOK, model), fixed(TOK, model), table, table]
        + [vector] * 3
        + [along(1, HIDDEN_STEP, axis=1), along(model, HIDDEN_STEP, axis=1)]
        + [along(HIDDEN_STEP, model, axis=0)],
        out_specs=[table, wide, tall, wide, fixed(model, tokens), fixed(4, WIDTH, tokens)]
        + [table, table, fixed(8, model), along(8, HIDDEN_STEP, axis=1)]
        + [slab] * 4,
        out_shape=[
            out((tokens, model), f32),
            out((tokens, hidden), bf16),
            out((hidden, tokens), bf16),
            out((tokens, hidden), bf16),
            out((model, tokens), bf16),
            out((4, WIDTH, tokens), bf16),
            out((tokens, model), bf16),
            out((tokens, model), f32),
            out((8, model), f32),
            out((8, hidden), f32),
        ]
        + [out((2, WIDTH, TOK), bf16)] * 4,
        scratch_shapes=[pltpu.VMEM((tokens, model), bf16), pltpu.VMEM((tokens, model), f32)],
        compiler_params=pltpu.CompilerParams(vmem_limit_bytes=VMEM_LIMIT),
        cost_estimate=CHEAP,
        name="feed",
    )(*slabs, output_own, *ordered, masked, down, output_bias, gain, bias, up_bias, up, weight)


def halved(found, own, keep_ref, away_ref, place):
    zero, one = found[:, 0].astype(jnp.bfloat16), found[:, 1].astype(jnp.bfloat16)
    keep_ref[place] = jnp.where(own == 0, zero, one)
    away_ref[place] = jnp.where(own == 0, one, zero)


def wide_kernel(
    info, attended_ref, branch_ref, turned_ref, down_ref, vector_ref, keep_ref, away_ref
):
    rows = HIDDEN_STEP // 8
    found = dot(turned_ref[...], down_ref[...], NN)
    found = found.reshape(2, 2, 2, rows, found.shape[-1])
    every = slice(None)
    halved(found, info[1], keep_ref, away_ref, (every, every, slice(0, rows)))
    found = dot(attended_ref[0], branch_ref[...], NN).reshape(2, 4, WIDTH // 8, -1)
    found = jnp.concatenate((found, vector_ref[...]), 2)
    found = found.reshape(2, 2, 2, 32, found.shape[-1])
    halved(found, info[1], keep_ref, away_ref, (every, every, slice(rows, rows + 32)))


def tall_kernel(info, second_t, grad_ref, keep_ref, away_ref):
    found = dot(second_t[...], grad_ref[...], NN)
    found = found.reshape(8, 2, -1, found.shape[-1])
    every = slice(None)
    halved(found, info[1], keep_ref, away_ref, (every, 0))


def out_kernel(swap_ref, active_ref, weight_ref, middle_ref, bias_ref, out_ref, acc, lanes):
    step = pl.program_id(0)
    found = dot(active_ref[...], weight_ref[...], NN)

    @pl.when(step == 0)
    def _():
        acc[...] = middle_ref[...] + bias_ref[...].reshape(1, -1) + found

    @pl.when(step > 0)
    def _():
        acc[...] += found

    @pl.when(step == pl.num_programs(0) - 1)
    def _():
        for slot in range(2):
            for part, column in columns(out_ref.shape[-1]):
                for parity in range(2):
                    lanes[part, pl.ds(parity, HALF, stride=2), :] = acc[
                        pl.ds(slot * TOK + parity * HALF, HALF), column
                    ]
                out_ref[slot ^ swap_ref[0], :, column] = lanes[part]


def fixed(*shape):
    return pl.BlockSpec(shape, lambda step, *info: (0,) * len(shape))


def along(*shape, axis):
    return pl.BlockSpec(
        shape, lambda step, *info: tuple(step if i == axis else 0 for i in range(len(shape)))
    )


def stepped(kernel, name, steps, info, operands, in_specs, out_specs, out_shape, scratch=()):
    return pl.pallas_call(
        kernel,
        grid_spec=pltpu.PrefetchScalarGridSpec(
            num_scalar_prefetch=1,
            grid=(steps,),
            in_specs=in_specs,
            out_specs=out_specs,
            scratch_shapes=list(scratch),
        ),
        out_shape=out_shape,
        compiler_params=pltpu.CompilerParams(vmem_limit_bytes=VMEM_LESS),
        cost_estimate=CHEAP,
        name=name,
    )(info, *operands)


def wide_shares(info, attended, branch, turned, down, vectors):
    hidden, tokens = turned.shape
    model = branch.shape[-1]
    return stepped(
        wide_kernel,
        "wide_shares",
        hidden // HIDDEN_STEP,
        info,
        (attended, branch, turned, down, vectors),
        [
            pl.BlockSpec((1, WIDTH, tokens), lambda step, info: (step ^ info[0], 0, 0)),
            fixed(tokens, model),
            along(HIDDEN_STEP, tokens, axis=0),
            fixed(tokens, model),
            along(2, 4, 8, model, axis=0),
        ],
        [along(2, 2, 128, model, axis=0)] * 2,
        [jax.ShapeDtypeStruct((8, 2, 128, model), jnp.bfloat16)] * 2,
    )


def tall_shares(info, second_t, grad):
    tokens, hidden = grad.shape
    model = second_t.shape[0]
    return stepped(
        tall_kernel,
        "tall_shares",
        hidden // HIDDEN_STEP,
        info,
        (second_t, grad),
        [fixed(model, tokens), along(tokens, HIDDEN_STEP, axis=1)],
        [along(8, 1, model // 16, HIDDEN_STEP, axis=1)] * 2,
        [
            jax.ShapeDtypeStruct((8, hidden // HIDDEN_STEP, model // 16, HIDDEN_STEP), jnp.bfloat16)
        ]
        * 2,
    )


def layer_out(swap, active, weight, middle, bias):
    tokens, hidden = active.shape
    model = weight.shape[-1]
    return stepped(
        out_kernel,
        "layer_out",
        hidden // HIDDEN_STEP,
        swap,
        (active, weight, middle, bias),
        [
            along(tokens, HIDDEN_STEP, axis=1),
            along(HIDDEN_STEP, model, axis=0),
            fixed(tokens, model),
            fixed(model),
        ],
        fixed(2, TOK, model),
        jax.ShapeDtypeStruct((2, TOK, model), jnp.float32),
        [pltpu.VMEM((tokens, model), jnp.float32), *lanes_of(model)],
    )


def project_triples(grads, weights):
    grads = jnp.concatenate([each[0] for each in grads], -1)
    return dot(grads, weights[...], NN)


def far_kernel(head0, heads, weights, out_ref):
    out_ref[0] = project_triples((head0, heads), weights).astype(jnp.bfloat16)


def near_kernel(head0, heads, weights, far_ref, keep_ref, away_ref):
    found = project_triples((head0, heads), weights) + far_ref[0].astype(jnp.float32)

    @pl.when(pl.program_id(0) % 2 == 0)
    def _():
        keep_ref[0] = found

    @pl.when(pl.program_id(0) % 2 == 1)
    def _():
        away_ref[0] = found.astype(jnp.bfloat16)


def back_specs(grads, weights, first):
    def block(width):
        return pl.BlockSpec((1, TOK, width), lambda step: (first + step, 0, 0))

    return [block(each.shape[-1]) for each in grads] + [
        pl.BlockSpec(weights.shape, lambda step: (0, 0))
    ]


def far_projection(grads, weights):
    model = weights.shape[-1]
    return pl.pallas_call(
        far_kernel,
        grid=(4,),
        in_specs=back_specs(grads, weights, 4),
        out_specs=pl.BlockSpec((1, TOK, model), lambda step: (step, 0, 0)),
        out_shape=jax.ShapeDtypeStruct((4, TOK, model), jnp.bfloat16),
        compiler_params=pltpu.CompilerParams(vmem_limit_bytes=VMEM_LESS),
        cost_estimate=CHEAP,
        name="far_projection",
    )(*grads, weights)


def near_projection(grads, weights, far):
    model = weights.shape[-1]
    own = pl.BlockSpec((1, TOK, model), lambda step: (step, 0, 0))
    pair = pl.BlockSpec((1, TOK, model), lambda step: (step // 2, 0, 0))
    return pl.pallas_call(
        near_kernel,
        grid=(4,),
        in_specs=[*back_specs(grads, weights, 0), own],
        out_specs=[pair, pair],
        out_shape=[
            jax.ShapeDtypeStruct((2, TOK, model), jnp.float32),
            jax.ShapeDtypeStruct((2, TOK, model), jnp.bfloat16),
        ],
        compiler_params=pltpu.CompilerParams(vmem_limit_bytes=VMEM_LESS),
        cost_estimate=CHEAP,
        name="near_projection",
    )(*grads, weights, far)


LATE_ROWS = 112
TRIPLE = 3 * HEAD_DIM


def late_kernel(info, *refs):
    normed, (head0, heads, keep_ref, away_ref) = refs[:BLOCKS], refs[BLOCKS:]
    total, acc = 0.0, None
    for delta in range(BLOCKS):
        grads = jnp.concatenate((head0[delta], heads[delta]), -1)
        found = dot(normed[delta][0:TOK, :], grads, TN)
        acc = found if acc is None else acc + found
        total = total + jnp.sum(grads.astype(jnp.float32), axis=0, keepdims=True)
    rows = acc.shape[0] // 8

    def packed(values):
        return jnp.concatenate(
            [values[:, 256 * head : 256 * head + TRIPLE] for head in range(OWN_HEADS)], 1
        )

    width = OWN_HEADS * TRIPLE
    sums = jnp.broadcast_to(packed(total), (8, LATE_ROWS - rows, width))
    found = jnp.concatenate((packed(acc).reshape(8, rows, width), sums), 1)
    found = found.reshape(2, 2, 2, LATE_ROWS, width)
    zero, one = found[:, 0].astype(jnp.bfloat16), found[:, 1].astype(jnp.bfloat16)
    keep_ref[...] = jnp.where(info[0] == 0, zero, one)
    away_ref[...] = jnp.where(info[0] == 0, one, zero)


def late_shares(info, normed, grads):
    width = OWN_HEADS * TRIPLE
    return stepped(
        late_kernel,
        "late_shares",
        1,
        info,
        (*normed, *grads),
        [fixed(*each.shape) for each in (*normed, *grads)],
        [fixed(2, 2, LATE_ROWS, width)] * 2,
        [jax.ShapeDtypeStruct((2, 2, LATE_ROWS, width), jnp.bfloat16)] * 2,
    )


def ordered_by(bits, refs):
    found = [ref[...].astype(jnp.float32) for ref in refs]
    for bit in range(2):
        flip = (bits >> bit & 1) == 1
        found = [
            jnp.where(flip, found[i ^ (1 << bit)], found[i]) for i in range(len(found))
        ]
    return found


def early_end_kernel(info, *refs):
    early, (down_ref, output_ref, up_ref, sums_ref) = refs[:4], refs[4:]
    rows = down_ref.shape[0] // 4
    more = output_ref.shape[0] // 4
    model = output_ref.shape[1]
    below = rows + more + 8
    for index, each in enumerate(ordered_by(info[0], early)):
        down_ref[index * rows : (index + 1) * rows, :] = each[0:rows]
        output_ref[index * more : (index + 1) * more, :] = each[rows : rows + more]
        if index == 0:
            sums_ref[...] = each[rows + more : below]
        for part, column in enumerate(range(0, up_ref.shape[1], model)):
            up_ref[index * more : (index + 1) * more, column : column + model] = each[
                below + part * more : below + (part + 1) * more
            ]


def early_end(info, early, hidden):
    model = early[0].shape[-1]
    part = model // 8
    return pl.pallas_call(
        early_end_kernel,
        in_specs=[pl.BlockSpec(memory_space=pltpu.SMEM)]
        + [pl.BlockSpec(memory_space=pltpu.VMEM)] * 4,
        out_specs=[pl.BlockSpec(memory_space=pltpu.VMEM)] * 4,
        out_shape=[
            jax.ShapeDtypeStruct((hidden // 8, model), jnp.float32),
            jax.ShapeDtypeStruct((part, model), jnp.float32),
            jax.ShapeDtypeStruct((part, hidden), jnp.float32),
            jax.ShapeDtypeStruct((8, model), jnp.float32),
        ],
        compiler_params=pltpu.CompilerParams(vmem_limit_bytes=VMEM_LESS),
        cost_estimate=CHEAP,
        name="early_end",
    )(info, *early)


def late_end_kernel(info, *refs):
    pieces_in, refs = refs[:4], refs[4:]
    weights, (gain_ref, bias_ref), refs = refs[:3], refs[3:5], refs[5:]
    outs, (sums_ref, norm_ref) = refs[:3], refs[3:]
    part = outs[0].shape[0]
    pieces_in = ordered_by(info[0], pieces_in)
    groups_in = [
        jnp.concatenate((pieces_in[2 * core][side], pieces_in[2 * core + 1][side]), 0)
        for side in range(2)
        for core in range(2)
    ]
    both = bias_grad = jnp.zeros((8, part), jnp.float32)
    ones = jnp.ones((8, outs[0].shape[1]), jnp.float32)
    for kind, (weight, out) in enumerate(zip(weights, outs)):
        found = jnp.concatenate(
            [
                each[:, TRIPLE * head + HEAD_DIM * kind : TRIPLE * head + HEAD_DIM * (kind + 1)]
                for each in groups_in
                for head in range(OWN_HEADS)
            ],
            1,
        )
        out[...] = found[0:part]
        sums_ref[8 * kind : 8 * kind + 8, :] = found[part : part + 8]
        mine = weight[...].astype(jnp.float32)

        def across(values):
            return lax.dot_general(ones, values, NT, precision=HIGH)

        bias_grad = bias_grad + across(mine * found[part : part + 1])
        both = both + across(mine * found[0:part])
    norm_ref[0:8, :] = (both - bias_ref[0] * bias_grad) / gain_ref[0]
    norm_ref[8:16, :] = bias_grad


def late_end(info, late, weights, gain, bias):
    model = weights[0].shape[0]
    part = model // 8
    own = pl.BlockSpec((part, model), lambda step, info: (info[1], 0))
    vector = pl.BlockSpec((1, 1, part), lambda step, info: (info[1], 0, 0))
    return stepped(
        late_end_kernel,
        "late_end",
        1,
        info,
        (*late, *weights, gain.reshape(8, 1, part), bias.reshape(8, 1, part)),
        [*[fixed(*late[0].shape)] * 4, own, own, own, vector, vector],
        [*[fixed(part, model)] * 3, fixed(24, model), fixed(16, part)],
        [
            *[jax.ShapeDtypeStruct((part, model), jnp.float32)] * 3,
            jax.ShapeDtypeStruct((24, model), jnp.float32),
            jax.ShapeDtypeStruct((16, part), jnp.float32),
        ],
    )


def whole(*shape):
    return pl.BlockSpec(shape, lambda head, info: (0,) * len(shape))


def per_head(*shape, first=0):
    return pl.BlockSpec((1, *shape), lambda head, info: (first + head, *(0,) * len(shape)))


def attention(info, normed, weight, bias):
    bf16, f32 = jnp.bfloat16, jnp.float32
    model = weight.shape[1]

    def out(dtype, *shape):
        return jax.ShapeDtypeStruct(shape, dtype)

    return pl.pallas_call(
        forward_kernel,
        grid_spec=pltpu.PrefetchScalarGridSpec(
            num_scalar_prefetch=1,
            grid=(OWN_HEADS,),
            in_specs=[
                *[whole(SENT, model)] * BLOCKS,
                pl.BlockSpec((384, model), lambda head, info: (head, 0)),
                pl.BlockSpec((1, 384), lambda head, info: (0, head)),
            ],
            out_specs=[
                *[whole(4, WIDTH, TOK)] * 2,
                per_head(HEAD_DIM, LEN),
                per_head(8, LEN),
                per_head(LEN, 128),
                per_head(PAR, 128),
                per_head(LEN, 128),
                per_head(HEAD_DIM, LEN),
                per_head(LEN, 128),
            ],
            scratch_shapes=[
                pltpu.VMEM((128, LEN), bf16),
                pltpu.VMEM((8, LEN), f32),
                pltpu.VMEM((80, LEN), f32),
                pltpu.VMEM((BLOCKS, HEAD_DIM, TOK), bf16),
            ],
        ),
        out_shape=[
            *[out(bf16, 4, WIDTH, TOK)] * 2,
            out(f32, OWN_HEADS, HEAD_DIM, LEN),
            out(f32, OWN_HEADS, 8, LEN),
            out(bf16, OWN_HEADS, LEN, 128),
            out(bf16, OWN_HEADS, PAR, 128),
            out(bf16, OWN_HEADS, LEN, 128),
            out(bf16, OWN_HEADS, HEAD_DIM, LEN),
            out(bf16, OWN_HEADS, LEN, 128),
        ],
        compiler_params=pltpu.CompilerParams(vmem_limit_bytes=VMEM_LIMIT),
        name="attention",
    )(info, *normed, weight, bias)


def attention_back(heads, info, held, grads, result, total):
    first, count = heads
    bf16, f32 = jnp.bfloat16, jnp.float32
    return pl.pallas_call(
        functools.partial(backward_kernel, first),
        grid_spec=pltpu.PrefetchScalarGridSpec(
            num_scalar_prefetch=1,
            grid=(count,),
            in_specs=[
                per_head(LEN, 128, first=first),
                per_head(PAR, 128, first=first),
                per_head(LEN, 128, first=first),
                per_head(HEAD_DIM, LEN, first=first),
                per_head(LEN, 128, first=first),
                *[whole(1, WIDTH, TOK)] * 4,
                whole(4, WIDTH, TOK),
                per_head(HEAD_DIM, LEN, first=first),
                per_head(8, LEN, first=first),
            ],
            out_specs=pl.BlockSpec((BLOCKS, TOK, 256), lambda head, info: (0, 0, head)),
            scratch_shapes=[
                pltpu.VMEM((BLOCKS, HEAD_DIM, TOK), bf16),
                pltpu.VMEM((128, LEN), bf16),
                pltpu.VMEM((1, LEN), f32),
                pltpu.VMEM((128, LEN), f32),
                pltpu.VMEM((LEN, 128), f32),
                pltpu.VMEM((LEN, 128), f32),
                pltpu.VMEM((LEN, 128), f32),
            ],
        ),
        out_shape=jax.ShapeDtypeStruct((BLOCKS, TOK, count * 256), bf16),
        compiler_params=pltpu.CompilerParams(vmem_limit_bytes=VMEM_LESS),
        cost_estimate=CHEAP,
        name="attention_back",
    )(info, *held, *grads, result, total)


def flipped(array, axis, bit):
    zero, one = (lax.index_in_dim(array, i, axis, keepdims=False) for i in range(2))
    return jnp.stack((pick(bit, zero, one), pick(bit, one, zero)), axis)


def entry(array, axis, index):
    return lax.dynamic_index_in_dim(array, index, axis, keepdims=False)


def reduced(array, axis, bit, pairs):
    return plus(entry(array, axis, bit), send(entry(array, axis, 1 - bit), pairs))


def plus(left, right):
    return (left.astype(jnp.float32) + right.astype(jnp.float32)).astype(jnp.bfloat16)


def collected(array, bit, pairs):
    other = send(array, pairs)
    return jnp.stack((pick(bit, array, other), pick(bit, other, array)))


def packed_rows(
    layer_input, doc_ids, cotangent, attn_norm_gain, attn_norm_bias, query_weight, query_bias,
    key_weight, value_weight, value_bias, output_weight, output_bias, feed_norm_gain,
    feed_norm_bias, up_weight, up_bias, down_weight, down_bias,
):
    bf16, f32 = jnp.bfloat16, jnp.float32
    model = layer_input.shape[-1]
    hidden_width = up_weight.shape[-1]
    row, seq = lax.axis_index("row"), lax.axis_index("seq")
    x, core, z, y = row >> 1, row & 1, seq >> 1, seq & 1
    swap = (z & 1)[None].astype(jnp.int32)
    place = 4 * core + 2 * (z & 1) + y
    group = 2 * y + core
    info = jnp.stack((place, OWN_HEADS * group)).astype(jnp.int32)

    ordered, blocks = [], []
    for slot in range(2):
        values, block = first_norm(
            slot, swap, layer_input, doc_ids, attn_norm_gain, attn_norm_bias
        )
        ordered.append(values)
        blocks.append(block)
    first = send(blocks[0], to_row(0))
    first, blocks[1] = tied((first, blocks[1]))
    normed = [first, send(first, SWAP_Y)]
    second = send(blocks[1], to_row(1))

    def other_order(array):
        array = array.reshape(2, 2, WIDTH, model)
        return flipped(flipped(array, 0, y), 1, z >> 1).reshape(4 * WIDTH, model)

    def own_columns(weight):
        own = lax.dynamic_slice_in_dim(weight, group * WIDTH, WIDTH, weight.ndim - 1)
        return own.reshape(*weight.shape[:-1], OWN_HEADS, HEAD_DIM)

    query_own, key_own, value_own = map(own_columns, (query_weight, key_weight, value_weight))
    triple_weight = jnp.stack((query_own, key_own, value_own), 2)
    triple_weight = jnp.pad(triple_weight, ((0, 0),) * 3 + ((0, 128 - HEAD_DIM),))
    triple_weight = triple_weight.reshape(model, OWN_HEADS * 384).T
    query_row, value_row = own_columns(query_bias), own_columns(value_bias)
    triple_bias = jnp.stack((query_row, jnp.zeros_like(query_row), value_row), 1)
    triple_bias = jnp.pad(triple_bias, ((0, 0), (0, 0), (0, 128 - HEAD_DIM))).reshape(-1)
    docs = doc_ids.reshape(2, HALF, 2).transpose(0, 2, 1).reshape(2, TOK)
    docs = flipped(docs, 0, z & 1)
    masked_grad = jnp.where((docs >= 0)[..., None], moved(sort_kernel, swap, cotangent), 0.0)
    down_grad = masked_grad.astype(bf16)
    output_own = other_order(output_weight)
    back_weight = jnp.stack((query_own, key_own, value_own, jnp.zeros_like(key_own)), 2)
    back_weight = back_weight.reshape(model, OWN_HEADS * 256).T
    (
        normed, second, output_own, back_weight, triple_weight, triple_bias, ordered_rows,
        masked_grad, down_grad,
    ) = tied(
        (
            normed, second, output_own, back_weight, triple_weight, triple_bias,
            jnp.stack(ordered), masked_grad, down_grad,
        )
    )
    normed.extend((second, send(second, SWAP_Y)))
    normed.extend([send(block, SWAP_CORE) for block in normed])
    sends, far_sends, result, total, *kept = attention(
        info, normed, triple_weight, triple_bias[None]
    )
    far_sends = send(far_sends, SWAP_CORE)
    slabs = [
        send(jnp.stack((sends[index], far_sends[index])), to_owner(index)) for index in range(4)
    ]
    (
        middle, active, turned, hidden_grad, second_t, attended, branch_grad, middle_grad, sums,
        hidden_sum, *slabs,
    ) = feed(
        slabs, output_own, ordered, masked_grad.reshape(2 * TOK, model),
        down_grad.reshape(2 * TOK, model), output_bias, feed_norm_gain, feed_norm_bias,
        up_bias[None], up_weight, down_weight,
    )
    grads = [send(slabs[index], inverse(to_owner(index))) for index in range(4)]

    vectors = [each.reshape(8, -1) for each in (*sums[:4], hidden_sum[0])]
    vectors = jnp.concatenate(vectors, 1)[:, None, None]
    vectors = jnp.pad(vectors, ((0, 0), (0, 3), (0, 7), (0, 0)))
    share_info = jnp.stack((2 * y + (z >> 1), core)).astype(jnp.int32)
    wide, wide_away = wide_shares(
        share_info, attended, branch_grad, turned, down_grad.reshape(2 * TOK, model), vectors
    )
    wide_away, second_t, hidden_grad, grads[0], grads[1] = tied(
        (wide_away, second_t, hidden_grad, grads[0], grads[1])
    )
    wide_away = send(wide_away, SWAP_CORE)
    tall, tall_away = tall_shares(share_info, second_t, hidden_grad)
    grads, wide, wide_away, tall, tall_away = tied((grads, wide, wide_away, tall, tall_away))
    grads.append(send(jnp.stack([pair[1] for pair in grads]), SWAP_CORE))
    tall_away = send(tall_away, SWAP_CORE)
    wide = plus(wide, wide_away).reshape(2, 2, 2, 2, -1, model)
    grads, wide = tied((grads, wide))
    wide_away = send(entry(wide, 3, 1 - x), SWAP_X)

    def back(heads):
        return attention_back(heads, info, kept, grads, result, total)

    head0 = back((0, 1))
    head0, grads, tall_away = tied((head0, grads, tall_away))
    tall = plus(tall, tall_away).reshape(2, 2, 2, hidden_width // model, 2, -1, model)
    tall, grads = tied((tall, grads))
    tall_away = send(entry(tall, 2, 1 - y), SWAP_Y)
    heads = back((1, 2))
    triple_grads = (head0, heads)
    far_half = far_projection(triple_grads, back_weight)
    far_half, triple_grads, wide_away, tall_away = tied(
        (far_half, triple_grads, wide_away, tall_away)
    )
    far_half = send(far_half, SWAP_CORE)
    late, late_away = late_shares((z & 1)[None].astype(jnp.int32), normed, triple_grads)
    far_half, late, late_away = tied((far_half, late, late_away))
    wide, tall = plus(entry(wide, 3, x), wide_away), plus(entry(tall, 2, y), tall_away)
    wide_away = send(entry(wide, 2, 1 - y), SWAP_Y)
    tall_away = send(entry(tall, 3, 1 - x), SWAP_X)
    late_away = send(late_away, SWAP_Z_LOW)
    near_keep, near_away = near_projection(triple_grads, back_weight, far_half)
    pieces_away = (near_away[0, :96], near_away[0, 96:], near_away[1])
    near_away = [send(each, SWAP_Y) for each in pieces_away]
    near_keep, near_away[0], wide_away, tall_away, late_away, active, middle = tied(
        (near_keep, near_away[0], wide_away, tall_away, late_away, active, middle)
    )
    tall = plus(entry(tall, 3, x), tall_away).reshape(2, 2, -1, model)
    early = jnp.concatenate((plus(entry(wide, 2, y), wide_away), tall), 2)
    late = plus(late, late_away)
    early_away = send(entry(early, 1, 1 - (z & 1)), SWAP_Z_LOW)
    late_away = send(entry(late, 0, 1 - (z >> 1)), SWAP_Z_HIGH)
    near_away, early_away, late_away, active, middle = tied(
        (near_away, early_away, late_away, active, middle)
    )
    early = plus(entry(early, 1, z & 1), early_away)
    early_away = send(entry(early, 0, 1 - (z >> 1)), SWAP_Z_HIGH)
    near_away = (jnp.concatenate(near_away[:2], 0), near_away[2])
    returned = []
    for slot in range(2):
        both = (near_keep[slot] + near_away[slot].astype(f32)).astype(bf16)
        returned.append(send(both, inverse(to_row(slot))))
    late = plus(entry(late, 0, z >> 1), late_away).reshape(2, 2, -1, late.shape[-1])
    late = reduced(late, 1, x, SWAP_X)
    other = send(entry(late, 0, 1 - y), SWAP_Y)
    out = layer_out(swap, active, down_weight, middle, down_bias)
    other, out, early_away = tied((other, out, early_away))
    early = plus(entry(early, 0, z >> 1), early_away)
    early = [early, send(early, SWAP_X)]
    late = entry(late, 0, y)
    late = jnp.stack((pick(y, late, other), pick(y, other, late)))
    late = [late, send(late, SWAP_X)]

    def all_four(pair):
        return [*pair, *(send(each, SWAP_CORE) for each in pair)]

    input_grad = last_norm(
        swap, ordered_rows, returned, middle_grad.reshape(2, TOK, model), attn_norm_gain
    )
    end_info = jnp.stack((2 * core + x, seq)).astype(jnp.int32)
    grad_down, grad_output, grad_up, sums = early_end(
        end_info, all_four(early), hidden_width
    )
    part = model // 8
    output_sum, down_sum, grad_feed_gain, grad_feed_bias, up_sum = jnp.split(
        sums[0], (part, 2 * part, 3 * part, 4 * part)
    )
    grad_query, grad_key, grad_value, sums, norm = late_end(
        end_info,
        all_four(late),
        (query_weight, key_weight, value_weight),
        attn_norm_gain,
        attn_norm_bias,
    )

    def own_part(array):
        return lax.dynamic_slice_in_dim(array, seq * part, part, 0)

    query_sum, value_sum = own_part(sums[0]), own_part(sums[16])
    grad_attn_gain, grad_attn_bias = norm[0], norm[8]
    return (
        out,
        input_grad,
        grad_attn_gain,
        grad_attn_bias,
        grad_query,
        query_sum,
        grad_key,
        grad_value,
        value_sum,
        grad_output,
        output_sum,
        grad_feed_gain,
        grad_feed_bias,
        grad_up,
        up_sum,
        grad_down,
        down_sum,
    )


def solution(mesh):
    placed = (
        P("row", "seq", None),
        P("row", "seq"),
        P("row", "seq", None),
        P(),
        P(),
        P(),
        P(),
        P(),
        P(),
        P(),
        P(),
        P(),
        P(),
        P(),
        P(),
        P(),
        P(),
        P(),
    )
    chosen = packed_rows if dict(mesh.shape) == {"row": 4, "seq": 8} else per_device
    return jax.shard_map(
        chosen,
        mesh=mesh,
        in_specs=placed,
        out_specs=(
            P("row", "seq", None),
            P("row", "seq", None),
            P("seq"),
            P("seq"),
            P("seq", None),
            P("seq"),
            P("seq", None),
            P("seq", None),
            P("seq"),
            P("seq", None),
            P("seq"),
            P("seq"),
            P("seq"),
            P("seq", None),
            P("seq"),
            P("seq", None),
            P("seq"),
        ),
        check_vma=False,
    )
```

```python
import functools
import math

import jax
import jax.numpy as jnp
from jax import lax
from jax.experimental import pallas as pl
from jax.experimental.pallas import tpu as pltpu
from jax.sharding import PartitionSpec as P

HEADS = 12
HEAD_DIM = 64
GROUP = 4
FIRST_DILATION = 1
SECOND_DILATION = 2
THIRD_DILATION = 4
FOURTH_DILATION = 6
FIFTH_DILATION = 12


EPS = 1e-05
NEG = -1e30
HIGH = lax.Precision.HIGHEST


def swapped(array, axis, apart):
    return lax.ppermute(array, axis, [(i, i ^ 1 << apart) for i in range(lax.axis_size(axis))])


def for_sending(array):

    def short(part):
        return part.astype(jnp.bfloat16) if part.dtype == jnp.float32 else part

    return jax.tree.map(short, array)


def layer_norm(values, gain, bias):
    center = values - jnp.mean(values, axis=-1, keepdims=True)
    spread = jnp.mean(center * center, axis=-1, keepdims=True)
    return center * lax.rsqrt(spread + EPS) * gain + bias


def project(inputs, weight):
    return jnp.einsum("ntd,df->ntf", inputs, weight, preferred_element_type=jnp.float32)


def project_back(grads, weight):
    return jnp.einsum("ntf,df->ntd", grads, weight, preferred_element_type=jnp.float32)


def weight_grad(inputs, grads):
    return jnp.einsum("ntd,ntf->df", inputs, grads, preferred_element_type=jnp.float32)


def column_sum(grads):
    return jnp.sum(grads.astype(jnp.float32), axis=(0, 1))


def pick_pairs(values, stride, picker):
    sequences, tokens, kinds, model_width = values.shape
    head_count = picker.shape[1]
    shaped = values.reshape(
        sequences, tokens // stride, stride, kinds, head_count, model_width // head_count
    )
    picked = jnp.einsum(
        "nsrche,rh->nsche", shaped, picker.astype(jnp.bfloat16), preferred_element_type=jnp.float32
    )
    return picked.astype(jnp.bfloat16).reshape(sequences, tokens // stride, kinds, model_width)


def spread_grads(values, stride, picker):
    sequences, slot_count, kinds, model_width = values.shape
    head_count = picker.shape[1]
    shaped = values.reshape(sequences, slot_count, kinds, head_count, model_width // head_count)
    spread = jnp.einsum("nsche,rh->nsrche", shaped, picker.astype(jnp.float32), precision=HIGH)
    return spread.reshape(sequences, slot_count * stride, kinds, model_width)


def group_gather(pieces, depth_list, device):
    gathered = list(pieces)
    for bit_index in range(max(depth_list)):
        active = [branch for branch in range(len(pieces)) if depth_list[branch] > bit_index]
        packed = jnp.concatenate([gathered[branch] for branch in active], 1)
        partner = swapped(packed, "seq", bit_index)
        lower = device // 2**bit_index % 2 == 0
        start = 0
        for branch in active:
            count = gathered[branch].shape[1]
            other = partner[:, start : start + count]
            start = start + count
            gathered[branch] = jnp.where(
                lower,
                jnp.concatenate((gathered[branch], other), 1),
                jnp.concatenate((other, gathered[branch]), 1),
            )
    return gathered


def group_return(pieces, depth_list, device):
    held = list(pieces)
    for bit_index in range(max(depth_list)):
        active = [branch for branch in range(len(pieces)) if depth_list[branch] > bit_index]
        lower = device // 2**bit_index % 2 == 0
        keep_parts = []
        send_parts = []
        for branch in active:
            sequences, count, kinds, model_width = held[branch].shape
            devices_left = 2 ** (depth_list[branch] - bit_index)
            slot_count = count // devices_left
            shaped = held[branch].reshape(
                sequences, devices_left // 2, 2, slot_count, kinds, model_width
            )
            even_part = shaped[:, :, 0].reshape(sequences, count // 2, kinds, model_width)
            odd_part = shaped[:, :, 1].reshape(sequences, count // 2, kinds, model_width)
            keep_parts.append(jnp.where(lower, even_part, odd_part))
            send_parts.append(jnp.where(lower, odd_part, even_part))
        received = swapped(for_sending(jnp.concatenate(send_parts, 1)), "seq", bit_index)
        start = 0
        for branch, kept in zip(active, keep_parts):
            count = kept.shape[1]
            held[branch] = kept + received[:, start : start + count]
            start = start + count
    return held


def per_device(
    layer_input,
    doc_ids,
    cotangent,
    attn_norm_gain,
    attn_norm_bias,
    query_weight,
    query_bias,
    key_weight,
    value_weight,
    value_bias,
    output_weight,
    output_bias,
    feed_norm_gain,
    feed_norm_bias,
    up_weight,
    up_bias,
    down_weight,
    down_bias,
):
    sequences, tokens, model_width = layer_input.shape
    head_count = HEADS
    head_size = HEAD_DIM
    score_scale = head_size ** (-0.5)
    device = lax.axis_index("seq")
    axis_count = lax.axis_size("seq")
    branch_strides = (
        FIRST_DILATION,
        SECOND_DILATION,
        THIRD_DILATION,
        FOURTH_DILATION,
        FIFTH_DILATION,
    )
    group_sizes = tuple((min(GROUP * 2**branch, axis_count) for branch in range(5)))
    depth_list = tuple((group_size.bit_length() - 1 for group_size in group_sizes))
    slot_counts = tuple((tokens // stride for stride in branch_strides))
    pickers = tuple(
        (
            jnp.arange(stride)[:, None] == jnp.arange(head_count)[None, :] % stride
            for stride in branch_strides
        )
    )
    docs_all = lax.all_gather(doc_ids, "seq", axis=1, tiled=True)
    segment_docs = []
    for branch in range(5):
        group_size = group_sizes[branch]
        group_start = device // group_size * group_size * tokens
        segment_docs.append(lax.dynamic_slice_in_dim(docs_all, group_start, group_size * tokens, 1))
    masked_grad = jnp.where((doc_ids >= 0)[..., None], cotangent, 0.0)
    h_first = layer_norm(layer_input, attn_norm_gain, attn_norm_bias).astype(jnp.bfloat16)
    query_low = (project(h_first, query_weight) + query_bias).astype(jnp.bfloat16)
    key_low = project(h_first, key_weight).astype(jnp.bfloat16)
    value_low = (project(h_first, value_weight) + value_bias).astype(jnp.bfloat16)
    pairs_low = jnp.stack((key_low, value_low), 2)
    own_sets = [
        pick_pairs(pairs_low, branch_strides[branch], pickers[branch]) for branch in range(5)
    ]
    gathered_sets = group_gather(own_sets, depth_list, device)

    def branch_scores(head_index, branch):
        stride = branch_strides[branch]
        group_size = group_sizes[branch]
        slot_count = slot_counts[branch]
        offset = head_index % stride
        chosen = jnp.arange(stride) == offset
        query_head = lax.dynamic_slice_in_dim(query_low, head_index * head_size, head_size, 2)
        query_sel = lax.dynamic_index_in_dim(
            query_head.reshape(sequences, slot_count, stride, head_size), offset, 2, keepdims=False
        )
        key_sel = lax.dynamic_slice_in_dim(
            gathered_sets[branch][:, :, 0], head_index * head_size, head_size, 2
        )
        value_sel = lax.dynamic_slice_in_dim(
            gathered_sets[branch][:, :, 1], head_index * head_size, head_size, 2
        )
        key_docs = lax.dynamic_index_in_dim(
            segment_docs[branch].reshape(sequences, group_size * slot_count, stride),
            offset,
            2,
            keepdims=False,
        )
        query_docs = lax.dynamic_index_in_dim(
            doc_ids.reshape(sequences, slot_count, stride), offset, 2, keepdims=False
        )
        key_index = jnp.arange(group_size * slot_count, dtype=jnp.int32)
        query_index = device % group_size * slot_count + jnp.arange(slot_count, dtype=jnp.int32)
        mask = (key_index[None, None, :] <= query_index[None, :, None]) & (
            key_docs[:, None, :] == query_docs[:, :, None]
        )
        score = jnp.where(
            mask,
            score_scale
            * jnp.einsum("nqe,nke->nqk", query_sel, key_sel, preferred_element_type=jnp.float32),
            NEG,
        )
        return (chosen, offset, query_sel, key_sel, value_sel, score)

    def head_forward(head_index):
        found = [branch_scores(head_index, branch) for branch in range(5)]
        total = jnp.full((sequences, tokens), NEG, dtype=jnp.float32)
        for branch in range(5):
            chosen, offset, query_sel, key_sel, value_sel, score = found[branch]
            part_total = jax.nn.logsumexp(score, axis=-1)
            spread = jnp.where(chosen, part_total[..., None], NEG).reshape(sequences, tokens)
            total = jnp.logaddexp(total, spread)
        result = jnp.zeros((sequences, tokens, head_size), dtype=jnp.float32)
        for branch in range(5):
            chosen, offset, query_sel, key_sel, value_sel, score = found[branch]
            stride = branch_strides[branch]
            total_sel = lax.dynamic_index_in_dim(
                total.reshape(sequences, slot_counts[branch], stride), offset, 2, keepdims=False
            )
            prob = jnp.exp(score - total_sel[..., None]).astype(jnp.bfloat16)
            part = jnp.einsum("nqk,nke->nqe", prob, value_sel, preferred_element_type=jnp.float32)
            result = result + jnp.where(chosen[:, None], part[:, :, None, :], 0.0).reshape(
                sequences, tokens, head_size
            )
        return (result, total)

    head_outs, totals = lax.map(head_forward, jnp.arange(head_count, dtype=jnp.int32))
    attended = (
        head_outs.transpose(1, 2, 0, 3).reshape(sequences, tokens, model_width).astype(jnp.bfloat16)
    )
    middle = layer_input + project(attended, output_weight) + output_bias
    h_second = layer_norm(middle, feed_norm_gain, feed_norm_bias).astype(jnp.bfloat16)
    hidden = project(h_second, up_weight) + up_bias
    active_full, gelu_pull = jax.vjp(jax.nn.gelu, hidden)
    active = active_full.astype(jnp.bfloat16)
    result_out = middle + project(active, down_weight) + down_bias
    down_grad = masked_grad.astype(jnp.bfloat16)
    grad_down_weight = weight_grad(active, down_grad)
    grad_down_bias = column_sum(down_grad)
    active_grad = jnp.einsum(
        "ntd,fd->ntf", down_grad, down_weight, preferred_element_type=jnp.float32
    )
    hidden_grad = gelu_pull(active_grad)[0].astype(jnp.bfloat16)
    grad_up_weight = weight_grad(h_second, hidden_grad)
    grad_up_bias = column_sum(hidden_grad)
    norm_input_grad = project_back(hidden_grad, up_weight)
    norm_pull = jax.vjp(layer_norm, middle, feed_norm_gain, feed_norm_bias)[1]
    middle_part, grad_feed_norm_gain, grad_feed_norm_bias = norm_pull(norm_input_grad)
    middle_grad = masked_grad + middle_part
    branch_grad = middle_grad.astype(jnp.bfloat16)
    grad_output_weight = weight_grad(attended, branch_grad)
    grad_output_bias = column_sum(branch_grad)
    attended_grad = project_back(branch_grad, output_weight).astype(jnp.bfloat16)

    def head_backward(item):
        head_index, total = item
        found = [branch_scores(head_index, branch) for branch in range(5)]
        out_grad = lax.dynamic_slice_in_dim(attended_grad, head_index * head_size, head_size, 2)
        balance = jnp.zeros((sequences, tokens), dtype=jnp.float32)
        kept = []
        for branch in range(5):
            chosen, offset, query_sel, key_sel, value_sel, score = found[branch]
            stride = branch_strides[branch]
            slot_count = slot_counts[branch]
            total_sel = lax.dynamic_index_in_dim(
                total.reshape(sequences, slot_count, stride), offset, 2, keepdims=False
            )
            grad_sel = lax.dynamic_index_in_dim(
                out_grad.reshape(sequences, slot_count, stride, head_size),
                offset,
                2,
                keepdims=False,
            )
            prob = jnp.exp(score - total_sel[..., None])
            flow = jnp.einsum(
                "nqe,nke->nqk", grad_sel, value_sel, preferred_element_type=jnp.float32
            )
            balance = balance + jnp.where(
                chosen, jnp.sum(prob * flow, axis=-1)[..., None], 0.0
            ).reshape(sequences, tokens)
            kept.append((prob, flow, grad_sel))
        query_part = jnp.zeros((sequences, tokens, head_size), dtype=jnp.float32)
        key_parts = []
        for branch in range(5):
            chosen, offset, query_sel, key_sel, value_sel, score = found[branch]
            prob, flow, grad_sel = kept[branch]
            stride = branch_strides[branch]
            balance_sel = lax.dynamic_index_in_dim(
                balance.reshape(sequences, slot_counts[branch], stride), offset, 2, keepdims=False
            )
            slope = (prob * (flow - balance_sel[..., None])).astype(jnp.bfloat16)
            part = score_scale * jnp.einsum(
                "nqk,nke->nqe", slope, key_sel, preferred_element_type=jnp.float32
            )
            query_part = query_part + jnp.where(chosen[:, None], part[:, :, None, :], 0.0).reshape(
                sequences, tokens, head_size
            )
            key_term = score_scale * jnp.einsum(
                "nqk,nqe->nke", slope, query_sel, preferred_element_type=jnp.float32
            )
            value_term = jnp.einsum(
                "nqk,nqe->nke",
                prob.astype(jnp.bfloat16),
                grad_sel,
                preferred_element_type=jnp.float32,
            )
            key_parts.append(jnp.stack((key_term, value_term), 2))
        return (query_part, balance, tuple(key_parts))

    query_heads, balances, far_parts = lax.map(
        head_backward, (jnp.arange(head_count, dtype=jnp.int32), totals)
    )
    returned_sets = []
    for branch in range(5):
        shaped = far_parts[branch].transpose(1, 2, 3, 0, 4)
        returned_sets.append(shaped.reshape(sequences, shaped.shape[1], 2, model_width))
    owned = group_return(returned_sets, depth_list, device)
    pair_grad = spread_grads(owned[0], branch_strides[0], pickers[0])
    for branch in range(1, 5):
        pair_grad = pair_grad + spread_grads(owned[branch], branch_strides[branch], pickers[branch])
    key_grad = pair_grad[:, :, 0].astype(jnp.bfloat16)
    value_grad = pair_grad[:, :, 1].astype(jnp.bfloat16)
    query_grad = (
        query_heads.transpose(1, 2, 0, 3)
        .reshape(sequences, tokens, model_width)
        .astype(jnp.bfloat16)
    )
    grad_query_weight = weight_grad(h_first, query_grad)
    grad_query_bias = column_sum(query_grad)
    grad_key_weight = weight_grad(h_first, key_grad)
    grad_value_weight = weight_grad(h_first, value_grad)
    grad_value_bias = column_sum(value_grad)
    first_grad = (
        project_back(query_grad, query_weight)
        + project_back(key_grad, key_weight)
        + project_back(value_grad, value_weight)
    )
    first_pull = jax.vjp(layer_norm, layer_input, attn_norm_gain, attn_norm_bias)[1]
    input_part, grad_attn_norm_gain, grad_attn_norm_bias = first_pull(first_grad)
    input_grad = middle_grad + input_part
    summed = (
        lax.psum_scatter(grad_attn_norm_gain, "seq", scatter_dimension=0, tiled=True),
        lax.psum_scatter(grad_attn_norm_bias, "seq", scatter_dimension=0, tiled=True),
        lax.psum_scatter(grad_query_weight, "seq", scatter_dimension=0, tiled=True),
        lax.psum_scatter(grad_query_bias, "seq", scatter_dimension=0, tiled=True),
        lax.psum_scatter(grad_key_weight, "seq", scatter_dimension=0, tiled=True),
        lax.psum_scatter(grad_value_weight, "seq", scatter_dimension=0, tiled=True),
        lax.psum_scatter(grad_value_bias, "seq", scatter_dimension=0, tiled=True),
        lax.psum_scatter(grad_output_weight, "seq", scatter_dimension=0, tiled=True),
        lax.psum_scatter(grad_output_bias, "seq", scatter_dimension=0, tiled=True),
        lax.psum_scatter(grad_feed_norm_gain, "seq", scatter_dimension=0, tiled=True),
        lax.psum_scatter(grad_feed_norm_bias, "seq", scatter_dimension=0, tiled=True),
        lax.psum_scatter(grad_up_weight, "seq", scatter_dimension=0, tiled=True),
        lax.psum_scatter(grad_up_bias, "seq", scatter_dimension=0, tiled=True),
        lax.psum_scatter(grad_down_weight, "seq", scatter_dimension=0, tiled=True),
        lax.psum_scatter(grad_down_bias, "seq", scatter_dimension=0, tiled=True),
    )
    final = (
        lax.psum(summed[0].astype(jnp.bfloat16), "row").astype(jnp.float32),
        lax.psum(summed[1].astype(jnp.bfloat16), "row").astype(jnp.float32),
        lax.psum(summed[2].astype(jnp.bfloat16), "row").astype(jnp.float32),
        lax.psum(summed[3].astype(jnp.bfloat16), "row").astype(jnp.float32),
        lax.psum(summed[4].astype(jnp.bfloat16), "row").astype(jnp.float32),
        lax.psum(summed[5].astype(jnp.bfloat16), "row").astype(jnp.float32),
        lax.psum(summed[6].astype(jnp.bfloat16), "row").astype(jnp.float32),
        lax.psum(summed[7].astype(jnp.bfloat16), "row").astype(jnp.float32),
        lax.psum(summed[8].astype(jnp.bfloat16), "row").astype(jnp.float32),
        lax.psum(summed[9].astype(jnp.bfloat16), "row").astype(jnp.float32),
        lax.psum(summed[10].astype(jnp.bfloat16), "row").astype(jnp.float32),
        lax.psum(summed[11].astype(jnp.bfloat16), "row").astype(jnp.float32),
        lax.psum(summed[12].astype(jnp.bfloat16), "row").astype(jnp.float32),
        lax.psum(summed[13].astype(jnp.bfloat16), "row").astype(jnp.float32),
        lax.psum(summed[14].astype(jnp.bfloat16), "row").astype(jnp.float32),
    )
    return (
        result_out,
        input_grad,
        final[0],
        final[1],
        final[2],
        final[3],
        final[4],
        final[5],
        final[6],
        final[7],
        final[8],
        final[9],
        final[10],
        final[11],
        final[12],
        final[13],
        final[14],
    )


TOK = 384
HALF = TOK // 2
BLOCKS = 8
LEN = TOK * BLOCKS
SEG = LEN // 2
PAR = SEG // 2
TILE = 256
TILES = PAR // TILE
OWN_HEADS = 3
WIDTH = OWN_HEADS * HEAD_DIM
FAR = -1e9
LOG2E = math.log2(math.e)
BOTH = ("row", "seq")
CHEAP = pl.CostEstimate(flops=0, bytes_accessed=0, transcendentals=0)
VMEM_LIMIT = 56 * 1024 * 1024
VMEM_LESS = 32 * 1024 * 1024


def permutation(move):
    pairs = []
    for x in range(2):
        for core in range(2):
            for z in range(4):
                for y in range(2):
                    core_to, z_to, y_to, x_to = move(core, z, y, x)
                    source = (2 * x + core) * 8 + 2 * z + y
                    pairs.append((source, (2 * x_to + core_to) * 8 + 2 * z_to + y_to))
    return pairs


def inverse(pairs):
    return sorted((b, a) for a, b in pairs)


def send(array, pairs):
    return lax.ppermute(array, BOTH, pairs)


def to_row(slot):
    return permutation(lambda core, z, y, x: (z >> 1, 2 * core + (slot ^ (z & 1)), y, x))


SWAP_CORE = permutation(lambda core, z, y, x: (1 - core, z, y, x))
SWAP_X = permutation(lambda core, z, y, x: (core, z, y, 1 - x))
SWAP_Y = permutation(lambda core, z, y, x: (core, z, 1 - y, x))
SWAP_Z_LOW = permutation(lambda core, z, y, x: (core, z ^ 1, y, x))
SWAP_Z_HIGH = permutation(lambda core, z, y, x: (core, z ^ 2, y, x))


def to_owner(delta):
    high, low, side = delta >> 2, delta >> 1 & 1, delta & 1
    return permutation(
        lambda core, z, y, x: (z >> 1, 2 * (core ^ high) + ((z & 1) ^ low), y ^ side, x)
    )


def pick(bit, zero, one):
    return jnp.where(bit == 0, zero, one)


def tied(values):
    return lax.optimization_barrier(values)


def columns(width):
    return [(part, slice(128 * part, 128 * (part + 1))) for part in range(width // 128)]


def read_sorted(in_ref, lanes):
    for part, column in columns(in_ref.shape[-1]):
        lanes[part] = in_ref[0, :, column]
    return [
        jnp.concatenate(
            [
                lanes[part, pl.ds(parity, in_ref.shape[1] // 2, stride=2), :]
                for part, _ in columns(in_ref.shape[-1])
            ],
            -1,
        )
        for parity in range(2)
    ]


def write_unsorted(out_ref, lanes, found):
    for part, column in columns(out_ref.shape[-1]):
        for parity in range(2):
            lanes[part, pl.ds(parity, HALF, stride=2), :] = found[parity][:, column]
        out_ref[0, :, column] = lanes[part]


def lanes_of(width, rows=TOK):
    return [pltpu.VMEM((width // 128, rows, 128), jnp.float32)]


SENT = TOK + 16


def norm_kernel(slot, swap_ref, in_ref, docs_ref, gain_ref, bias_ref, sorted_ref, out_ref, lanes):
    step = pl.program_id(0)
    gain, bias = gain_ref[...].reshape(1, -1), bias_ref[...].reshape(1, -1)
    count = in_ref.shape[1] // 2
    for parity, values in enumerate(read_sorted(in_ref, lanes)):
        rows = pl.ds(pl.multiple_of(parity * HALF + step * count, count), count)
        sorted_ref[rows, :] = values
        out_ref[rows, :] = layer_norm(values, gain, bias).astype(jnp.bfloat16)

    @pl.when(step == 0)
    def _():
        docs = docs_ref[pl.ds(slot ^ swap_ref[0], 1), :]
        lines = [
            jnp.broadcast_to(
                jnp.sum(jnp.where(found, 1.0, 0.0), axis=1, keepdims=True), (8, out_ref.shape[1])
            )
            for found in (docs == 0, docs < 0)
        ]
        out_ref[TOK:SENT, :] = jnp.concatenate(lines, 0).astype(jnp.bfloat16)


def first_norm(slot, swap, inputs, docs, gain, bias):
    width = inputs.shape[-1]
    steps = 2
    vector = pl.BlockSpec((width,), lambda step, swap: (0,))
    return pl.pallas_call(
        functools.partial(norm_kernel, slot),
        grid_spec=pltpu.PrefetchScalarGridSpec(
            num_scalar_prefetch=1,
            grid=(steps,),
            in_specs=[
                pl.BlockSpec(
                    (1, TOK // steps, width), lambda step, swap: (slot ^ swap[0], step, 0)
                ),
                pl.BlockSpec((2, TOK), lambda step, swap: (0, 0)),
                vector,
                vector,
            ],
            out_specs=[
                pl.BlockSpec((TOK, width), lambda step, swap: (0, 0)),
                pl.BlockSpec((SENT, width), lambda step, swap: (0, 0)),
            ],
            scratch_shapes=lanes_of(width, TOK // steps),
        ),
        out_shape=[
            jax.ShapeDtypeStruct((TOK, width), jnp.float32),
            jax.ShapeDtypeStruct((SENT, width), jnp.bfloat16),
        ],
        cost_estimate=CHEAP,
        name="first_norm",
    )(swap, inputs, docs, gain, bias)


def sort_kernel(swap_ref, in_ref, out_ref, lanes):
    for parity, values in enumerate(read_sorted(in_ref, lanes)):
        out_ref[0, pl.ds(parity * HALF, HALF), :] = values


def unsort_kernel(swap_ref, in_ref, out_ref, lanes):
    found = [in_ref[0, pl.ds(parity * HALF, HALF), :] for parity in range(2)]
    write_unsorted(out_ref, lanes, found)


def moved(kernel, swap, array):
    block = (1, TOK, array.shape[-1])
    return pl.pallas_call(
        kernel,
        grid_spec=pltpu.PrefetchScalarGridSpec(
            num_scalar_prefetch=1,
            grid=(2,),
            in_specs=[pl.BlockSpec(block, lambda slot, swap: (slot ^ swap[0], 0, 0))],
            out_specs=pl.BlockSpec(block, lambda slot, swap: (slot, 0, 0)),
            scratch_shapes=lanes_of(block[-1]),
        ),
        out_shape=jax.ShapeDtypeStruct(array.shape, array.dtype),
        name=kernel.__name__,
    )(swap, array)


def norm_back(values, grads, gain):
    center = values - jnp.mean(values, axis=-1, keepdims=True)
    scale = lax.rsqrt(jnp.mean(center * center, axis=-1, keepdims=True) + EPS)
    unit = center * scale
    scaled = grads * gain
    mean_scaled = jnp.mean(scaled, axis=-1, keepdims=True)
    mean_both = jnp.mean(scaled * unit, axis=-1, keepdims=True)
    return scale * (scaled - mean_scaled - unit * mean_both)


def last_kernel(swap_ref, values_ref, first_ref, second_ref, through_ref, gain_ref, out_ref, lanes):
    slot = pl.program_id(0) ^ swap_ref[0]
    found = []
    for parity in range(2):
        rows = pl.ds(parity * HALF, HALF)
        grads = jnp.where(slot == 0, first_ref[rows, :], second_ref[rows, :])
        part = norm_back(
            values_ref[0, rows, :], grads.astype(jnp.float32), gain_ref[...].reshape(1, -1)
        )
        found.append(through_ref[0, rows, :] + part)
    write_unsorted(out_ref, lanes, found)


def last_norm(swap, values, grads, through, gain):
    width = values.shape[-1]
    block = (1, TOK, width)
    own = pl.BlockSpec(block, lambda slot, swap: (slot ^ swap[0], 0, 0))
    whole_slot = pl.BlockSpec((TOK, width), lambda slot, swap: (0, 0))
    return pl.pallas_call(
        last_kernel,
        grid_spec=pltpu.PrefetchScalarGridSpec(
            num_scalar_prefetch=1,
            grid=(2,),
            in_specs=[
                own,
                whole_slot,
                whole_slot,
                own,
                pl.BlockSpec((width,), lambda slot, swap: (0,)),
            ],
            out_specs=pl.BlockSpec(block, lambda slot, swap: (slot, 0, 0)),
            scratch_shapes=lanes_of(width),
        ),
        out_shape=jax.ShapeDtypeStruct(values.shape, jnp.float32),
        cost_estimate=CHEAP,
        name="last_norm",
    )(swap, values, *grads, through, gain)


NT = (((1,), (1,)), ((), ()))
NN = (((1,), (0,)), ((), ()))


def dot(left, right, dims):
    return lax.dot_general(left, right, dims, preferred_element_type=jnp.float32)


def pieces():
    for block in range(BLOCKS):
        for parity in range(2):
            place = block // 4 * SEG + parity * PAR + block % 4 * HALF
            yield block, parity, place


def causal(parts, later):
    keys = lax.broadcasted_iota(jnp.int32, parts.shape, 0)
    queries = lax.broadcasted_iota(jnp.int32, parts.shape, 1)
    return jnp.where(keys <= queries + later, parts, NEG)


def aligned(start):
    return pl.multiple_of(start, TILE)


def groups(index):
    segment, query_parity, key_parity = index >> 2, index >> 1 & 1, index & 1
    query_base = segment * SEG + query_parity * PAR
    key_base = segment * SEG + key_parity * PAR
    later = jnp.where(query_parity < key_parity, -1, 0)
    return query_base, key_base, later


class Tile:
    def __init__(self, segment, parity, tile):
        self.rows = pl.ds(segment * SEG + parity * PAR + tile * TILE, TILE)
        self.parts = []
        for key_parity in range(2):
            start = segment * SEG + key_parity * PAR
            if tile:
                self.parts.append((start, tile * TILE, None))
            later = -1 if parity < key_parity else 0
            self.parts.append((start + tile * TILE, TILE, later))


def near_tiles():
    return [
        Tile(segment, parity, tile)
        for segment in range(2)
        for parity in range(2)
        for tile in range(TILES)
    ]


def in_turn(tiles, first, second):
    held = None
    for tile in tiles:
        found = first(tile)
        if held is not None:
            second(*held)
        held = tile, found
    second(*held)


def marks(head, place, first_doc, padding):
    row = lax.broadcasted_iota(jnp.int32, (16, place.shape[1]), 0)
    turn = lax.rem(place + (FIFTH_DILATION - head), FIFTH_DILATION)

    def members(dilation):
        return lax.rem(turn, dilation) == 0

    found = jnp.where(members(THIRD_DILATION), 2, 3)
    found = jnp.where(members(FOURTH_DILATION), 1, found)
    found = jnp.where(members(FIFTH_DILATION), 0, found)
    kind = jnp.broadcast_to(jnp.where(members(SECOND_DILATION), found, 4), row.shape)
    spot = place.astype(jnp.float32)
    doc = jnp.where(spot < first_doc, 0, jnp.where(spot >= LEN - padding, 2, 1))
    doc = jnp.broadcast_to(doc, row.shape)

    def chosen(condition):
        return jnp.where(condition, 1.0, 0.0)

    same_doc = chosen((row >= 8) & (row < 11) & (doc == row - 8))
    near = same_doc + chosen((row < 8) & (kind == (row & 3)))
    far = same_doc + chosen((row >= 12) & (kind == row - 12))
    other = row & 3
    count = (
        2
        + jnp.where(((other & 1) == 0) & ((kind & 1) == 0), 1, 0)
        + jnp.where((other < 2) & (kind < 2), 1, 0)
        + jnp.where((other == 0) & (kind == 0), 1, 0)
    )
    log3, log5 = math.log2(3), math.log2(5)
    high3, high5 = round(log3 * 64) / 64, round(log5 * 64) / 64

    def by_count(two, three, five):
        return jnp.where(count == 2, two, jnp.where(count == 3, three, five))

    key = jnp.where(
        row < 4,
        by_count(1.0, high3, high5),
        jnp.where(row < 8, by_count(0.0, log3 - high3, log5 - high5), by_count(0.0, 1.0, 2.0)),
    )
    key = jnp.where((kind < 4) & ((row < 8) | (row >= 12)), key, 0.0)
    key = jnp.where((row >= 8) & (row < 11) & (doc != row - 8), FAR, key)
    return near, far, key


def beside(mark):
    count = mark.shape[1]
    mark = jnp.concatenate(
        (jnp.zeros((HEAD_DIM, count)), mark, jnp.zeros((128 - HEAD_DIM - 16, count))), 0
    )
    return mark.T.astype(jnp.bfloat16)


def forward_kernel(info, *refs):
    normed, refs = refs[:BLOCKS], refs[BLOCKS:]
    (
        weight_ref, bias_ref, send_ref, away_ref, result_ref, total_ref, query_ref, far_ref, key_ref, key_t_ref, value_ref, value_t, most, acc, parted,
    ) = refs
    query, far, key, value, key_t = (
        each.at[0] for each in (query_ref, far_ref, key_ref, value_ref, key_t_ref)
    )
    bf16 = jnp.bfloat16
    head = pl.program_id(0)
    place = info[0]
    parity_of_head = (info[1] + head) & 1
    for delta in range(BLOCKS):
        block = place ^ delta
        found = dot(normed[delta][0:TOK, :], weight_ref[...], NT) + bias_ref[...]
        for parity in range(2):
            start = (block >> 2) * SEG + parity * PAR + (block & 3) * HALF
            rows = pl.ds(pl.multiple_of(start, HALF), HALF)
            part = found[parity * HALF : (parity + 1) * HALF]
            query[rows, :] = (part[:, 0:128] * (LOG2E * HEAD_DIM**-0.5)).astype(bf16)
            key[rows, :] = part[:, 128:256].astype(bf16)
            value[rows, :] = part[:, 256:384].astype(bf16)
    counts = sum(each[TOK:SENT, 0:128].astype(jnp.float32) for each in normed)
    first_doc, padding = counts[0:1, 0:1], counts[8:9, 0:1]
    global_head = info[1] + head
    index = lax.broadcasted_iota(jnp.int32, (1, TILE), 1)
    for tile in range(TILES):
        own = query[pl.ds(aligned(SEG + parity_of_head * PAR + tile * TILE), TILE), :]
        spot = SEG + parity_of_head + 2 * (tile * TILE + index)
        mark = marks(global_head, spot, first_doc, padding)[1]
        far[tile * TILE : (tile + 1) * TILE, :] = own + beside(mark)
    for tile in range(LEN // TILE):
        rows = pl.ds(tile * TILE, TILE)
        segment, parity, start = tile * TILE // SEG, tile * TILE // PAR % 2, tile * TILE % PAR
        spot = segment * SEG + parity + 2 * (start + index)
        near, _, key_mark = marks(global_head, spot, first_doc, padding)
        query[rows, :] += beside(near)
        key[rows, :] += beside(key_mark)

    row = lax.broadcasted_iota(jnp.int32, (128, TILE), 0)
    for tile in range(LEN // TILE):
        cols = pl.ds(tile * TILE, TILE)
        turned = value[cols, :].T
        value_t[:, cols] = jnp.where(row == HEAD_DIM, jnp.ones_like(turned), turned)
        key_t[:, cols] = key[cols, :].T[0:HEAD_DIM]

    def scores(tile):
        return [
            (dot(key[pl.ds(start, count), :], query[tile.rows, :], NT), start, count, later)
            for start, count, later in tile.parts
        ]

    def finish(tile, parts):
        parts = [
            (each if later is None else causal(each, later), start, count)
            for each, start, count, later in parts
        ]
        new = functools.reduce(
            jnp.maximum, [jnp.max(each, axis=0, keepdims=True) for each, _, _ in parts]
        )
        total = None
        for each, start, count in parts:
            prob = jnp.exp2(each - new).astype(jnp.bfloat16)
            part = dot(value_t[0:80, pl.ds(start, count)], prob, NN)
            total = part if total is None else total + part
        acc[:, tile.rows] = total
        most[0:1, tile.rows] = new

    in_turn(near_tiles(), scores, finish)

    def far_scores(tile):
        rows = pl.ds(aligned(parity_of_head * PAR), PAR)
        return dot(key[rows, :], far[pl.ds(tile * TILE, TILE), :], NT)

    def far_finish(tile, parts):
        cols = pl.ds(aligned(SEG + parity_of_head * PAR + tile * TILE), TILE)
        old = most[0:1, cols]
        new = jnp.maximum(old, jnp.max(parts, axis=0, keepdims=True))
        prob = jnp.exp2(parts - new).astype(jnp.bfloat16)
        part = dot(value_t[0:80, pl.ds(aligned(parity_of_head * PAR), PAR)], prob, NN)
        acc[:, cols] = acc[:, cols] * jnp.exp2(old - new) + part
        most[0:1, cols] = new

    in_turn(range(TILES), far_scores, far_finish)

    weight = acc[HEAD_DIM : HEAD_DIM + 1, :]
    result = acc[0:HEAD_DIM, :] / weight
    result_ref[0] = result
    total_ref[0] = jnp.broadcast_to(most[0:1, :] + jnp.log2(weight), (8, LEN))
    heads = pl.ds(pl.multiple_of(head * HEAD_DIM, HEAD_DIM), HEAD_DIM)
    for block, parity, start in pieces():
        part = result[:, start : start + HALF].astype(bf16)
        parted[place ^ block, :, parity * HALF : (parity + 1) * HALF] = part
    send_ref[:, heads, :] = parted[0:4]
    away_ref[:, heads, :] = parted[4:8]


def backward_kernel(
    first_head, info, query_ref, far_ref, key_ref, key_t_ref, value_ref, near0, near1, near2,
    near3, away_ref, result_ref, total_ref, out_ref, grad_ref, grad_t, balance, query_grad,
    key_grad, value_grad, turned,
):
    query, far, key, value, key_t = (
        each.at[0] for each in (query_ref, far_ref, key_ref, value_ref, key_t_ref)
    )
    head = first_head + pl.program_id(0)
    place = info[0]
    parity_of_head = (info[1] + head) & 1
    heads = pl.ds(pl.multiple_of(head * HEAD_DIM, HEAD_DIM), HEAD_DIM)
    grad_t[HEAD_DIM:128, :] = jnp.zeros((128 - HEAD_DIM, LEN), jnp.bfloat16)
    for index, near in enumerate((near0, near1, near2, near3)):
        grad_ref[index] = near[0, heads, :]
        grad_ref[4 + index] = away_ref[index, heads, :]
    for block, parity, start in pieces():
        part = grad_ref[place ^ block, :, parity * HALF : (parity + 1) * HALF]
        grad_t[0:HEAD_DIM, start : start + HALF] = part
    balance[...] = jnp.sum(
        grad_t[0:HEAD_DIM, :].astype(jnp.float32) * result_ref[0], axis=0, keepdims=True
    )
    query_grad[HEAD_DIM:128, :] = jnp.zeros((128 - HEAD_DIM, LEN), jnp.float32)
    key_grad[...] = jnp.zeros(key_grad.shape, jnp.float32)
    value_grad[...] = jnp.zeros(value_grad.shape, jnp.float32)

    def products(tile):
        found = []
        for start, count, later in tile.parts:
            rows = pl.ds(start, count)
            found.append(
                (
                    dot(key[rows, :], query[tile.rows, :], NT),
                    dot(value[rows, :], grad_t[:, tile.rows], NN),
                )
            )
        return found

    def spread(rows, queries, grads, scores, flow, total, level):
        prob = jnp.exp2(scores - total)
        slope = (prob * (flow - level)).astype(jnp.bfloat16)
        value_grad[rows, :] += dot(prob.astype(jnp.bfloat16), grads, NT)
        key_grad[rows, :] += dot(slope, queries, NN)
        return dot(key_t[0:HEAD_DIM, rows], slope, NN)

    def finish(tile, found):
        total, level = total_ref[0, 0:1, tile.rows], balance[0:1, tile.rows]
        result = None
        for (start, count, later), (scores, flow) in zip(tile.parts, found):
            if later is not None:
                scores = causal(scores, later)
            part = spread(
                pl.ds(start, count), query[tile.rows, :], grad_t[:, tile.rows], scores, flow,
                total, level,
            )
            result = part if result is None else result + part
        query_grad[0:HEAD_DIM, tile.rows] = result

    in_turn(near_tiles(), products, finish)
    far_rows = pl.ds(aligned(parity_of_head * PAR), PAR)

    def far_columns(tile):
        return pl.ds(aligned(SEG + parity_of_head * PAR + tile * TILE), TILE)

    def far_products(tile):
        return (
            dot(key[far_rows, :], far[pl.ds(tile * TILE, TILE), :], NT),
            dot(value[far_rows, :], grad_t[:, far_columns(tile)], NN),
        )

    def far_finish(tile, found):
        cols = far_columns(tile)
        query_grad[0:HEAD_DIM, cols] += spread(
            far_rows, far[pl.ds(tile * TILE, TILE), :], grad_t[:, cols], *found,
            total_ref[0, 0:1, cols], balance[0:1, cols],
        )

    in_turn(range(TILES), far_products, far_finish)

    for tile in range(LEN // TILE):
        cols = pl.ds(tile * TILE, TILE)
        turned[cols, :] = query_grad[:, cols].T
    first = lax.broadcasted_iota(jnp.int32, (HALF, 128), 1) < HEAD_DIM
    for block, parity, start in pieces():
        rows = pl.ds(parity * HALF, HALF)
        delta = place ^ block
        own = pl.ds(start, HALF)
        pair = jnp.where(
            first,
            turned[own, :] * HEAD_DIM**-0.5,
            pltpu.roll(key_grad[own, :], HEAD_DIM, axis=1) * (1 / LOG2E),
        )
        out_ref[delta, rows, 0:128] = pair.astype(jnp.bfloat16)
        out_ref[delta, rows, 128:256] = jnp.where(first, value_grad[own, :], 0.0).astype(
            jnp.bfloat16
        )


TN = (((0,), (0,)), ((), ()))
HIDDEN_STEP = 768
ROOT = math.sqrt(2 / math.pi)
CUBE = 0.044715


def feed_kernel(
    *refs,
):
    slabs, refs = refs[:4], refs[4:]
    (
        output_ref, ordered0, ordered1, masked_ref, down_ref, output_bias, gain_ref, bias_ref,
        up_bias, up_ref, weight_ref, middle_ref, active_ref, turned_ref, grad_ref, second_t,
        attended_ref, branch_ref, through_ref, sums_ref, hidden_sum,
    ), refs = refs[:21], refs[21:]
    sends, (second, back) = refs[:4], refs[4:]
    step = pl.program_id(0)
    bf16, f32 = jnp.bfloat16, jnp.float32

    @pl.when(step == 0)
    def _():
        back[...] = jnp.zeros(back.shape, f32)
        for slot, ordered in enumerate((ordered0, ordered1)):
            rows = pl.ds(slot * TOK, TOK)
            found = ordered[...] + output_bias[...].reshape(1, -1)
            for side in range(2):
                for high in range(2):
                    index = 2 * side + high
                    slab = slabs[2 * slot + side][high]
                    attended_ref[index, :, slot * TOK : (slot + 1) * TOK] = slab
                    found = found + dot(slab, output_ref[pl.ds(index * WIDTH, WIDTH), :], TN)
            middle_ref[rows, :] = found
            normed = layer_norm(found, gain_ref[...].reshape(1, -1), bias_ref[...].reshape(1, -1))
            second[rows, :] = normed.astype(bf16)
            second_t[:, slot * TOK : (slot + 1) * TOK] = normed.T.astype(bf16)

    sums = jnp.zeros((1, HIDDEN_STEP), f32)
    for part in range(3):
        rows = pl.ds(part * TILE, TILE)
        hidden = dot(second[rows, :], up_ref[...], NN) + up_bias[...]
        active_grad = dot(down_ref[rows, :], weight_ref[...], NT)
        square = hidden * hidden
        bent = jnp.tanh(hidden * (ROOT + ROOT * CUBE * square))
        half = 0.5 + 0.5 * bent
        active = hidden * half
        slope = half + hidden * (half * (1.0 - bent)) * (ROOT + 3 * ROOT * CUBE * square)
        active_ref[rows, :] = active.astype(bf16)
        turned_ref[:, part * TILE : (part + 1) * TILE] = active.T.astype(bf16)
        grad = (slope * active_grad).astype(bf16)
        grad_ref[rows, :] = grad
        sums = sums + jnp.sum(grad.astype(f32), axis=0, keepdims=True)
        back[rows, :] += dot(grad, up_ref[...], NT)
    hidden_sum[...] = jnp.broadcast_to(sums, hidden_sum.shape)

    @pl.when(step == pl.num_programs(0) - 1)
    def _():
        sums_ref[...] = jnp.zeros(sums_ref.shape, f32)
        gain = gain_ref[...].reshape(1, -1)
        for slot in range(2):
            rows = pl.ds(slot * TOK, TOK)
            middle, grads = middle_ref[rows, :], back[rows, :]
            center = middle - jnp.mean(middle, axis=-1, keepdims=True)
            scale = lax.rsqrt(jnp.mean(center * center, axis=-1, keepdims=True) + EPS)
            unit = center * scale
            scaled = grads * gain
            mean_scaled = jnp.mean(scaled, axis=-1, keepdims=True)
            mean_both = jnp.mean(scaled * unit, axis=-1, keepdims=True)
            through = masked_ref[rows, :] + scale * (scaled - mean_scaled - unit * mean_both)
            through_ref[rows, :] = through
            branch = through.astype(bf16)
            branch_ref[rows, :] = branch
            for index, each in enumerate(
                (branch.astype(f32), down_ref[rows, :].astype(f32), grads * unit, grads)
            ):
                sums_ref[index : index + 1, :] += jnp.sum(each, axis=0, keepdims=True)
            for side in range(2):
                for high in range(2):
                    index = 2 * side + high
                    found = dot(output_ref[pl.ds(index * WIDTH, WIDTH), :], branch, NT)
                    sends[2 * slot + side][high] = found.astype(bf16)


def feed(slabs, output_own, ordered, masked, down, output_bias, gain, bias, up_bias, up, weight):
    bf16, f32 = jnp.bfloat16, jnp.float32
    model, hidden = up.shape
    tokens = 2 * TOK

    slab = fixed(2, WIDTH, TOK)
    table = fixed(tokens, model)
    vector = fixed(model)
    wide = along(tokens, HIDDEN_STEP, axis=1)
    tall = along(HIDDEN_STEP, tokens, axis=0)
    out = jax.ShapeDtypeStruct
    return pl.pallas_call(
        feed_kernel,
        grid=(hidden // HIDDEN_STEP,),
        in_specs=[slab] * 4
        + [fixed(model, model), fixed(TOK, model), fixed(TOK, model), table, table]
        + [vector] * 3
        + [along(1, HIDDEN_STEP, axis=1), along(model, HIDDEN_STEP, axis=1)]
        + [along(HIDDEN_STEP, model, axis=0)],
        out_specs=[table, wide, tall, wide, fixed(model, tokens), fixed(4, WIDTH, tokens)]
        + [table, table, fixed(8, model), along(8, HIDDEN_STEP, axis=1)]
        + [slab] * 4,
        out_shape=[
            out((tokens, model), f32),
            out((tokens, hidden), bf16),
            out((hidden, tokens), bf16),
            out((tokens, hidden), bf16),
            out((model, tokens), bf16),
            out((4, WIDTH, tokens), bf16),
            out((tokens, model), bf16),
            out((tokens, model), f32),
            out((8, model), f32),
            out((8, hidden), f32),
        ]
        + [out((2, WIDTH, TOK), bf16)] * 4,
        scratch_shapes=[pltpu.VMEM((tokens, model), bf16), pltpu.VMEM((tokens, model), f32)],
        compiler_params=pltpu.CompilerParams(vmem_limit_bytes=VMEM_LIMIT),
        cost_estimate=CHEAP,
        name="feed",
    )(*slabs, output_own, *ordered, masked, down, output_bias, gain, bias, up_bias, up, weight)


def halved(found, own, keep_ref, away_ref, place):
    zero, one = found[:, 0].astype(jnp.bfloat16), found[:, 1].astype(jnp.bfloat16)
    keep_ref[place] = jnp.where(own == 0, zero, one)
    away_ref[place] = jnp.where(own == 0, one, zero)


def wide_kernel(
    info, attended_ref, branch_ref, turned_ref, down_ref, vector_ref, keep_ref, away_ref
):
    rows = HIDDEN_STEP // 8
    found = dot(turned_ref[...], down_ref[...], NN)
    found = found.reshape(2, 2, 2, rows, found.shape[-1])
    every = slice(None)
    halved(found, info[1], keep_ref, away_ref, (every, every, slice(0, rows)))
    found = dot(attended_ref[0], branch_ref[...], NN).reshape(2, 4, WIDTH // 8, -1)
    found = jnp.concatenate((found, vector_ref[...]), 2)
    found = found.reshape(2, 2, 2, 32, found.shape[-1])
    halved(found, info[1], keep_ref, away_ref, (every, every, slice(rows, rows + 32)))


def tall_kernel(info, second_t, grad_ref, keep_ref, away_ref):
    found = dot(second_t[...], grad_ref[...], NN)
    found = found.reshape(8, 2, -1, found.shape[-1])
    every = slice(None)
    halved(found, info[1], keep_ref, away_ref, (every, 0))


def out_kernel(swap_ref, active_ref, weight_ref, middle_ref, bias_ref, out_ref, acc, lanes):
    step = pl.program_id(0)
    found = dot(active_ref[...], weight_ref[...], NN)

    @pl.when(step == 0)
    def _():
        acc[...] = middle_ref[...] + bias_ref[...].reshape(1, -1) + found

    @pl.when(step > 0)
    def _():
        acc[...] += found

    @pl.when(step == pl.num_programs(0) - 1)
    def _():
        for slot in range(2):
            for part, column in columns(out_ref.shape[-1]):
                for parity in range(2):
                    lanes[part, pl.ds(parity, HALF, stride=2), :] = acc[
                        pl.ds(slot * TOK + parity * HALF, HALF), column
                    ]
                out_ref[slot ^ swap_ref[0], :, column] = lanes[part]


def fixed(*shape):
    return pl.BlockSpec(shape, lambda step, *info: (0,) * len(shape))


def along(*shape, axis):
    return pl.BlockSpec(
        shape, lambda step, *info: tuple(step if i == axis else 0 for i in range(len(shape)))
    )


def stepped(kernel, name, steps, info, operands, in_specs, out_specs, out_shape, scratch=()):
    return pl.pallas_call(
        kernel,
        grid_spec=pltpu.PrefetchScalarGridSpec(
            num_scalar_prefetch=1,
            grid=(steps,),
            in_specs=in_specs,
            out_specs=out_specs,
            scratch_shapes=list(scratch),
        ),
        out_shape=out_shape,
        compiler_params=pltpu.CompilerParams(vmem_limit_bytes=VMEM_LESS),
        cost_estimate=CHEAP,
        name=name,
    )(info, *operands)


def wide_shares(info, attended, branch, turned, down, vectors):
    hidden, tokens = turned.shape
    model = branch.shape[-1]
    return stepped(
        wide_kernel,
        "wide_shares",
        hidden // HIDDEN_STEP,
        info,
        (attended, branch, turned, down, vectors),
        [
            pl.BlockSpec((1, WIDTH, tokens), lambda step, info: (step ^ info[0], 0, 0)),
            fixed(tokens, model),
            along(HIDDEN_STEP, tokens, axis=0),
            fixed(tokens, model),
            along(2, 4, 8, model, axis=0),
        ],
        [along(2, 2, 128, model, axis=0)] * 2,
        [jax.ShapeDtypeStruct((8, 2, 128, model), jnp.bfloat16)] * 2,
    )


def tall_shares(info, second_t, grad):
    tokens, hidden = grad.shape
    model = second_t.shape[0]
    return stepped(
        tall_kernel,
        "tall_shares",
        hidden // HIDDEN_STEP,
        info,
        (second_t, grad),
        [fixed(model, tokens), along(tokens, HIDDEN_STEP, axis=1)],
        [along(8, 1, model // 16, HIDDEN_STEP, axis=1)] * 2,
        [
            jax.ShapeDtypeStruct((8, hidden // HIDDEN_STEP, model // 16, HIDDEN_STEP), jnp.bfloat16)
        ]
        * 2,
    )


def layer_out(swap, active, weight, middle, bias):
    tokens, hidden = active.shape
    model = weight.shape[-1]
    return stepped(
        out_kernel,
        "layer_out",
        hidden // HIDDEN_STEP,
        swap,
        (active, weight, middle, bias),
        [
            along(tokens, HIDDEN_STEP, axis=1),
            along(HIDDEN_STEP, model, axis=0),
            fixed(tokens, model),
            fixed(model),
        ],
        fixed(2, TOK, model),
        jax.ShapeDtypeStruct((2, TOK, model), jnp.float32),
        [pltpu.VMEM((tokens, model), jnp.float32), *lanes_of(model)],
    )


def project_triples(grads, weights):
    grads = jnp.concatenate([each[0] for each in grads], -1)
    return dot(grads, weights[...], NN)


def far_kernel(head0, heads, weights, out_ref):
    out_ref[0] = project_triples((head0, heads), weights).astype(jnp.bfloat16)


def near_kernel(head0, heads, weights, far_ref, keep_ref, away_ref):
    found = project_triples((head0, heads), weights) + far_ref[0].astype(jnp.float32)

    @pl.when(pl.program_id(0) % 2 == 0)
    def _():
        keep_ref[0] = found

    @pl.when(pl.program_id(0) % 2 == 1)
    def _():
        away_ref[0] = found.astype(jnp.bfloat16)


def back_specs(grads, weights, first):
    def block(width):
        return pl.BlockSpec((1, TOK, width), lambda step: (first + step, 0, 0))

    return [block(each.shape[-1]) for each in grads] + [
        pl.BlockSpec(weights.shape, lambda step: (0, 0))
    ]


def far_projection(grads, weights):
    model = weights.shape[-1]
    return pl.pallas_call(
        far_kernel,
        grid=(4,),
        in_specs=back_specs(grads, weights, 4),
        out_specs=pl.BlockSpec((1, TOK, model), lambda step: (step, 0, 0)),
        out_shape=jax.ShapeDtypeStruct((4, TOK, model), jnp.bfloat16),
        compiler_params=pltpu.CompilerParams(vmem_limit_bytes=VMEM_LESS),
        cost_estimate=CHEAP,
        name="far_projection",
    )(*grads, weights)


def near_projection(grads, weights, far):
    model = weights.shape[-1]
    own = pl.BlockSpec((1, TOK, model), lambda step: (step, 0, 0))
    pair = pl.BlockSpec((1, TOK, model), lambda step: (step // 2, 0, 0))
    return pl.pallas_call(
        near_kernel,
        grid=(4,),
        in_specs=[*back_specs(grads, weights, 0), own],
        out_specs=[pair, pair],
        out_shape=[
            jax.ShapeDtypeStruct((2, TOK, model), jnp.float32),
            jax.ShapeDtypeStruct((2, TOK, model), jnp.bfloat16),
        ],
        compiler_params=pltpu.CompilerParams(vmem_limit_bytes=VMEM_LESS),
        cost_estimate=CHEAP,
        name="near_projection",
    )(*grads, weights, far)


LATE_ROWS = 112
TRIPLE = 3 * HEAD_DIM


def late_kernel(info, *refs):
    normed, (head0, heads, keep_ref, away_ref) = refs[:BLOCKS], refs[BLOCKS:]
    total, acc = 0.0, None
    for delta in range(BLOCKS):
        grads = jnp.concatenate((head0[delta], heads[delta]), -1)
        found = dot(normed[delta][0:TOK, :], grads, TN)
        acc = found if acc is None else acc + found
        total = total + jnp.sum(grads.astype(jnp.float32), axis=0, keepdims=True)
    rows = acc.shape[0] // 8

    def packed(values):
        return jnp.concatenate(
            [values[:, 256 * head : 256 * head + TRIPLE] for head in range(OWN_HEADS)], 1
        )

    width = OWN_HEADS * TRIPLE
    sums = jnp.broadcast_to(packed(total), (8, LATE_ROWS - rows, width))
    found = jnp.concatenate((packed(acc).reshape(8, rows, width), sums), 1)
    found = found.reshape(2, 2, 2, LATE_ROWS, width)
    zero, one = found[:, 0].astype(jnp.bfloat16), found[:, 1].astype(jnp.bfloat16)
    keep_ref[...] = jnp.where(info[0] == 0, zero, one)
    away_ref[...] = jnp.where(info[0] == 0, one, zero)


def late_shares(info, normed, grads):
    width = OWN_HEADS * TRIPLE
    return stepped(
        late_kernel,
        "late_shares",
        1,
        info,
        (*normed, *grads),
        [fixed(*each.shape) for each in (*normed, *grads)],
        [fixed(2, 2, LATE_ROWS, width)] * 2,
        [jax.ShapeDtypeStruct((2, 2, LATE_ROWS, width), jnp.bfloat16)] * 2,
    )


def ordered_by(bits, refs):
    found = [ref[...].astype(jnp.float32) for ref in refs]
    for bit in range(2):
        flip = (bits >> bit & 1) == 1
        found = [
            jnp.where(flip, found[i ^ (1 << bit)], found[i]) for i in range(len(found))
        ]
    return found


def early_end_kernel(info, *refs):
    early, (down_ref, output_ref, up_ref, sums_ref) = refs[:4], refs[4:]
    rows = down_ref.shape[0] // 4
    more = output_ref.shape[0] // 4
    model = output_ref.shape[1]
    below = rows + more + 8
    for index, each in enumerate(ordered_by(info[0], early)):
        down_ref[index * rows : (index + 1) * rows, :] = each[0:rows]
        output_ref[index * more : (index + 1) * more, :] = each[rows : rows + more]
        if index == 0:
            sums_ref[...] = each[rows + more : below]
        for part, column in enumerate(range(0, up_ref.shape[1], model)):
            up_ref[index * more : (index + 1) * more, column : column + model] = each[
                below + part * more : below + (part + 1) * more
            ]


def early_end(info, early, hidden):
    model = early[0].shape[-1]
    part = model // 8
    return pl.pallas_call(
        early_end_kernel,
        in_specs=[pl.BlockSpec(memory_space=pltpu.SMEM)]
        + [pl.BlockSpec(memory_space=pltpu.VMEM)] * 4,
        out_specs=[pl.BlockSpec(memory_space=pltpu.VMEM)] * 4,
        out_shape=[
            jax.ShapeDtypeStruct((hidden // 8, model), jnp.float32),
            jax.ShapeDtypeStruct((part, model), jnp.float32),
            jax.ShapeDtypeStruct((part, hidden), jnp.float32),
            jax.ShapeDtypeStruct((8, model), jnp.float32),
        ],
        compiler_params=pltpu.CompilerParams(vmem_limit_bytes=VMEM_LESS),
        cost_estimate=CHEAP,
        name="early_end",
    )(info, *early)


def late_end_kernel(info, *refs):
    pieces_in, refs = refs[:4], refs[4:]
    weights, (gain_ref, bias_ref), refs = refs[:3], refs[3:5], refs[5:]
    outs, (sums_ref, norm_ref) = refs[:3], refs[3:]
    part = outs[0].shape[0]
    pieces_in = ordered_by(info[0], pieces_in)
    groups_in = [
        jnp.concatenate((pieces_in[2 * core][side], pieces_in[2 * core + 1][side]), 0)
        for side in range(2)
        for core in range(2)
    ]
    both = bias_grad = jnp.zeros((8, part), jnp.float32)
    ones = jnp.ones((8, outs[0].shape[1]), jnp.float32)
    for kind, (weight, out) in enumerate(zip(weights, outs)):
        found = jnp.concatenate(
            [
                each[:, TRIPLE * head + HEAD_DIM * kind : TRIPLE * head + HEAD_DIM * (kind + 1)]
                for each in groups_in
                for head in range(OWN_HEADS)
            ],
            1,
        )
        out[...] = found[0:part]
        sums_ref[8 * kind : 8 * kind + 8, :] = found[part : part + 8]
        mine = weight[...].astype(jnp.float32)

        def across(values):
            return lax.dot_general(ones, values, NT, precision=HIGH)

        bias_grad = bias_grad + across(mine * found[part : part + 1])
        both = both + across(mine * found[0:part])
    norm_ref[0:8, :] = (both - bias_ref[0] * bias_grad) / gain_ref[0]
    norm_ref[8:16, :] = bias_grad


def late_end(info, late, weights, gain, bias):
    model = weights[0].shape[0]
    part = model // 8
    own = pl.BlockSpec((part, model), lambda step, info: (info[1], 0))
    vector = pl.BlockSpec((1, 1, part), lambda step, info: (info[1], 0, 0))
    return stepped(
        late_end_kernel,
        "late_end",
        1,
        info,
        (*late, *weights, gain.reshape(8, 1, part), bias.reshape(8, 1, part)),
        [*[fixed(*late[0].shape)] * 4, own, own, own, vector, vector],
        [*[fixed(part, model)] * 3, fixed(24, model), fixed(16, part)],
        [
            *[jax.ShapeDtypeStruct((part, model), jnp.float32)] * 3,
            jax.ShapeDtypeStruct((24, model), jnp.float32),
            jax.ShapeDtypeStruct((16, part), jnp.float32),
        ],
    )


def whole(*shape):
    return pl.BlockSpec(shape, lambda head, info: (0,) * len(shape))


def per_head(*shape, first=0):
    return pl.BlockSpec((1, *shape), lambda head, info: (first + head, *(0,) * len(shape)))


def attention(info, normed, weight, bias):
    bf16, f32 = jnp.bfloat16, jnp.float32
    model = weight.shape[1]

    def out(dtype, *shape):
        return jax.ShapeDtypeStruct(shape, dtype)

    return pl.pallas_call(
        forward_kernel,
        grid_spec=pltpu.PrefetchScalarGridSpec(
            num_scalar_prefetch=1,
            grid=(OWN_HEADS,),
            in_specs=[
                *[whole(SENT, model)] * BLOCKS,
                pl.BlockSpec((384, model), lambda head, info: (head, 0)),
                pl.BlockSpec((1, 384), lambda head, info: (0, head)),
            ],
            out_specs=[
                *[whole(4, WIDTH, TOK)] * 2,
                per_head(HEAD_DIM, LEN),
                per_head(8, LEN),
                per_head(LEN, 128),
                per_head(PAR, 128),
                per_head(LEN, 128),
                per_head(HEAD_DIM, LEN),
                per_head(LEN, 128),
            ],
            scratch_shapes=[
                pltpu.VMEM((128, LEN), bf16),
                pltpu.VMEM((8, LEN), f32),
                pltpu.VMEM((80, LEN), f32),
                pltpu.VMEM((BLOCKS, HEAD_DIM, TOK), bf16),
            ],
        ),
        out_shape=[
            *[out(bf16, 4, WIDTH, TOK)] * 2,
            out(f32, OWN_HEADS, HEAD_DIM, LEN),
            out(f32, OWN_HEADS, 8, LEN),
            out(bf16, OWN_HEADS, LEN, 128),
            out(bf16, OWN_HEADS, PAR, 128),
            out(bf16, OWN_HEADS, LEN, 128),
            out(bf16, OWN_HEADS, HEAD_DIM, LEN),
            out(bf16, OWN_HEADS, LEN, 128),
        ],
        compiler_params=pltpu.CompilerParams(vmem_limit_bytes=VMEM_LIMIT),
        name="attention",
    )(info, *normed, weight, bias)


def attention_back(heads, info, held, grads, result, total):
    first, count = heads
    bf16, f32 = jnp.bfloat16, jnp.float32
    return pl.pallas_call(
        functools.partial(backward_kernel, first),
        grid_spec=pltpu.PrefetchScalarGridSpec(
            num_scalar_prefetch=1,
            grid=(count,),
            in_specs=[
                per_head(LEN, 128, first=first),
                per_head(PAR, 128, first=first),
                per_head(LEN, 128, first=first),
                per_head(HEAD_DIM, LEN, first=first),
                per_head(LEN, 128, first=first),
                *[whole(1, WIDTH, TOK)] * 4,
                whole(4, WIDTH, TOK),
                per_head(HEAD_DIM, LEN, first=first),
                per_head(8, LEN, first=first),
            ],
            out_specs=pl.BlockSpec((BLOCKS, TOK, 256), lambda head, info: (0, 0, head)),
            scratch_shapes=[
                pltpu.VMEM((BLOCKS, HEAD_DIM, TOK), bf16),
                pltpu.VMEM((128, LEN), bf16),
                pltpu.VMEM((1, LEN), f32),
                pltpu.VMEM((128, LEN), f32),
                pltpu.VMEM((LEN, 128), f32),
                pltpu.VMEM((LEN, 128), f32),
                pltpu.VMEM((LEN, 128), f32),
            ],
        ),
        out_shape=jax.ShapeDtypeStruct((BLOCKS, TOK, count * 256), bf16),
        compiler_params=pltpu.CompilerParams(vmem_limit_bytes=VMEM_LESS),
        cost_estimate=CHEAP,
        name="attention_back",
    )(info, *held, *grads, result, total)


def flipped(array, axis, bit):
    zero, one = (lax.index_in_dim(array, i, axis, keepdims=False) for i in range(2))
    return jnp.stack((pick(bit, zero, one), pick(bit, one, zero)), axis)


def entry(array, axis, index):
    return lax.dynamic_index_in_dim(array, index, axis, keepdims=False)


def reduced(array, axis, bit, pairs):
    return plus(entry(array, axis, bit), send(entry(array, axis, 1 - bit), pairs))


def plus(left, right):
    return (left.astype(jnp.float32) + right.astype(jnp.float32)).astype(jnp.bfloat16)


def collected(array, bit, pairs):
    other = send(array, pairs)
    return jnp.stack((pick(bit, array, other), pick(bit, other, array)))


def packed_rows(
    layer_input, doc_ids, cotangent, attn_norm_gain, attn_norm_bias, query_weight, query_bias,
    key_weight, value_weight, value_bias, output_weight, output_bias, feed_norm_gain,
    feed_norm_bias, up_weight, up_bias, down_weight, down_bias,
):
    bf16, f32 = jnp.bfloat16, jnp.float32
    model = layer_input.shape[-1]
    hidden_width = up_weight.shape[-1]
    row, seq = lax.axis_index("row"), lax.axis_index("seq")
    x, core, z, y = row >> 1, row & 1, seq >> 1, seq & 1
    swap = (z & 1)[None].astype(jnp.int32)
    place = 4 * core + 2 * (z & 1) + y
    group = 2 * y + core
    info = jnp.stack((place, OWN_HEADS * group)).astype(jnp.int32)

    ordered, blocks = [], []
    for slot in range(2):
        values, block = first_norm(
            slot, swap, layer_input, doc_ids, attn_norm_gain, attn_norm_bias
        )
        ordered.append(values)
        blocks.append(block)
    first = send(blocks[0], to_row(0))
    first, blocks[1] = tied((first, blocks[1]))
    normed = [first, send(first, SWAP_Y)]
    second = send(blocks[1], to_row(1))

    def other_order(array):
        array = array.reshape(2, 2, WIDTH, model)
        return flipped(flipped(array, 0, y), 1, z >> 1).reshape(4 * WIDTH, model)

    def own_columns(weight):
        own = lax.dynamic_slice_in_dim(weight, group * WIDTH, WIDTH, weight.ndim - 1)
        return own.reshape(*weight.shape[:-1], OWN_HEADS, HEAD_DIM)

    query_own, key_own, value_own = map(own_columns, (query_weight, key_weight, value_weight))
    triple_weight = jnp.stack((query_own, key_own, value_own), 2)
    triple_weight = jnp.pad(triple_weight, ((0, 0),) * 3 + ((0, 128 - HEAD_DIM),))
    triple_weight = triple_weight.reshape(model, OWN_HEADS * 384).T
    query_row, value_row = own_columns(query_bias), own_columns(value_bias)
    triple_bias = jnp.stack((query_row, jnp.zeros_like(query_row), value_row), 1)
    triple_bias = jnp.pad(triple_bias, ((0, 0), (0, 0), (0, 128 - HEAD_DIM))).reshape(-1)
    docs = doc_ids.reshape(2, HALF, 2).transpose(0, 2, 1).reshape(2, TOK)
    docs = flipped(docs, 0, z & 1)
    masked_grad = jnp.where((docs >= 0)[..., None], moved(sort_kernel, swap, cotangent), 0.0)
    down_grad = masked_grad.astype(bf16)
    output_own = other_order(output_weight)
    back_weight = jnp.stack((query_own, key_own, value_own, jnp.zeros_like(key_own)), 2)
    back_weight = back_weight.reshape(model, OWN_HEADS * 256).T
    (
        normed, second, output_own, back_weight, triple_weight, triple_bias, ordered_rows,
        masked_grad, down_grad,
    ) = tied(
        (
            normed, second, output_own, back_weight, triple_weight, triple_bias,
            jnp.stack(ordered), masked_grad, down_grad,
        )
    )
    normed.extend((second, send(second, SWAP_Y)))
    normed.extend([send(block, SWAP_CORE) for block in normed])
    sends, far_sends, result, total, *kept = attention(
        info, normed, triple_weight, triple_bias[None]
    )
    far_sends = send(far_sends, SWAP_CORE)
    slabs = [
        send(jnp.stack((sends[index], far_sends[index])), to_owner(index)) for index in range(4)
    ]
    (
        middle, active, turned, hidden_grad, second_t, attended, branch_grad, middle_grad, sums,
        hidden_sum, *slabs,
    ) = feed(
        slabs, output_own, ordered, masked_grad.reshape(2 * TOK, model),
        down_grad.reshape(2 * TOK, model), output_bias, feed_norm_gain, feed_norm_bias,
        up_bias[None], up_weight, down_weight,
    )
    grads = [send(slabs[index], inverse(to_owner(index))) for index in range(4)]

    vectors = [each.reshape(8, -1) for each in (*sums[:4], hidden_sum[0])]
    vectors = jnp.concatenate(vectors, 1)[:, None, None]
    vectors = jnp.pad(vectors, ((0, 0), (0, 3), (0, 7), (0, 0)))
    share_info = jnp.stack((2 * y + (z >> 1), core)).astype(jnp.int32)
    wide, wide_away = wide_shares(
        share_info, attended, branch_grad, turned, down_grad.reshape(2 * TOK, model), vectors
    )
    wide_away, second_t, hidden_grad, grads[1], grads[3] = tied(
        (wide_away, second_t, hidden_grad, grads[1], grads[3])
    )
    wide_away = send(wide_away, SWAP_CORE)
    tall, tall_away = tall_shares(share_info, second_t, hidden_grad)
    grads, wide, wide_away, tall, tall_away = tied((grads, wide, wide_away, tall, tall_away))
    grads.append(send(jnp.stack([pair[1] for pair in grads]), SWAP_CORE))
    tall_away = send(tall_away, SWAP_CORE)
    wide = plus(wide, wide_away).reshape(2, 2, 2, 2, -1, model)
    grads, wide = tied((grads, wide))
    wide_away = send(entry(wide, 3, 1 - x), SWAP_X)

    def back(heads):
        return attention_back(heads, info, kept, grads, result, total)

    head0 = back((0, 1))
    head0, grads, tall_away = tied((head0, grads, tall_away))
    tall = plus(tall, tall_away).reshape(2, 2, 2, hidden_width // model, 2, -1, model)
    tall, grads = tied((tall, grads))
    tall_away = send(entry(tall, 2, 1 - y), SWAP_Y)
    heads = back((1, 2))
    triple_grads = (head0, heads)
    far_half = far_projection(triple_grads, back_weight)
    far_half, triple_grads, wide_away, tall_away = tied(
        (far_half, triple_grads, wide_away, tall_away)
    )
    far_half = send(far_half, SWAP_CORE)
    late, late_away = late_shares((z & 1)[None].astype(jnp.int32), normed, triple_grads)
    far_half, late, late_away = tied((far_half, late, late_away))
    wide, tall = plus(entry(wide, 3, x), wide_away), plus(entry(tall, 2, y), tall_away)
    wide_away = send(entry(wide, 2, 1 - y), SWAP_Y)
    tall_away = send(entry(tall, 3, 1 - x), SWAP_X)
    late_away = send(late_away, SWAP_Z_LOW)
    near_keep, near_away = near_projection(triple_grads, back_weight, far_half)
    pieces_away = (near_away[0, :96], near_away[0, 96:], near_away[1])
    near_away = [send(each, SWAP_Y) for each in pieces_away]
    near_keep, near_away[0], wide_away, tall_away, late_away, active, middle = tied(
        (near_keep, near_away[0], wide_away, tall_away, late_away, active, middle)
    )
    tall = plus(entry(tall, 3, x), tall_away).reshape(2, 2, -1, model)
    early = jnp.concatenate((plus(entry(wide, 2, y), wide_away), tall), 2)
    late = plus(late, late_away)
    early_away = send(entry(early, 1, 1 - (z & 1)), SWAP_Z_LOW)
    late_away = send(entry(late, 0, 1 - (z >> 1)), SWAP_Z_HIGH)
    near_away, early_away, late_away, active, middle = tied(
        (near_away, early_away, late_away, active, middle)
    )
    early = plus(entry(early, 1, z & 1), early_away)
    early_away = send(entry(early, 0, 1 - (z >> 1)), SWAP_Z_HIGH)
    near_away = (jnp.concatenate(near_away[:2], 0), near_away[2])
    returned = []
    for slot in range(2):
        both = (near_keep[slot] + near_away[slot].astype(f32)).astype(bf16)
        returned.append(send(both, inverse(to_row(slot))))
    late = plus(entry(late, 0, z >> 1), late_away).reshape(2, 2, -1, late.shape[-1])
    late = reduced(late, 1, x, SWAP_X)
    other = send(entry(late, 0, 1 - y), SWAP_Y)
    out = layer_out(swap, active, down_weight, middle, down_bias)
    other, out, early_away = tied((other, out, early_away))
    early = plus(entry(early, 0, z >> 1), early_away)
    early = [early, send(early, SWAP_X)]
    late = entry(late, 0, y)
    late = jnp.stack((pick(y, late, other), pick(y, other, late)))
    late = [late, send(late, SWAP_X)]

    def all_four(pair):
        return [*pair, *(send(each, SWAP_CORE) for each in pair)]

    input_grad = last_norm(
        swap, ordered_rows, returned, middle_grad.reshape(2, TOK, model), attn_norm_gain
    )
    end_info = jnp.stack((2 * core + x, seq)).astype(jnp.int32)
    grad_down, grad_output, grad_up, sums = early_end(
        end_info, all_four(early), hidden_width
    )
    part = model // 8
    output_sum, down_sum, grad_feed_gain, grad_feed_bias, up_sum = jnp.split(
        sums[0], (part, 2 * part, 3 * part, 4 * part)
    )
    grad_query, grad_key, grad_value, sums, norm = late_end(
        end_info,
        all_four(late),
        (query_weight, key_weight, value_weight),
        attn_norm_gain,
        attn_norm_bias,
    )

    def own_part(array):
        return lax.dynamic_slice_in_dim(array, seq * part, part, 0)

    query_sum, value_sum = own_part(sums[0]), own_part(sums[16])
    grad_attn_gain, grad_attn_bias = norm[0], norm[8]
    return (
        out,
        input_grad,
        grad_attn_gain,
        grad_attn_bias,
        grad_query,
        query_sum,
        grad_key,
        grad_value,
        value_sum,
        grad_output,
        output_sum,
        grad_feed_gain,
        grad_feed_bias,
        grad_up,
        up_sum,
        grad_down,
        down_sum,
    )


def solution(mesh):
    placed = (
        P("row", "seq", None),
        P("row", "seq"),
        P("row", "seq", None),
        P(),
        P(),
        P(),
        P(),
        P(),
        P(),
        P(),
        P(),
        P(),
        P(),
        P(),
        P(),
        P(),
        P(),
        P(),
    )
    chosen = packed_rows if dict(mesh.shape) == {"row": 4, "seq": 8} else per_device
    return jax.shard_map(
        chosen,
        mesh=mesh,
        in_specs=placed,
        out_specs=(
            P("row", "seq", None),
            P("row", "seq", None),
            P("seq"),
            P("seq"),
            P("seq", None),
            P("seq"),
            P("seq", None),
            P("seq", None),
            P("seq"),
            P("seq", None),
            P("seq"),
            P("seq"),
            P("seq"),
            P("seq", None),
            P("seq"),
            P("seq", None),
            P("seq"),
        ),
        check_vma=False,
    )
```
